32 devices in a mesh: groups: 2 (over x), node: 16 (over z, y, core).
Axes of the slice: x: 2, y: 2, z: 4, core: 2. Of those that a mesh axis runs over, the one named last changes fastest.
Arguments:
- tokens: bfloat16 [4096, 3584], P(('groups', 'node')), parts along dimension 0, may hold values from -6 to 6
- expert_ids: int32 [4096, 4], P(('groups', 'node')), parts along dimension 0, may hold values from 0 to 7, all different within a row; in each aligned block of 128 rows (0 to 127, 128 to 255, ...) at most 80 rows name the same one
- gate_codes: int32 [4096, 4], P(('groups', 'node')), parts along dimension 0, may hold values from 1 to 4096
- w_gate: bfloat16 [3584, 8192], P(None, 'node'), may hold values from -0.09375 to 0.09375
- w_up: bfloat16 [3584, 8192], P(None, 'node'), may hold values from -0.09375 to 0.09375
- w_down: bfloat16 [8192, 3584], P('node'), may hold values from -0.1875 to 0.1875
Outputs:
- mixed: bfloat16 [4096, 3584], P(('groups', 'node')), parts along dimension 0
The draws below stay inside these ranges and needn't reach their ends.
There are 2 independent parts, one for each index of `groups`. The reference program is written for one: setup_inputs(seed, part) draws one part's arguments, and reference() takes and returns one part's arrays. A program takes and returns all parts, laid end to end along the dimension named above; an argument that names none is the same for every part. Nothing has to cross between parts.
Inputs may be any that keep to these rules, and one draw needn't show every extreme that they name: `expert_ids`: each row names 4 different experts. In the rows of one device no expert is named more than 80 times, a bound that some block reaches.
All inputs are finite; a program needn't handle non-finite values.
Results may differ from the reference program's by a relative error of at most 0.0067.
Values may be sent and summed in bfloat16 or wider, within the bound.
No kernel may reach another device: no remote copies, remote signals or barrier semaphores. Data moves between devices by JAX's collectives and lax.ppermute only.
A program may use at most 128 MiB of HBM per device.

```python
import math
import jax
import jax.numpy as jnp
import numpy as np
from jax import lax

D = 3584
HID = 1024
SPAN = 2
TOP = 4
TOK_DEV = 128
EXPERTS = 8
CAP = 80
TOKENS = 2048
N_NODE = 16


def set_ends(array, own_key, least, top_value):
    shape = array.shape
    place = [jax.random.randint(jax.random.fold_in(own_key, axis), (), 0, shape[axis]) for axis in range(len(shape))]
    array = array.at[tuple(place)].set(least)
    longest = shape.index(max(shape))
    place[longest] = (place[longest] + 1) % shape[longest]
    return array.at[tuple(place)].set(top_value)


def shard_levels(key, dims, cuts, low, top_value):
    gain = 1.0
    for axis_at, blocks in cuts:
        heights = jax.random.uniform(jax.random.fold_in(jax.random.fold_in(key, 6), axis_at), (blocks,), jnp.float32, low / len(cuts), top_value / len(cuts))
        gain = gain * jnp.repeat(jnp.exp(heights), dims[axis_at] // blocks).reshape((-1,) + (1,) * (len(dims) - 1 - axis_at))
    return gain


def shared_out(rng, own, number, rows, amount, top, bound, lean):
    order = jax.random.permutation(rng, amount)
    packed, usual = portions_of(amount, rows * top, bound, lean, True), portions_of(amount, rows * top, bound, lean, False)
    places = jnp.arange(amount)

    def named(tallies, offset_by):
        used = int((tallies > 0).sum())
        fixed = max(1, used // 4)
        shifted = fixed + (places - fixed + offset_by * (used - fixed)) % max(1, amount - fixed)
        return jnp.zeros((amount,), jnp.int32).at[order[jnp.where(places < fixed, places, shifted)]].set(jnp.asarray(tallies, jnp.int32))

    tallies = jnp.where(number % 4 == 0, named(packed, number // 4), named(usual, number - number // 4 - 1))
    mixed = jax.random.permutation(jax.random.fold_in(own, 3), amount)
    source_of, taker = mixed[0:amount // 2 * 2:2], mixed[1:amount // 2 * 2:2]
    room = jnp.minimum(tallies[source_of] - 1, bound - tallies[taker]) // 2
    room = jnp.where((source_of == order[0]) | (taker == order[0]) | (tallies[taker] == 0), 0, jnp.maximum(room, 0))
    shifted = jax.random.randint(jax.random.fold_in(own, 4), (amount // 2,), 0, 1 << 20) % (room + 1)
    tallies = tallies.at[source_of].add(-shifted).at[taker].add(shifted)
    items = jnp.searchsorted(jnp.cumsum(tallies), jnp.arange(rows * top), side="right").astype(jnp.int32)
    grid = items.reshape(top, rows).T
    grid = grid[jax.random.permutation(jax.random.fold_in(own, 1), rows)]
    offset_by = jax.random.randint(jax.random.fold_in(own, 2), (rows, 1), 0, top)
    return jnp.take_along_axis(grid, (jnp.arange(top)[None, :] + offset_by) % top, axis=1)


def portions_of(amount, total, limit, skew, full):
    loads = [(1 << 20) // math.isqrt(rank ** skew) + 1 for rank in range(1, amount + 1)]
    largest = limit if full else min(limit, max(-(-total // amount), total * loads[0] // sum(loads)))
    least = 1 if total - largest >= amount - 1 else 0
    counts, spare = [largest] + [least] * (amount - 1), total - largest - least * (amount - 1)
    while spare > 0:
        movable = [i for i in range(1, amount) if counts[i] < largest] or [i for i in range(1, amount) if counts[i] < limit]
        whole, left = sum([loads[i] for i in movable]), spare
        for i in movable:
            addition = min(limit - counts[i], max(1, left * loads[i] // whole), spare)
            counts[i] = counts[i] + addition
            spare = spare - addition
    return np.array(counts)


def gaussian(stream_key, dims, spread, limit, cuts=(), held_as=jnp.bfloat16):
    entries = spread * jax.random.normal(stream_key, dims, jnp.float32)
    if cuts:
        entries = entries * shard_levels(stream_key, dims, cuts, -0.22, 0.18)
    return jnp.clip(entries, -limit, limit).astype(held_as)


def setup_inputs(seed: int = 0, part: int = 0) -> dict:
    keys = jax.random.split(jax.random.key(seed), 7)
    part_keys = jax.random.split(jax.random.fold_in(keys[6], part), 7)
    tokens = gaussian(part_keys[0], (TOKENS, D), 1.0, 6.0, ((0, 16),))
    expert_ids_keys = jax.random.split(jax.random.fold_in(part_keys[1], 1), TOKENS // TOK_DEV)
    expert_ids_turns = jax.random.permutation(jax.random.fold_in(part_keys[1], 3), TOKENS // TOK_DEV)
    expert_ids = jax.vmap(lambda own, number: shared_out(jax.random.fold_in(part_keys[1], 2), own, number, TOK_DEV, EXPERTS, TOP, CAP, 2))(expert_ids_keys, expert_ids_turns).reshape((TOKENS, TOP))
    gate_codes = set_ends(jax.random.randint(part_keys[2], (TOKENS, TOP), 1, 4097), jax.random.fold_in(part_keys[2], 1), 1, 4096).astype(jnp.int32)
    w_gate = gaussian(keys[3], (D, EXPERTS * HID), D ** -0.5, 0.09375, ((1, 16),))
    w_up = gaussian(keys[4], (D, EXPERTS * HID), D ** -0.5, 0.09375, ((1, 16),))
    w_down = gaussian(keys[5], (EXPERTS * HID, D), HID ** -0.5, 0.1875, ((0, 16),))
    return dict(tokens=tokens, expert_ids=expert_ids, gate_codes=gate_codes, w_gate=w_gate, w_up=w_up, w_down=w_down)


def reference(tokens, expert_ids, gate_codes, w_gate, w_up, w_down):
    blocks = N_NODE
    width = HID // SPAN
    flat = expert_ids.reshape(blocks, TOK_DEV * TOP)
    onehot = (flat[:, :, None] == jnp.arange(EXPERTS, dtype=jnp.int32)[None, None, :]).astype(jnp.int32)
    ranks = jnp.sum((jnp.cumsum(onehot, 1) - onehot) * onehot, 2).astype(jnp.int32)
    column = (jnp.arange(blocks, dtype=jnp.int32)[:, None] * CAP + ranks).astype(jnp.int32)
    owner_tok = (jnp.arange(blocks, dtype=jnp.int32)[:, None] * TOK_DEV
                 + jnp.arange(TOK_DEV * TOP, dtype=jnp.int32)[None, :] // TOP).astype(jnp.int32)
    owners = jnp.full((EXPERTS, blocks * CAP), -1, jnp.int32).at[flat, column].set(owner_tok)

    def one_expert(expert):
        who = owners[expert]
        rows = jnp.where((who >= 0)[:, None], tokens[jnp.maximum(who, 0)], jnp.zeros((), tokens.dtype))
        total = jnp.zeros((blocks * CAP, D), jnp.float32)
        for half in range(SPAN):
            start = (expert * HID + half * width).astype(jnp.int32)
            gate_cols = lax.dynamic_slice_in_dim(w_gate, start, width, 1)
            up_cols = lax.dynamic_slice_in_dim(w_up, start, width, 1)
            down_rows = lax.dynamic_slice_in_dim(w_down, start, width, 0)
            gate = jnp.dot(rows, gate_cols, preferred_element_type=jnp.float32)
            upper = jnp.dot(rows, up_cols, preferred_element_type=jnp.float32)
            hidden = (jax.nn.silu(gate) * upper).astype(jnp.bfloat16)
            partial_out = jnp.dot(hidden, down_rows, preferred_element_type=jnp.float32).astype(jnp.bfloat16)
            total = total + partial_out.astype(jnp.float32)
        return total.astype(jnp.bfloat16)

    combined = lax.map(one_expert, jnp.arange(EXPERTS, dtype=jnp.int32))
    picked = combined[flat, column].astype(jnp.float32).reshape(TOKENS, TOP, D)
    weights = gate_codes.astype(jnp.float32) * (1.0 / 4096.0)
    return jnp.sum(picked * weights[:, :, None], 1).astype(jnp.bfloat16)
```

```python
import jax
import jax.numpy as jnp
from jax import lax
from jax.sharding import PartitionSpec as P

SPAN = 2
CHUNKS = 4


def body(tokens, expert_ids, gate_codes, w_gate, w_up, w_down):
    nodes = lax.axis_size("node")
    expert = lax.axis_index("node") // SPAN
    tok, top = expert_ids.shape
    dim = tokens.shape[1]
    rows_of = tok // CHUNKS
    table = lax.all_gather(
        jnp.concatenate([expert_ids, gate_codes], 1), "node", axis=0, tiled=False
    )
    ids, codes = table[:, :, :top], table[:, :, top:]
    scale = jnp.sum(jnp.where(ids == expert, codes, 0), 2).astype(jnp.float32) * (1.0 / 4096.0)
    outs = []
    for c in range(CHUNKS):
        mine = tokens[c * rows_of : (c + 1) * rows_of]
        rows = lax.all_gather(mine, "node", axis=0, tiled=True)
        weight = scale[:, c * rows_of : (c + 1) * rows_of].reshape(nodes * rows_of, 1)
        gate = jnp.dot(rows, w_gate, preferred_element_type=jnp.float32)
        upward = jnp.dot(rows, w_up, preferred_element_type=jnp.float32)
        hidden = (jax.nn.silu(gate) * upward * weight).astype(jnp.bfloat16)
        part = jnp.dot(hidden, w_down, preferred_element_type=jnp.float32).astype(jnp.bfloat16)
        outs.append(lax.psum_scatter(part, "node", scatter_dimension=0, tiled=True))
    return jnp.concatenate(outs, 0)


def solution(mesh):
    in_specs = (
        P(("groups", "node"), None),
        P(("groups", "node"), None),
        P(("groups", "node"), None),
        P(None, "node"),
        P(None, "node"),
        P("node", None),
    )
    out_specs = P(("groups", "node"), None)
    return jax.shard_map(body, mesh=mesh, in_specs=in_specs, out_specs=out_specs, check_vma=False)
```

```python
import jax
import jax.numpy as jnp
from jax import lax
from jax.sharding import PartitionSpec as P

SPAN = 2


def body(tokens, expert_ids, gate_codes, w_gate, w_up, w_down):
    nodes = lax.axis_size("node")
    ring = nodes // SPAN
    far = ring // 2
    tok, top = expert_ids.shape
    half = tok // 2

    def chip_at(pos):
        return 2 * pos if pos < far else 2 * (ring - 1 - pos) + 1

    def perm(step):
        return [
            (chip_at(pos) * SPAN + core, chip_at((pos + step) % ring) * SPAN + core)
            for pos in range(ring)
            for core in range(SPAN)
        ]

    forward, backward = perm(1), perm(-1)
    swap = [(node, node ^ 1) for node in range(nodes)]

    me = lax.axis_index("node")
    expert, core = me // SPAN, me % SPAN
    pos = jnp.where(expert % 2 == 0, expert // 2, ring - 1 - expert // 2)

    ahead = [[tokens[:half]], [tokens[half:]]]
    behind = [[tokens[:half]], [tokens[half:]]]
    for s in range(1, far + 1):
        for h in range(2):
            if s < far or h == 0:
                ahead[h].append(lax.ppermute(ahead[h][-1], "node", forward))
            if s < far or h == 1:
                behind[h].append(lax.ppermute(behind[h][-1], "node", backward))

    others = [lax.ppermute(w, "node", swap) for w in (w_gate, w_up, w_down)]
    pairs = [(w_gate, w_up, w_down), tuple(others)]

    table = lax.all_gather(
        jnp.concatenate([expert_ids, gate_codes], 1), "node", axis=0, tiled=False
    )
    ids, codes = table[:, :, :top], table[:, :, top:]
    scale = jnp.sum(jnp.where(ids == expert, codes, 0), 2).astype(jnp.float32) * (1.0 / 4096.0)

    def scale_at(offset):
        origin = (pos + offset) % ring
        chip = jnp.where(origin < far, 2 * origin, 2 * (ring - 1 - origin) + 1)
        return lax.dynamic_index_in_dim(scale, chip * SPAN + core, 0, keepdims=False)

    def expert_part(rows, weight):
        total = None
        for gate_w, up_w, down_w in pairs:
            gate = jnp.dot(rows, gate_w, preferred_element_type=jnp.float32)
            upward = jnp.dot(rows, up_w, preferred_element_type=jnp.float32)
            hidden = (jax.nn.silu(gate) * upward * weight[:, None]).astype(jnp.bfloat16)
            part = jnp.dot(hidden, down_w, preferred_element_type=jnp.float32)
            total = part if total is None else total + part
        return total.astype(jnp.bfloat16)

    parts = {}

    def work(offsets):
        blocks, weights, names = [], [], []
        for offset in offsets:
            source = ahead if offset <= 0 else behind
            for h in range(2):
                if abs(offset) == far:
                    blocks.append((ahead, behind)[h][h][far])
                else:
                    blocks.append(source[h][abs(offset)])
                names.append((offset, h))
            weights.append(scale_at(offset))
        out = expert_part(jnp.concatenate(blocks, 0), jnp.concatenate(weights, 0))
        for i, (offset, h) in enumerate(names):
            parts[offset, h] = out[i * half : (i + 1) * half]

    work([0])
    for s in range(1, far):
        work([-s, s])
    work([far])
    parts[-far, 1] = parts[far, 1]

    def add(*terms):
        return sum(t.astype(jnp.float32) for t in terms).astype(jnp.bfloat16)

    outs = []
    for h in range(2):
        came = {}
        for sign, way in ((1, forward), (-1, backward)):
            first = far if (h == 0) == (sign == 1) else far - 1
            total = parts[sign * first, h]
            for d in range(first - 1, -1, -1):
                arrived = lax.ppermute(total, "node", way)
                total = add(parts[sign * d, h], arrived) if d else arrived
            came[sign] = total
        outs.append(add(parts[0, h], came[1], came[-1]))
    return jnp.concatenate(outs, 0)


def solution(mesh):
    in_specs = (
        P(("groups", "node"), None),
        P(("groups", "node"), None),
        P(("groups", "node"), None),
        P(None, "node"),
        P(None, "node"),
        P("node", None),
    )
    out_specs = P(("groups", "node"), None)
    return jax.shard_map(body, mesh=mesh, in_specs=in_specs, out_specs=out_specs, check_vma=False)
```

```python
import functools

import jax
import jax.numpy as jnp
from jax import lax
from jax.experimental import pallas as pl
from jax.experimental.pallas import tpu as pltpu
from jax.sharding import PartitionSpec as P

SPAN = 2
LANES = 128
DIGIT = 64
TILE = 256
WIDE = 512
MIB = 1 << 20


def expert_kernel(n, experts, dim, half, tiles, expert_ref, *refs):
    blocks, weights, outs = refs[:n], refs[n : n + 6], refs[n + 6 : 2 * n + 6]
    rows_ref, scale_ref, total_ref = refs[2 * n + 6 :]
    step = pl.program_id(0)

    @pl.when(step == 0)
    def _():
        lane = lax.broadcasted_iota(jnp.int32, (half, LANES), 1)
        expert = expert_ref[0]
        for i, block in enumerate(blocks):
            at = pl.ds(i * half, half)
            rows_ref[at, :] = block[:, :dim]
            digits = block[:, dim:].astype(jnp.float32)
            codes = jnp.where(lane == expert, digits * float(DIGIT), 0.0)
            codes = codes + jnp.where(lane == expert + experts, digits, 0.0)
            code = jnp.sum(codes, 1, keepdims=True) * (1.0 / 4096.0)
            scale_ref[at, :] = jnp.broadcast_to(code, (half, LANES))

    def add_tile(gate_ref, up_ref, down_ref, first):
        rows = rows_ref[...]
        gate = jnp.dot(rows, gate_ref[...], preferred_element_type=jnp.float32)
        upward = jnp.dot(rows, up_ref[...], preferred_element_type=jnp.float32)
        hidden = gate / (1.0 + jnp.exp(-gate)) * upward * scale_ref[:, :1]
        hidden = hidden.astype(jnp.bfloat16)
        for c in range(0, dim, WIDE):
            part = jnp.dot(hidden, down_ref[:, c : c + WIDE], preferred_element_type=jnp.float32)
            if first:
                total_ref[:, c : c + WIDE] = part
            else:
                total_ref[:, c : c + WIDE] += part

    @pl.when(step == 0)
    def _():
        add_tile(*weights[:3], True)

    @pl.when((step > 0) & (step < tiles))
    def _():
        add_tile(*weights[:3], False)

    @pl.when(step >= tiles)
    def _():
        add_tile(*weights[3:], False)

    @pl.when(step == 2 * tiles - 1)
    def _():
        for i, out in enumerate(outs):
            out[...] = total_ref[i * half : (i + 1) * half, :].astype(jnp.bfloat16)


def expert_parts(experts, expert, blocks, own, other):
    half, wide = blocks[0].shape
    dim, hid = own[0].shape
    n, tiles = len(blocks), hid // TILE

    def mine(j):
        return jnp.minimum(j, tiles - 1)

    def theirs(j):
        return jnp.maximum(j - tiles, 0)

    specs = [pl.BlockSpec(memory_space=pltpu.SMEM)]
    specs += [pl.BlockSpec((half, wide), lambda j: (0, 0))] * n
    for at in (mine, theirs):
        column = pl.BlockSpec((dim, TILE), lambda j, at=at: (0, at(j)))
        specs += [column, column, pl.BlockSpec((TILE, dim), lambda j, at=at: (at(j), 0))]
    return pl.pallas_call(
        functools.partial(expert_kernel, n, experts, dim, half, tiles),
        grid=(2 * tiles,),
        in_specs=specs,
        out_specs=[pl.BlockSpec((half, dim), lambda j: (0, 0))] * n,
        out_shape=[jax.ShapeDtypeStruct((half, dim), jnp.bfloat16)] * n,
        scratch_shapes=[
            pltpu.VMEM((n * half, dim), jnp.bfloat16),
            pltpu.VMEM((n * half, LANES), jnp.float32),
            pltpu.VMEM((n * half, dim), jnp.float32),
        ],
        compiler_params=pltpu.CompilerParams(vmem_limit_bytes=48 * MIB),
        cost_estimate=pl.CostEstimate(flops=1024, bytes_accessed=1024, transcendentals=0),
    )(expert, *blocks, *own, *other)


def add_kernel(*refs):
    total = refs[0][...].astype(jnp.float32)
    for ref in refs[1:-1]:
        total = total + ref[...].astype(jnp.float32)
    refs[-1][...] = total.astype(refs[-1].dtype)


def add(*terms):
    rows, dim = terms[0].shape
    block = pl.BlockSpec((rows, dim // 2), lambda j: (0, j))
    return pl.pallas_call(
        add_kernel,
        grid=(2,),
        in_specs=[block] * len(terms),
        out_specs=block,
        out_shape=jax.ShapeDtypeStruct((rows, dim), jnp.bfloat16),
        cost_estimate=pl.CostEstimate(flops=1024, bytes_accessed=1024, transcendentals=0),
    )(*terms)


def rows_kernel(experts, top, half, tokens_ref, ids_ref, codes_ref, *outs):
    dim = tokens_ref.shape[1]
    lane = lax.broadcasted_iota(jnp.int32, (half, LANES), 1)
    expert = jnp.where(lane < experts, lane, lane - experts)
    for i, out in enumerate(outs):
        at = pl.ds(i * half, half)
        ids, codes = ids_ref[at, :], codes_ref[at, :]
        code = jnp.zeros((half, LANES), jnp.int32)
        for k in range(top):
            code = code + jnp.where(ids[:, k : k + 1] == expert, codes[:, k : k + 1], 0)
        digits = jnp.where(lane < experts, code // DIGIT, code % DIGIT)
        out[:, :dim] = tokens_ref[at, :]
        out[:, dim:] = digits.astype(jnp.float32).astype(out.dtype)


def with_codes(experts, tokens, ids, codes):
    tok, dim = tokens.shape
    half = tok // 2
    return pl.pallas_call(
        functools.partial(rows_kernel, experts, ids.shape[1], half),
        out_shape=[jax.ShapeDtypeStruct((half, dim + LANES), tokens.dtype)] * 2,
        cost_estimate=pl.CostEstimate(flops=1024, bytes_accessed=1024, transcendentals=0),
    )(tokens, ids, codes)


def body(tokens, expert_ids, gate_codes, w_gate, w_up, w_down):
    nodes = lax.axis_size("node")
    ring = nodes // SPAN
    far = ring // 2
    tok, top = expert_ids.shape
    half = tok // 2

    def chip_at(pos):
        return 2 * pos if pos < far else 2 * (ring - 1 - pos) + 1

    def perm(step):
        return [
            (chip_at(pos) * SPAN + core, chip_at((pos + step) % ring) * SPAN + core)
            for pos in range(ring)
            for core in range(SPAN)
        ]

    forward, backward = perm(1), perm(-1)
    swap = [(node, node ^ 1) for node in range(nodes)]
    expert = (lax.axis_index("node") // SPAN).astype(jnp.int32).reshape(1)

    rows = with_codes(ring, tokens, expert_ids, gate_codes)

    ahead = [[rows[0]], [rows[1]]]
    behind = [[rows[0]], [rows[1]]]
    parts = {}

    def send(s, after):
        held = [parts[name] for name in after]
        sides = [(ahead, h, forward) for h in range(2) if s < far or h == 0]
        sides += [(behind, h, backward) for h in range(2) if s < far or h == 1]
        last = [(side, h) for side in (ahead, behind) for h in range(2)]
        if s > 1:
            blocks = [side[h][s - 1] for side, h in last]
            blocks, held = lax.optimization_barrier((blocks, held))
            parts.update(zip(after, held))
            for (side, h), block in zip(last, blocks):
                side[h][s - 1] = block
        for side, h, way in sides:
            side[h].append(lax.ppermute(side[h][s - 1], "node", way))

    def work(offsets, after=()):
        names = [(offset, h) for offset in offsets for h in range(2)]
        blocks = []
        for offset, h in names:
            if abs(offset) == far:
                blocks.append((ahead, behind)[h][h][far])
            else:
                blocks.append((ahead if offset <= 0 else behind)[h][abs(offset)])
        held = [parts[name] for name in after]
        blocks, held = lax.optimization_barrier((blocks, held))
        parts.update(zip(after, held))
        parts.update(zip(names, expert_parts(ring, expert, blocks, own, other)))
        return names

    send(1, [])
    own, _ = lax.optimization_barrier(((w_gate, w_up, w_down), rows))
    other = tuple(lax.ppermute(w, "node", swap) for w in own)
    done = []
    for s in range(2, far + 1):
        send(s, done)
        done = work([0, -1, 1] if s == 2 else [1 - s, s - 1])
    work([far], done)
    parts[-far, 1] = parts[far, 1]

    outs = []
    for h in range(2):
        came = {}
        for sign, way in ((1, forward), (-1, backward)):
            first = far if (h == 0) == (sign == 1) else far - 1
            total = parts[sign * first, h]
            for d in range(first - 1, -1, -1):
                arrived = lax.ppermute(total, "node", way)
                total = add(parts[sign * d, h], arrived) if d else arrived
            came[sign] = total
        outs.append(add(parts[0, h], came[1], came[-1]))
    return jnp.concatenate(outs, 0)


def solution(mesh):
    in_specs = (
        P(("groups", "node"), None),
        P(("groups", "node"), None),
        P(("groups", "node"), None),
        P(None, "node"),
        P(None, "node"),
        P("node", None),
    )
    out_specs = P(("groups", "node"), None)
    return jax.shard_map(body, mesh=mesh, in_specs=in_specs, out_specs=out_specs, check_vma=False)
```

```python
import functools

import jax
import jax.numpy as jnp
from jax import lax
from jax.experimental import pallas as pl
from jax.experimental.pallas import tpu as pltpu
from jax.sharding import PartitionSpec as P

SPAN = 2
LANES = 128
DIGIT = 64
TILE = 256
WIDE = 512
MIB = 1 << 20


def expert_kernel(n, experts, dim, half, expert_ref, *refs):
    blocks, weights, outs = refs[:n], refs[n : n + 6], refs[n + 6 : 2 * n + 6]
    rows_ref, scale_ref, hidden_ref = refs[2 * n + 6 :]
    hid = weights[0].shape[1]
    lane = lax.broadcasted_iota(jnp.int32, (half, LANES), 1)
    expert = expert_ref[0]
    for i, block in enumerate(blocks):
        at = pl.ds(i * half, half)
        rows_ref[at, :] = block[:, :dim]
        digits = block[:, dim:].astype(jnp.float32)
        codes = jnp.where(lane == expert, digits * float(DIGIT), 0.0)
        codes = codes + jnp.where(lane == expert + experts, digits, 0.0)
        code = jnp.sum(codes, 1, keepdims=True) * (1.0 / 4096.0)
        scale_ref[at, :] = jnp.broadcast_to(code, (half, LANES))

    for side in range(SPAN):
        gate_ref, up_ref, _ = weights[3 * side : 3 * side + 3]

        def hidden_tile(j, carry, side=side, gate_ref=gate_ref, up_ref=up_ref):
            at = pl.ds(pl.multiple_of(j * TILE, TILE), TILE)
            rows = rows_ref[...]
            gate = jnp.dot(rows, gate_ref[:, at], preferred_element_type=jnp.float32)
            upward = jnp.dot(rows, up_ref[:, at], preferred_element_type=jnp.float32)
            hidden = gate / (1.0 + jnp.exp(-gate)) * upward * scale_ref[:, :1]
            to = pl.ds(pl.multiple_of(side * hid + j * TILE, TILE), TILE)
            hidden_ref[:, to] = hidden.astype(jnp.bfloat16)
            return carry

        lax.fori_loop(0, hid // TILE, hidden_tile, 0)

    def out_tile(j, carry):
        at = pl.ds(pl.multiple_of(j * WIDE, WIDE), WIDE)
        part = jnp.dot(
            hidden_ref[:, :hid], weights[2][:, at], preferred_element_type=jnp.float32
        ) + jnp.dot(hidden_ref[:, hid:], weights[5][:, at], preferred_element_type=jnp.float32)
        part = part.astype(jnp.bfloat16)
        for i, out in enumerate(outs):
            out[:, at] = part[i * half : (i + 1) * half, :]
        return carry

    lax.fori_loop(0, dim // WIDE, out_tile, 0)


def small_cost():
    return pl.CostEstimate(flops=1024, bytes_accessed=1024, transcendentals=0)


def expert_parts(experts, expert, blocks, own, other):
    half = blocks[0].shape[0]
    dim, hid = own[0].shape
    n = len(blocks)
    specs = [pl.BlockSpec(memory_space=pltpu.SMEM)]
    specs += [pl.BlockSpec(memory_space=pltpu.VMEM)] * (n + 6)
    return pl.pallas_call(
        functools.partial(expert_kernel, n, experts, dim, half),
        in_specs=specs,
        out_specs=[pl.BlockSpec(memory_space=pltpu.VMEM)] * n,
        out_shape=[jax.ShapeDtypeStruct((half, dim), jnp.bfloat16)] * n,
        scratch_shapes=[
            pltpu.VMEM((n * half, dim), jnp.bfloat16),
            pltpu.VMEM((n * half, LANES), jnp.float32),
            pltpu.VMEM((n * half, SPAN * hid), jnp.bfloat16),
        ],
        compiler_params=pltpu.CompilerParams(vmem_limit_bytes=16 * MIB),
        cost_estimate=small_cost(),
    )(expert, *blocks, *own, *other)


def add_kernel(left_ref, right_ref, out_ref):
    total = left_ref[...].astype(jnp.float32) + right_ref[...].astype(jnp.float32)
    out_ref[...] = total.astype(out_ref.dtype)


def add(left, right):
    return pl.pallas_call(
        add_kernel,
        out_shape=jax.ShapeDtypeStruct(left.shape, left.dtype),
        cost_estimate=small_cost(),
    )(left, right)


def close_kernel(*refs):
    out_ref = refs[-1]
    half = refs[0].shape[0]
    for h in range(2):
        terms = refs[3 * h : 3 * h + 3]
        total = sum(ref[...].astype(jnp.float32) for ref in terms)
        out_ref[h * half : (h + 1) * half, :] = total.astype(out_ref.dtype)


def close(terms):
    half, dim = terms[0].shape
    return pl.pallas_call(
        close_kernel,
        out_shape=jax.ShapeDtypeStruct((2 * half, dim), terms[0].dtype),
        cost_estimate=small_cost(),
    )(*terms)


def rows_kernel(experts, top, half, tokens_ref, ids_ref, codes_ref, *outs):
    dim = tokens_ref.shape[1]
    row = lax.broadcasted_iota(jnp.int32, (LANES, 2 * half), 0)
    expert = jnp.where(row < experts, row, row - experts)
    code = jnp.zeros((LANES, 2 * half), jnp.int32)
    for k in range(top):
        code = code + jnp.where(ids_ref[k : k + 1, :] == expert, codes_ref[k : k + 1, :], 0)
    digits = jnp.where(row < experts, code // DIGIT, code % DIGIT)
    digits = jnp.transpose(digits.astype(jnp.float32)).astype(tokens_ref.dtype)
    for i, out in enumerate(outs):
        out[:, :dim] = tokens_ref[pl.ds(i * half, half), :]
        out[:, dim:] = digits[i * half : (i + 1) * half, :]


def with_codes(experts, tokens, ids, codes):
    tok, dim = tokens.shape
    half = tok // 2
    return pl.pallas_call(
        functools.partial(rows_kernel, experts, ids.shape[1], half),
        out_shape=[jax.ShapeDtypeStruct((half, dim + LANES), tokens.dtype)] * 2,
        cost_estimate=small_cost(),
    )(tokens, ids.T, codes.T)


def body(tokens, expert_ids, gate_codes, w_gate, w_up, w_down):
    nodes = lax.axis_size("node")
    ring = nodes // SPAN
    far = ring // 2
    tok, top = expert_ids.shape
    half = tok // 2

    def chip_at(pos):
        return 2 * pos if pos < far else 2 * (ring - 1 - pos) + 1

    def perm(step):
        return [
            (chip_at(pos) * SPAN + core, chip_at((pos + step) % ring) * SPAN + core)
            for pos in range(ring)
            for core in range(SPAN)
        ]

    forward, backward = perm(1), perm(-1)
    swap = [(node, node ^ 1) for node in range(nodes)]
    expert = (lax.axis_index("node") // SPAN).astype(jnp.int32).reshape(1)

    rows = with_codes(ring, tokens, expert_ids, gate_codes)

    ahead = [[rows[0]], [rows[1]]]
    behind = [[rows[0]], [rows[1]]]
    parts = {}

    def send(s, after):
        for h in range(2):
            if s > 1:
                held = [parts[name] for name in after]
                pair, held = lax.optimization_barrier(([ahead[h][s - 1], behind[h][s - 1]], held))
                parts.update(zip(after, held))
                ahead[h][s - 1], behind[h][s - 1] = pair
            if s < far or h == 0:
                ahead[h].append(lax.ppermute(ahead[h][s - 1], "node", forward))
            if s < far or h == 1:
                behind[h].append(lax.ppermute(behind[h][s - 1], "node", backward))

    def work(offsets, after=()):
        names = [(offset, h) for offset in offsets for h in range(2)]
        blocks = []
        for offset, h in names:
            if abs(offset) == far:
                blocks.append((ahead, behind)[h][h][far])
            else:
                blocks.append((ahead if offset <= 0 else behind)[h][abs(offset)])
        held = [parts[name] for name in after]
        blocks, held = lax.optimization_barrier((blocks, held))
        parts.update(zip(after, held))
        parts.update(zip(names, expert_parts(ring, expert, blocks, own, other)))
        return names

    send(1, [])
    own, _ = lax.optimization_barrier(((w_gate, w_up, w_down), rows))
    other = []
    for weight in own:
        weight, *other = lax.optimization_barrier((weight, *other))
        other.append(lax.ppermute(weight, "node", swap))
    done = []
    for s in range(2, far + 1):
        send(s, done)
        done = work([0, -1, 1] if s == 2 else [1 - s, s - 1])
    work([far], done)
    parts[-far, 1] = parts[far, 1]

    streams = [(h, sign) for h in range(2) for sign in (1, -1)]
    ways = {1: forward, -1: backward}
    early = [(h, sign) for h, sign in streams if (h == 0) != (sign == 1)]
    late = [stream for stream in streams if stream not in early]
    came = {}
    for h, sign in early:
        came[h, sign] = lax.ppermute(parts[sign * (far - 1), h], "node", ways[sign])
    first = [parts[sign * far, h] for h, sign in late]
    first, held = lax.optimization_barrier((first, [came[stream] for stream in early]))
    came.update(zip(early, held))
    for (h, sign), total in zip(late, first):
        came[h, sign] = lax.ppermute(total, "node", ways[sign])
    for d in range(far - 1, 0, -1):
        for h, sign in early + late:
            at = d - 1 if (h, sign) in early else d
            if at:
                total = add(parts[sign * at, h], came[h, sign])
                came[h, sign] = lax.ppermute(total, "node", ways[sign])
    return close([t for h in range(2) for t in (parts[0, h], came[h, 1], came[h, -1])])


def solution(mesh):
    in_specs = (
        P(("groups", "node"), None),
        P(("groups", "node"), None),
        P(("groups", "node"), None),
        P(None, "node"),
        P(None, "node"),
        P("node", None),
    )
    out_specs = P(("groups", "node"), None)
    return jax.shard_map(body, mesh=mesh, in_specs=in_specs, out_specs=out_specs, check_vma=False)
```

```python
import functools

import jax
import jax.numpy as jnp
from jax import lax
from jax.experimental import pallas as pl
from jax.experimental.pallas import tpu as pltpu
from jax.sharding import PartitionSpec as P

SPAN = 2
LANES = 128
DIGIT = 64
TILE = 256
WIDE = 512
MIB = 1 << 20


def expert_kernel(n, experts, dim, half, expert_ref, *refs):
    blocks, weights, outs = refs[:n], refs[n : n + 6], refs[n + 6 : 2 * n + 6]
    rows_ref, scale_ref, hidden_ref = refs[2 * n + 6 :]
    hid = weights[0].shape[1]
    lane = lax.broadcasted_iota(jnp.int32, (half, LANES), 1)
    expert = expert_ref[0]
    for i, block in enumerate(blocks):
        at = pl.ds(i * half, half)
        rows_ref[at, :] = block[:, :dim]
        digits = block[:, dim:].astype(jnp.float32)
        codes = jnp.where(lane == expert, digits * float(DIGIT), 0.0)
        codes = codes + jnp.where(lane == expert + experts, digits, 0.0)
        code = jnp.sum(codes, 1, keepdims=True) * (1.0 / 4096.0)
        scale_ref[at, :] = jnp.broadcast_to(code, (half, LANES))

    for side in range(SPAN):
        gate_ref, up_ref, _ = weights[3 * side : 3 * side + 3]

        def hidden_tile(j, carry, side=side, gate_ref=gate_ref, up_ref=up_ref):
            at = pl.ds(pl.multiple_of(j * TILE, TILE), TILE)
            rows = rows_ref[...]
            gate = jnp.dot(rows, gate_ref[:, at], preferred_element_type=jnp.float32)
            upward = jnp.dot(rows, up_ref[:, at], preferred_element_type=jnp.float32)
            hidden = gate / (1.0 + jnp.exp(-gate)) * upward * scale_ref[:, :1]
            to = pl.ds(pl.multiple_of(side * hid + j * TILE, TILE), TILE)
            hidden_ref[:, to] = hidden.astype(jnp.bfloat16)
            return carry

        lax.fori_loop(0, hid // TILE, hidden_tile, 0)

    def out_tile(j, carry):
        at = pl.ds(pl.multiple_of(j * WIDE, WIDE), WIDE)
        part = jnp.dot(
            hidden_ref[:, :hid], weights[2][:, at], preferred_element_type=jnp.float32
        ) + jnp.dot(hidden_ref[:, hid:], weights[5][:, at], preferred_element_type=jnp.float32)
        part = part.astype(jnp.bfloat16)
        for i, out in enumerate(outs):
            out[:, at] = part[i * half : (i + 1) * half, :]
        return carry

    lax.fori_loop(0, dim // WIDE, out_tile, 0)


def small_cost():
    return pl.CostEstimate(flops=1024, bytes_accessed=1024, transcendentals=0)


def expert_parts(experts, expert, blocks, own, other):
    half = blocks[0].shape[0]
    dim, hid = own[0].shape
    n = len(blocks)
    specs = [pl.BlockSpec(memory_space=pltpu.SMEM)]
    specs += [pl.BlockSpec(memory_space=pltpu.VMEM)] * (n + 6)
    return pl.pallas_call(
        functools.partial(expert_kernel, n, experts, dim, half),
        in_specs=specs,
        out_specs=[pl.BlockSpec(memory_space=pltpu.VMEM)] * n,
        out_shape=[jax.ShapeDtypeStruct((half, dim), jnp.bfloat16)] * n,
        scratch_shapes=[
            pltpu.VMEM((n * half, dim), jnp.bfloat16),
            pltpu.VMEM((n * half, LANES), jnp.float32),
            pltpu.VMEM((n * half, SPAN * hid), jnp.bfloat16),
        ],
        compiler_params=pltpu.CompilerParams(vmem_limit_bytes=10 * MIB),
        cost_estimate=small_cost(),
    )(expert, *blocks, *own, *other)


def add_kernel(n, *refs):
    for left_ref, right_ref, out_ref in zip(refs[:n], refs[n : 2 * n], refs[2 * n :]):
        out_ref[...] = left_ref[...] + right_ref[...]


def add(lefts, rights):
    n = len(lefts)
    return pl.pallas_call(
        functools.partial(add_kernel, n),
        out_shape=[jax.ShapeDtypeStruct(left.shape, left.dtype) for left in lefts],
        cost_estimate=small_cost(),
    )(*lefts, *rights)


def close_kernel(*refs):
    out_ref = refs[-1]
    half = refs[0].shape[0]
    for h in range(2):
        terms = refs[3 * h : 3 * h + 3]
        total = sum(ref[...].astype(jnp.float32) for ref in terms)
        out_ref[h * half : (h + 1) * half, :] = total.astype(out_ref.dtype)


def close(terms):
    half, dim = terms[0].shape
    return pl.pallas_call(
        close_kernel,
        out_shape=jax.ShapeDtypeStruct((2 * half, dim), terms[0].dtype),
        cost_estimate=small_cost(),
    )(*terms)


def rows_kernel(experts, top, half, tokens_ref, ids_ref, codes_ref, *outs):
    dim = tokens_ref.shape[1]
    row = lax.broadcasted_iota(jnp.int32, (LANES, 2 * half), 0)
    expert = jnp.where(row < experts, row, row - experts)
    code = jnp.zeros((LANES, 2 * half), jnp.int32)
    for k in range(top):
        code = code + jnp.where(ids_ref[k : k + 1, :] == expert, codes_ref[k : k + 1, :], 0)
    digits = jnp.where(row < experts, code // DIGIT, code % DIGIT)
    digits = jnp.transpose(digits.astype(jnp.float32)).astype(tokens_ref.dtype)
    for i, out in enumerate(outs):
        out[:, :dim] = tokens_ref[pl.ds(i * half, half), :]
        out[:, dim:] = digits[i * half : (i + 1) * half, :]


def with_codes(experts, tokens, ids, codes):
    tok, dim = tokens.shape
    half = tok // 2
    return pl.pallas_call(
        functools.partial(rows_kernel, experts, ids.shape[1], half),
        out_shape=[jax.ShapeDtypeStruct((half, dim + LANES), tokens.dtype)] * 2,
        cost_estimate=small_cost(),
    )(tokens, ids.T, codes.T)


def hand_on_kernel(expert_ref, *refs):
    refs[-1][0] = expert_ref[0]


def hand_on(expert, arrays):
    return pl.pallas_call(
        hand_on_kernel,
        in_specs=[pl.BlockSpec(memory_space=pltpu.SMEM)]
        + [pl.BlockSpec(memory_space=pltpu.VMEM)] * len(arrays),
        out_specs=pl.BlockSpec(memory_space=pltpu.SMEM),
        out_shape=jax.ShapeDtypeStruct(expert.shape, expert.dtype),
        cost_estimate=small_cost(),
    )(expert, *arrays)


def body(tokens, expert_ids, gate_codes, w_gate, w_up, w_down):
    nodes = lax.axis_size("node")
    ring = nodes // SPAN
    far = ring // 2
    tok, top = expert_ids.shape
    half = tok // 2

    def chip_at(pos):
        return 2 * pos if pos < far else 2 * (ring - 1 - pos) + 1

    def perm(step):
        return [
            (chip_at(pos) * SPAN + core, chip_at((pos + step) % ring) * SPAN + core)
            for pos in range(ring)
            for core in range(SPAN)
        ]

    forward, backward = perm(1), perm(-1)
    swap = [(node, node ^ 1) for node in range(nodes)]
    expert = (lax.axis_index("node") // SPAN).astype(jnp.int32).reshape(1)

    rows = with_codes(ring, tokens, expert_ids, gate_codes)

    ahead = [[rows[0]], [rows[1]]]
    behind = [[rows[0]], [rows[1]]]
    parts = {}

    def send(s, after):
        for h in range(2):
            if s > 1:
                held = [parts[name] for name in after]
                pair, held = lax.optimization_barrier(([ahead[h][s - 1], behind[h][s - 1]], held))
                parts.update(zip(after, held))
                ahead[h][s - 1], behind[h][s - 1] = pair
            if s < far or h == 0:
                ahead[h].append(lax.ppermute(ahead[h][s - 1], "node", forward))
            if s < far or h == 1:
                behind[h].append(lax.ppermute(behind[h][s - 1], "node", backward))

    def work(offsets, expert, after=()):
        names = [(offset, h) for offset in offsets for h in range(2)]
        blocks = []
        for offset, h in names:
            if abs(offset) == far:
                blocks.append((ahead, behind)[h][h][far])
            else:
                blocks.append((ahead if offset <= 0 else behind)[h][abs(offset)])
        held = [parts[name] for name in after]
        blocks, held = lax.optimization_barrier((blocks, held))
        parts.update(zip(after, held))
        parts.update(zip(names, expert_parts(ring, expert, blocks, own, other)))
        return names

    send(1, [])
    own, _ = lax.optimization_barrier(((w_gate, w_up, w_down), rows))
    expert = hand_on(expert, own)
    other = [lax.ppermute(own[0], "node", swap)]
    for h, weight in ((0, own[1]), (1, own[2])):
        pair, expert, weight = lax.optimization_barrier(
            ([ahead[h][1], behind[h][1]], expert, weight)
        )
        ahead[h][1], behind[h][1] = pair
        other.append(lax.ppermute(weight, "node", swap))
    done = []
    for s in range(2, far + 1):
        send(s, done)
        done = work([1 - s, s - 1], expert)
    work([0, far], expert, done)
    parts[-far, 1] = parts[far, 1]

    streams = [(h, sign) for h in range(2) for sign in (1, -1)]
    ways = {1: forward, -1: backward}
    early = [(h, sign) for h, sign in streams if (h == 0) != (sign == 1)]
    late = [stream for stream in streams if stream not in early]
    came = {}
    for h, sign in early:
        came[h, sign] = lax.ppermute(parts[sign * (far - 1), h], "node", ways[sign])
    first = [parts[sign * far, h] for h, sign in late]
    first, held = lax.optimization_barrier((first, [came[stream] for stream in early]))
    came.update(zip(early, held))
    for (h, sign), total in zip(late, first):
        came[h, sign] = lax.ppermute(total, "node", ways[sign])
    for d in range(far - 1, 0, -1):
        for group, at in ((early, d - 1), (late, d)):
            if at:
                lefts = [parts[sign * at, h] for h, sign in group]
                totals = add(lefts, [came[stream] for stream in group])
                for (h, sign), total in zip(group, totals):
                    came[h, sign] = lax.ppermute(total, "node", ways[sign])
    return close([t for h in range(2) for t in (parts[0, h], came[h, 1], came[h, -1])])


def solution(mesh):
    in_specs = (
        P(("groups", "node"), None),
        P(("groups", "node"), None),
        P(("groups", "node"), None),
        P(None, "node"),
        P(None, "node"),
        P("node", None),
    )
    out_specs = P(("groups", "node"), None)
    return jax.shard_map(body, mesh=mesh, in_specs=in_specs, out_specs=out_specs, check_vma=False)
```

```python
import functools

import jax
import jax.numpy as jnp
from jax import lax
from jax.experimental import pallas as pl
from jax.experimental.pallas import tpu as pltpu
from jax.sharding import PartitionSpec as P

SPAN = 2
LANES = 128
DIGIT = 64
TILE = 256
WIDE = 512
MIB = 1 << 20


def expert_kernel(n, experts, dim, half, expert_ref, *refs):
    blocks, weights, outs = refs[:n], refs[n : n + 6], refs[n + 6 : 2 * n + 6]
    rows_ref, scale_ref, hidden_ref = refs[2 * n + 6 :]
    hid = weights[0].shape[1]
    lane = lax.broadcasted_iota(jnp.int32, (half, LANES), 1)
    expert = expert_ref[0]
    for i, block in enumerate(blocks):
        at = pl.ds(i * half, half)
        rows_ref[at, :] = block[:, :dim]
        digits = block[:, dim:].astype(jnp.float32)
        codes = jnp.where(lane == expert, digits * float(DIGIT), 0.0)
        codes = codes + jnp.where(lane == expert + experts, digits, 0.0)
        code = jnp.sum(codes, 1, keepdims=True) * (1.0 / 4096.0)
        scale_ref[at, :] = jnp.broadcast_to(code, (half, LANES))

    for side in range(SPAN):
        gate_ref, up_ref, _ = weights[3 * side : 3 * side + 3]

        def hidden_tile(j, carry, side=side, gate_ref=gate_ref, up_ref=up_ref):
            at = pl.ds(pl.multiple_of(j * TILE, TILE), TILE)
            rows = rows_ref[...]
            gate = jnp.dot(rows, gate_ref[:, at], preferred_element_type=jnp.float32)
            upward = jnp.dot(rows, up_ref[:, at], preferred_element_type=jnp.float32)
            hidden = gate / (1.0 + jnp.exp(-gate)) * upward * scale_ref[:, :1]
            to = pl.ds(pl.multiple_of(side * hid + j * TILE, TILE), TILE)
            hidden_ref[:, to] = hidden.astype(jnp.bfloat16)
            return carry

        lax.fori_loop(0, hid // TILE, hidden_tile, 0)

    def out_tile(j, carry):
        at = pl.ds(pl.multiple_of(j * WIDE, WIDE), WIDE)
        part = jnp.dot(
            hidden_ref[:, :hid], weights[2][:, at], preferred_element_type=jnp.float32
        ) + jnp.dot(hidden_ref[:, hid:], weights[5][:, at], preferred_element_type=jnp.float32)
        part = part.astype(jnp.bfloat16)
        for i, out in enumerate(outs):
            out[:, at] = part[i * half : (i + 1) * half, :]
        return carry

    lax.fori_loop(0, dim // WIDE, out_tile, 0)


def small_cost():
    return pl.CostEstimate(flops=1024, bytes_accessed=1024, transcendentals=0)


def expert_parts(experts, expert, blocks, own, other):
    half = blocks[0].shape[0]
    dim, hid = own[0].shape
    n = len(blocks)
    specs = [pl.BlockSpec(memory_space=pltpu.SMEM)]
    specs += [pl.BlockSpec(memory_space=pltpu.VMEM)] * (n + 6)
    return pl.pallas_call(
        functools.partial(expert_kernel, n, experts, dim, half),
        in_specs=specs,
        out_specs=[pl.BlockSpec(memory_space=pltpu.VMEM)] * n,
        out_shape=[jax.ShapeDtypeStruct((half, dim), jnp.bfloat16)] * n,
        scratch_shapes=[
            pltpu.VMEM((n * half, dim), jnp.bfloat16),
            pltpu.VMEM((n * half, LANES), jnp.float32),
            pltpu.VMEM((n * half, SPAN * hid), jnp.bfloat16),
        ],
        compiler_params=pltpu.CompilerParams(vmem_limit_bytes=10 * MIB),
        cost_estimate=small_cost(),
    )(expert, *blocks, *own, *other)


def add_kernel(n, *refs):
    for left_ref, right_ref, out_ref in zip(refs[:n], refs[n : 2 * n], refs[-n:]):
        out_ref[...] = left_ref[...] + right_ref[...]


def add(lefts, rights, after):
    n = len(lefts)
    return pl.pallas_call(
        functools.partial(add_kernel, n),
        in_specs=[pl.BlockSpec(memory_space=pltpu.VMEM)] * (2 * n)
        + [pl.BlockSpec(memory_space=pl.ANY)] * len(after),
        out_specs=[pl.BlockSpec(memory_space=pltpu.VMEM)] * n,
        out_shape=[jax.ShapeDtypeStruct(left.shape, left.dtype) for left in lefts],
        compiler_params=pltpu.CompilerParams(vmem_limit_bytes=6 * MIB),
        cost_estimate=small_cost(),
    )(*lefts, *rights, *after)


def close_kernel(*refs):
    out_ref = refs[-1]
    half = refs[0].shape[0]
    for h in range(2):
        terms = refs[3 * h : 3 * h + 3]
        total = sum(ref[...].astype(jnp.float32) for ref in terms)
        out_ref[h * half : (h + 1) * half, :] = total.astype(out_ref.dtype)


def close(terms):
    half, dim = terms[0].shape
    return pl.pallas_call(
        close_kernel,
        out_shape=jax.ShapeDtypeStruct((2 * half, dim), terms[0].dtype),
        compiler_params=pltpu.CompilerParams(vmem_limit_bytes=8 * MIB),
        cost_estimate=small_cost(),
    )(*terms)


def rows_kernel(experts, top, half, tokens_ref, ids_ref, codes_ref, *outs):
    dim = tokens_ref.shape[1]
    row = lax.broadcasted_iota(jnp.int32, (LANES, 2 * half), 0)
    expert = jnp.where(row < experts, row, row - experts)
    code = jnp.zeros((LANES, 2 * half), jnp.int32)
    for k in range(top):
        code = code + jnp.where(ids_ref[k : k + 1, :] == expert, codes_ref[k : k + 1, :], 0)
    digits = jnp.where(row < experts, code // DIGIT, code % DIGIT)
    digits = jnp.transpose(digits.astype(jnp.float32)).astype(tokens_ref.dtype)
    for i, out in enumerate(outs):
        out[:, :dim] = tokens_ref[pl.ds(i * half, half), :]
        out[:, dim:] = digits[i * half : (i + 1) * half, :]


def with_codes(experts, tokens, ids, codes):
    tok, dim = tokens.shape
    half = tok // 2
    return pl.pallas_call(
        functools.partial(rows_kernel, experts, ids.shape[1], half),
        out_shape=[jax.ShapeDtypeStruct((half, dim + LANES), tokens.dtype)] * 2,
        compiler_params=pltpu.CompilerParams(vmem_limit_bytes=6 * MIB),
        cost_estimate=small_cost(),
    )(tokens, ids.T, codes.T)


def hand_on_kernel(expert_ref, *refs):
    refs[-1][0] = expert_ref[0]


def hand_on(expert, arrays):
    return pl.pallas_call(
        hand_on_kernel,
        in_specs=[pl.BlockSpec(memory_space=pltpu.SMEM)]
        + [pl.BlockSpec(memory_space=pltpu.VMEM)] * len(arrays),
        out_specs=pl.BlockSpec(memory_space=pltpu.SMEM),
        out_shape=jax.ShapeDtypeStruct(expert.shape, expert.dtype),
        compiler_params=pltpu.CompilerParams(vmem_limit_bytes=2 * MIB),
        cost_estimate=small_cost(),
    )(expert, *arrays)


def body(tokens, expert_ids, gate_codes, w_gate, w_up, w_down):
    nodes = lax.axis_size("node")
    ring = nodes // SPAN
    far = ring // 2
    tok, top = expert_ids.shape
    half = tok // 2

    def chip_at(pos):
        return 2 * pos if pos < far else 2 * (ring - 1 - pos) + 1

    def perm(step):
        return [
            (chip_at(pos) * SPAN + core, chip_at((pos + step) % ring) * SPAN + core)
            for pos in range(ring)
            for core in range(SPAN)
        ]

    forward, backward = perm(1), perm(-1)
    swap = [(node, node ^ 1) for node in range(nodes)]
    expert = (lax.axis_index("node") // SPAN).astype(jnp.int32).reshape(1)

    rows = with_codes(ring, tokens, expert_ids, gate_codes)

    ahead = [[rows[0]], [rows[1]]]
    behind = [[rows[0]], [rows[1]]]
    parts = {}

    def send(s, after=(), behind_half=0):
        for h in range(2):
            if s > 1:
                names = after if h == behind_half else ()
                held = [parts[name] for name in names]
                pair, held = lax.optimization_barrier(([ahead[h][s - 1], behind[h][s - 1]], held))
                parts.update(zip(names, held))
                ahead[h][s - 1], behind[h][s - 1] = pair
            if s < far or h == 0:
                ahead[h].append(lax.ppermute(ahead[h][s - 1], "node", forward))
            if s < far or h == 1:
                behind[h].append(lax.ppermute(behind[h][s - 1], "node", backward))

    def work(offsets, expert, after=()):
        names = [(offset, h) for offset in offsets for h in range(2)]
        blocks = []
        for offset, h in names:
            if abs(offset) == far:
                blocks.append((ahead, behind)[h][h][far])
            else:
                blocks.append((ahead if offset <= 0 else behind)[h][abs(offset)])
        held = [parts[name] for name in after]
        blocks, held = lax.optimization_barrier((blocks, held))
        parts.update(zip(after, held))
        parts.update(zip(names, expert_parts(ring, expert, blocks, own, other)))
        return names

    send(1)
    own, _ = lax.optimization_barrier(((w_gate, w_up, w_down), rows))
    expert = hand_on(expert, own)
    other = [lax.ppermute(own[0], "node", swap)]
    arrived = [ahead[0][1], behind[0][1], ahead[1][1], behind[1][1]]
    arrived, expert, up, down = lax.optimization_barrier((arrived, expert, own[1], own[2]))
    ahead[0][1], behind[0][1], ahead[1][1], behind[1][1] = arrived
    other += [lax.ppermute(up, "node", swap), lax.ppermute(down, "node", swap)]
    done = []
    for s in range(2, far + 1):
        send(s, done, 1 if s < far else 0)
        done = work([1 - s, s - 1], expert)
    work([0, far], expert, done)
    parts[-far, 1] = parts[far, 1]

    streams = [(h, sign) for h in range(2) for sign in (1, -1)]
    ways = {1: forward, -1: backward}
    early = [(h, sign) for h, sign in streams if (h == 0) != (sign == 1)]
    late = [stream for stream in streams if stream not in early]
    came = {}

    def pass_on(group, totals):
        for (h, sign), total in zip(group, totals):
            came[h, sign] = lax.ppermute(total, "node", ways[sign])

    def summed(group, at, after=()):
        lefts = [parts[sign * at, h] for h, sign in group]
        return add(lefts, [came[stream] for stream in group], after)

    pass_on(early, [parts[sign * (far - 1), h] for h, sign in early])
    late_totals = [parts[sign * far, h] for h, sign in late]
    held = [came[stream] for stream in early]
    late_totals, held = lax.optimization_barrier((late_totals, held))
    came.update(zip(early, held))
    for at in range(far - 1, -1, -1):
        if at > 1:
            pass_on(early, summed(early, at - 1))
        pass_on(late, late_totals)
        if at:
            late_totals = summed(late, at, [came[stream] for stream in early])
    return close([t for h in range(2) for t in (parts[0, h], came[h, 1], came[h, -1])])


def solution(mesh):
    in_specs = (
        P(("groups", "node"), None),
        P(("groups", "node"), None),
        P(("groups", "node"), None),
        P(None, "node"),
        P(None, "node"),
        P("node", None),
    )
    out_specs = P(("groups", "node"), None)
    return jax.shard_map(body, mesh=mesh, in_specs=in_specs, out_specs=out_specs, check_vma=False)
```

```python
import functools

import jax
import jax.numpy as jnp
from jax import lax
from jax.experimental import pallas as pl
from jax.experimental.pallas import tpu as pltpu
from jax.sharding import PartitionSpec as P

SPAN = 2
LANES = 128
DIGIT = 64
TILE = 256
WIDE = 512
MIB = 1 << 20


def expert_kernel(n, experts, dim, half, expert_ref, *refs):
    blocks, weights, outs = refs[:n], refs[n : n + 6], refs[n + 6 : -3]
    rows_ref, scale_ref, hidden_ref = refs[-3:]
    hid = weights[0].shape[1]
    expert = expert_ref[0]
    first = 0
    for block in blocks:
        count = block.shape[0]
        lane = lax.broadcasted_iota(jnp.int32, (count, LANES), 1)
        at = pl.ds(first, count)
        first += count
        rows_ref[at, :] = block[:, :dim]
        digits = block[:, dim:].astype(jnp.float32)
        codes = jnp.where(lane == expert, digits * float(DIGIT), 0.0)
        codes = codes + jnp.where(lane == expert + experts, digits, 0.0)
        code = jnp.sum(codes, 1, keepdims=True) * (1.0 / 4096.0)
        scale_ref[at, :] = jnp.broadcast_to(code, (count, LANES))

    for side in range(SPAN):
        gate_ref, up_ref, _ = weights[3 * side : 3 * side + 3]

        def hidden_tile(j, carry, side=side, gate_ref=gate_ref, up_ref=up_ref):
            at = pl.ds(pl.multiple_of(j * TILE, TILE), TILE)
            rows = rows_ref[...]
            gate = jnp.dot(rows, gate_ref[:, at], preferred_element_type=jnp.float32)
            upward = jnp.dot(rows, up_ref[:, at], preferred_element_type=jnp.float32)
            hidden = gate / (1.0 + jnp.exp(-gate)) * upward * scale_ref[:, :1]
            to = pl.ds(pl.multiple_of(side * hid + j * TILE, TILE), TILE)
            hidden_ref[:, to] = hidden.astype(jnp.bfloat16)
            return carry

        lax.fori_loop(0, hid // TILE, hidden_tile, 0)

    def out_tile(j, carry):
        at = pl.ds(pl.multiple_of(j * WIDE, WIDE), WIDE)
        part = jnp.dot(
            hidden_ref[:, :hid], weights[2][:, at], preferred_element_type=jnp.float32
        ) + jnp.dot(hidden_ref[:, hid:], weights[5][:, at], preferred_element_type=jnp.float32)
        part = part.astype(jnp.bfloat16)
        for i, out in enumerate(outs):
            out[:, at] = part[i * half : (i + 1) * half, :]
        return carry

    lax.fori_loop(0, dim // WIDE, out_tile, 0)


def small_cost():
    return pl.CostEstimate(flops=1024, bytes_accessed=1024, transcendentals=0)


def expert_parts(experts, half, expert, blocks, own, other):
    dim, hid = own[0].shape
    n, rows = len(blocks), sum(block.shape[0] for block in blocks)
    specs = [pl.BlockSpec(memory_space=pltpu.SMEM)]
    specs += [pl.BlockSpec(memory_space=pltpu.VMEM)] * (n + 6)
    return pl.pallas_call(
        functools.partial(expert_kernel, n, experts, dim, half),
        in_specs=specs,
        out_specs=[pl.BlockSpec(memory_space=pltpu.VMEM)] * (rows // half),
        out_shape=[jax.ShapeDtypeStruct((half, dim), jnp.bfloat16)] * (rows // half),
        scratch_shapes=[
            pltpu.VMEM((rows, dim), jnp.bfloat16),
            pltpu.VMEM((rows, LANES), jnp.float32),
            pltpu.VMEM((rows, SPAN * hid), jnp.bfloat16),
        ],
        compiler_params=pltpu.CompilerParams(vmem_limit_bytes=(13 if rows <= 256 else 16) * MIB),
        cost_estimate=small_cost(),
    )(expert, *blocks, *own, *other)


def add_kernel(n, pieces, first, *refs):
    outs = refs[-n * pieces :]
    size = outs[0].shape[0]
    for i, (left_ref, right_ref) in enumerate(zip(refs[:n], refs[n : 2 * n])):
        for p in range(pieces):
            left = left_ref[first + p * size : first + (p + 1) * size, :]
            outs[i * pieces + p][...] = left + right_ref[p * size : (p + 1) * size, :]


def add(lefts, rights, after=(), pieces=1, first=0):
    n = len(lefts)
    rows, dim = rights[0].shape
    shape = jax.ShapeDtypeStruct((rows // pieces, dim), rights[0].dtype)
    return pl.pallas_call(
        functools.partial(add_kernel, n, pieces, first),
        in_specs=[pl.BlockSpec(memory_space=pltpu.VMEM)] * (2 * n)
        + [pl.BlockSpec(memory_space=pl.ANY)] * len(after),
        out_specs=[pl.BlockSpec(memory_space=pltpu.VMEM)] * (n * pieces),
        out_shape=[shape] * (n * pieces),
        compiler_params=pltpu.CompilerParams(vmem_limit_bytes=6 * MIB),
        cost_estimate=small_cost(),
    )(*lefts, *rights, *after)


def split_kernel(n, *refs):
    for i, ref in enumerate(refs[:n]):
        half = ref.shape[0] // 2
        for h in range(2):
            refs[n + 2 * i + h][...] = ref[h * half : (h + 1) * half, :]


def split(arrays):
    n = len(arrays)
    rows, dim = arrays[0].shape
    return pl.pallas_call(
        functools.partial(split_kernel, n),
        in_specs=[pl.BlockSpec(memory_space=pltpu.VMEM)] * n,
        out_specs=[pl.BlockSpec(memory_space=pltpu.VMEM)] * (2 * n),
        out_shape=[jax.ShapeDtypeStruct((rows // 2, dim), arrays[0].dtype)] * (2 * n),
        compiler_params=pltpu.CompilerParams(vmem_limit_bytes=6 * MIB),
        cost_estimate=small_cost(),
    )(*arrays)


def close_kernel(halves, *refs):
    out_ref, taken = refs[-1], 0
    for h, pieces in enumerate(halves):
        base_ref, whole_ref = refs[taken : taken + 2]
        half = base_ref.shape[0]
        size = half // pieces
        for p in range(pieces):
            at = slice(p * size, (p + 1) * size)
            total = base_ref[at, :].astype(jnp.float32) + whole_ref[at, :].astype(jnp.float32)
            total = total + refs[taken + 2 + p][...].astype(jnp.float32)
            out_ref[h * half + p * size : h * half + (p + 1) * size, :] = total.astype(out_ref.dtype)
        taken += 2 + pieces


def close(halves):
    half, dim = halves[0][0].shape
    terms = [term for terms in halves for term in terms]
    return pl.pallas_call(
        functools.partial(close_kernel, [len(terms) - 2 for terms in halves]),
        in_specs=[pl.BlockSpec(memory_space=pltpu.VMEM)] * len(terms),
        out_shape=jax.ShapeDtypeStruct((2 * half, dim), terms[0].dtype),
        compiler_params=pltpu.CompilerParams(vmem_limit_bytes=8 * MIB),
        cost_estimate=small_cost(),
    )(*terms)


def rows_kernel(experts, top, tokens_ref, ids_ref, codes_ref, out_ref):
    tok, dim = tokens_ref.shape
    row = lax.broadcasted_iota(jnp.int32, (LANES, tok), 0)
    expert = jnp.where(row < experts, row, row - experts)
    code = jnp.zeros((LANES, tok), jnp.int32)
    for k in range(top):
        code = code + jnp.where(ids_ref[k : k + 1, :] == expert, codes_ref[k : k + 1, :], 0)
    digits = jnp.where(row < experts, code // DIGIT, code % DIGIT)
    out_ref[:, :dim] = tokens_ref[...]
    out_ref[:, dim:] = jnp.transpose(digits.astype(jnp.float32)).astype(out_ref.dtype)


def with_codes(experts, tokens, ids, codes):
    tok, dim = tokens.shape
    return pl.pallas_call(
        functools.partial(rows_kernel, experts, ids.shape[1]),
        out_shape=jax.ShapeDtypeStruct((tok, dim + LANES), tokens.dtype),
        compiler_params=pltpu.CompilerParams(vmem_limit_bytes=6 * MIB),
        cost_estimate=small_cost(),
    )(tokens, ids.T, codes.T)


def hand_on_kernel(expert_ref, *refs):
    refs[-1][0] = expert_ref[0]


def hand_on(expert, arrays):
    return pl.pallas_call(
        hand_on_kernel,
        in_specs=[pl.BlockSpec(memory_space=pltpu.SMEM)]
        + [pl.BlockSpec(memory_space=pltpu.VMEM)] * len(arrays),
        out_specs=pl.BlockSpec(memory_space=pltpu.SMEM),
        out_shape=jax.ShapeDtypeStruct(expert.shape, expert.dtype),
        compiler_params=pltpu.CompilerParams(vmem_limit_bytes=2 * MIB),
        cost_estimate=small_cost(),
    )(expert, *arrays)


def body(tokens, expert_ids, gate_codes, w_gate, w_up, w_down):
    nodes = lax.axis_size("node")
    ring = nodes // SPAN
    far = ring // 2
    tok, top = expert_ids.shape
    half = tok // 2

    def chip_at(pos):
        return 2 * pos if pos < far else 2 * (ring - 1 - pos) + 1

    def perm(step):
        return [
            (chip_at(pos) * SPAN + core, chip_at((pos + step) % ring) * SPAN + core)
            for pos in range(ring)
            for core in range(SPAN)
        ]

    forward, backward = perm(1), perm(-1)
    swap = [(node, node ^ 1) for node in range(nodes)]
    expert = (lax.axis_index("node") // SPAN).astype(jnp.int32).reshape(1)

    rows = with_codes(ring, tokens, expert_ids, gate_codes)

    near = [lax.ppermute(rows, "node", forward), lax.ppermute(rows, "node", backward)]
    own, _ = lax.optimization_barrier(((w_gate, w_up, w_down), rows))
    expert = hand_on(expert, own)
    other = [lax.ppermute(weight, "node", swap) for weight in own]

    near, expert = lax.optimization_barrier((near, expert))
    halves = split(near)
    ahead, behind = ([None, halves[0]], [None, halves[1]]), ([None, halves[2]], [None, halves[3]])
    parts = {}

    def work(names, blocks, after=()):
        held = [parts[name] for name in after]
        blocks, held = lax.optimization_barrier((blocks, held))
        parts.update(zip(after, held))
        parts.update(zip(names, expert_parts(ring, half, expert, blocks, own, other)))
        return names

    def send(s, h, after):
        held = [parts[name] for name in after]
        pair, held = lax.optimization_barrier(([ahead[h][s - 1], behind[h][s - 1]], held))
        parts.update(zip(after, held))
        ahead[h][s - 1], behind[h][s - 1] = pair
        if s < far or h == 0:
            ahead[h].append(lax.ppermute(ahead[h][s - 1], "node", forward))
        if s < far or h == 1:
            behind[h].append(lax.ppermute(behind[h][s - 1], "node", backward))

    for h in range(2):
        send(2, h, [])
    names = [(offset, h) for offset in (0, -1, 1) for h in range(2)]
    done = [work(names, [rows, *near])]
    for s in range(3, far + 1):
        for h in range(2):
            send(s, h, done.pop(0))
            done.append(work([(1 - s, h), (s - 1, h)], [ahead[h][s - 1], behind[h][s - 1]]))
    last = done.pop()
    firsts = [(1 - far, 0), (far - 1, 1)]
    held, ahead[0][far] = lax.optimization_barrier(
        ([parts[name] for name in firsts], ahead[0][far])
    )
    parts.update(zip(firsts, held))
    work([(far, 0), (far, 1)], [ahead[0][far], behind[1][far]], last)
    parts[-far, 1] = parts[far, 1]

    streams = [(h, sign) for h in range(2) for sign in (1, -1)]
    ways = {1: forward, -1: backward}
    early = [(h, sign) for h, sign in streams if (h == 0) != (sign == 1)]
    late = [stream for stream in streams if stream not in early]
    came = {}

    def pass_on(group, totals):
        for (h, sign), total in zip(group, totals):
            came[h, sign] = lax.ppermute(total, "node", ways[sign])

    def summed(group, at, after=(), **how):
        lefts = [parts[sign * at, h] for h, sign in group]
        return add(lefts, [came[stream] for stream in group], after, **how)

    pass_on(early, [parts[sign * (far - 1), h] for h, sign in early])
    late_totals = [parts[sign * far, h] for h, sign in late]
    held = [came[stream] for stream in early]
    late_totals, held = lax.optimization_barrier((late_totals, held))
    came.update(zip(early, held))
    for at in range(far - 1, 1, -1):
        pass_on(early, summed(early, at - 1))
        pass_on(late, late_totals)
        waited = [came[stream] for stream in early]
        late_totals = summed(late, at, waited, pieces=2 if at == 2 else 1)

    pieces = []
    for p in range(2):
        pass_on(late, late_totals[p::2])
        pass_on(late, summed(late, 1, first=p * (half // 2)))
        pieces.append([came[stream] for stream in late])
    shorter = dict(early)
    return close(
        [
            [parts[0, h], came[h, shorter[h]], *(piece[h] for piece in pieces)]
            for h in range(2)
        ]
    )


def solution(mesh):
    in_specs = (
        P(("groups", "node"), None),
        P(("groups", "node"), None),
        P(("groups", "node"), None),
        P(None, "node"),
        P(None, "node"),
        P("node", None),
    )
    out_specs = P(("groups", "node"), None)
    return jax.shard_map(body, mesh=mesh, in_specs=in_specs, out_specs=out_specs, check_vma=False)
```

```python
import functools

import jax
import jax.numpy as jnp
from jax import lax
from jax.experimental import pallas as pl
from jax.experimental.pallas import tpu as pltpu
from jax.sharding import PartitionSpec as P

SPAN = 2
LANES = 128
DIGIT = 64
TILE = 256
WIDE = 512
MIB = 1 << 20


def expert_kernel(n, experts, dim, half, expert_ref, *refs):
    blocks, weights, outs = refs[:n], refs[n : n + 6], refs[n + 6 : -3]
    rows_ref, scale_ref, hidden_ref = refs[-3:]
    hid = weights[0].shape[1]
    expert = expert_ref[0]
    first = 0
    for block in blocks:
        count = block.shape[0]
        lane = lax.broadcasted_iota(jnp.int32, (count, LANES), 1)
        at = pl.ds(first, count)
        first += count
        rows_ref[at, :] = block[:, :dim]
        digits = block[:, dim:].astype(jnp.float32)
        codes = jnp.where(lane == expert, digits * float(DIGIT), 0.0)
        codes = codes + jnp.where(lane == expert + experts, digits, 0.0)
        code = jnp.sum(codes, 1, keepdims=True) * (1.0 / 4096.0)
        scale_ref[at, :] = jnp.broadcast_to(code, (count, LANES))

    for side in range(SPAN):
        gate_ref, up_ref, _ = weights[3 * side : 3 * side + 3]

        def hidden_tile(j, carry, side=side, gate_ref=gate_ref, up_ref=up_ref):
            at = pl.ds(pl.multiple_of(j * TILE, TILE), TILE)
            rows = rows_ref[...]
            gate = jnp.dot(rows, gate_ref[:, at], preferred_element_type=jnp.float32)
            upward = jnp.dot(rows, up_ref[:, at], preferred_element_type=jnp.float32)
            hidden = gate / (1.0 + jnp.exp(-gate)) * upward * scale_ref[:, :1]
            to = pl.ds(pl.multiple_of(side * hid + j * TILE, TILE), TILE)
            hidden_ref[:, to] = hidden.astype(jnp.bfloat16)
            return carry

        lax.fori_loop(0, hid // TILE, hidden_tile, 0)

    def out_tile(j, carry):
        at = pl.ds(pl.multiple_of(j * WIDE, WIDE), WIDE)
        part = jnp.dot(
            hidden_ref[:, :hid], weights[2][:, at], preferred_element_type=jnp.float32
        ) + jnp.dot(hidden_ref[:, hid:], weights[5][:, at], preferred_element_type=jnp.float32)
        part = part.astype(jnp.bfloat16)
        for i, out in enumerate(outs):
            out[:, at] = part[i * half : (i + 1) * half, :]
        return carry

    lax.fori_loop(0, dim // WIDE, out_tile, 0)


def small_cost():
    return pl.CostEstimate(flops=1024, bytes_accessed=1024, transcendentals=0)


def expert_parts(experts, half, expert, blocks, own, other):
    dim, hid = own[0].shape
    n, rows = len(blocks), sum(block.shape[0] for block in blocks)
    specs = [pl.BlockSpec(memory_space=pltpu.SMEM)]
    specs += [pl.BlockSpec(memory_space=pltpu.VMEM)] * (n + 6)
    return pl.pallas_call(
        functools.partial(expert_kernel, n, experts, dim, half),
        in_specs=specs,
        out_specs=[pl.BlockSpec(memory_space=pltpu.VMEM)] * (rows // half),
        out_shape=[jax.ShapeDtypeStruct((half, dim), jnp.bfloat16)] * (rows // half),
        scratch_shapes=[
            pltpu.VMEM((rows, dim), jnp.bfloat16),
            pltpu.VMEM((rows, LANES), jnp.float32),
            pltpu.VMEM((rows, SPAN * hid), jnp.bfloat16),
        ],
        compiler_params=pltpu.CompilerParams(vmem_limit_bytes=8 * MIB),
        cost_estimate=small_cost(),
    )(expert, *blocks, *own, *other)


def add_kernel(n, pieces, first, *refs):
    outs = refs[-n * pieces :]
    size = outs[0].shape[0]
    for i, (left_ref, right_ref) in enumerate(zip(refs[:n], refs[n : 2 * n])):
        for p in range(pieces):
            left = left_ref[first + p * size : first + (p + 1) * size, :]
            outs[i * pieces + p][...] = left + right_ref[p * size : (p + 1) * size, :]


def add(lefts, rights, after=(), pieces=1, first=0):
    n = len(lefts)
    rows, dim = rights[0].shape
    shape = jax.ShapeDtypeStruct((rows // pieces, dim), rights[0].dtype)
    return pl.pallas_call(
        functools.partial(add_kernel, n, pieces, first),
        in_specs=[pl.BlockSpec(memory_space=pltpu.VMEM)] * (2 * n)
        + [pl.BlockSpec(memory_space=pl.ANY)] * len(after),
        out_specs=[pl.BlockSpec(memory_space=pltpu.VMEM)] * (n * pieces),
        out_shape=[shape] * (n * pieces),
        compiler_params=pltpu.CompilerParams(vmem_limit_bytes=6 * MIB),
        cost_estimate=small_cost(),
    )(*lefts, *rights, *after)


def split_kernel(n, *refs):
    for i, ref in enumerate(refs[:n]):
        half = ref.shape[0] // 2
        for h in range(2):
            refs[n + 2 * i + h][...] = ref[h * half : (h + 1) * half, :]


def split(arrays):
    n = len(arrays)
    rows, dim = arrays[0].shape
    return pl.pallas_call(
        functools.partial(split_kernel, n),
        in_specs=[pl.BlockSpec(memory_space=pltpu.VMEM)] * n,
        out_specs=[pl.BlockSpec(memory_space=pltpu.VMEM)] * (2 * n),
        out_shape=[jax.ShapeDtypeStruct((rows // 2, dim), arrays[0].dtype)] * (2 * n),
        compiler_params=pltpu.CompilerParams(vmem_limit_bytes=6 * MIB),
        cost_estimate=small_cost(),
    )(*arrays)


def close_kernel(halves, *refs):
    out_ref, taken = refs[-1], 0
    for h, pieces in enumerate(halves):
        base_ref, whole_ref = refs[taken : taken + 2]
        half = base_ref.shape[0]
        size = half // pieces
        for p in range(pieces):
            at = slice(p * size, (p + 1) * size)
            total = base_ref[at, :].astype(jnp.float32) + whole_ref[at, :].astype(jnp.float32)
            total = total + refs[taken + 2 + p][...].astype(jnp.float32)
            out_ref[h * half + p * size : h * half + (p + 1) * size, :] = total.astype(out_ref.dtype)
        taken += 2 + pieces


def close(halves):
    half, dim = halves[0][0].shape
    terms = [term for terms in halves for term in terms]
    return pl.pallas_call(
        functools.partial(close_kernel, [len(terms) - 2 for terms in halves]),
        in_specs=[pl.BlockSpec(memory_space=pltpu.VMEM)] * len(terms),
        out_shape=jax.ShapeDtypeStruct((2 * half, dim), terms[0].dtype),
        compiler_params=pltpu.CompilerParams(vmem_limit_bytes=8 * MIB),
        cost_estimate=small_cost(),
    )(*terms)


def rows_kernel(experts, top, tokens_ref, ids_ref, codes_ref, out_ref):
    tok, dim = tokens_ref.shape
    row = lax.broadcasted_iota(jnp.int32, (LANES, tok), 0)
    expert = jnp.where(row < experts, row, row - experts)
    code = jnp.zeros((LANES, tok), jnp.int32)
    for k in range(top):
        code = code + jnp.where(ids_ref[k : k + 1, :] == expert, codes_ref[k : k + 1, :], 0)
    digits = jnp.where(row < experts, code // DIGIT, code % DIGIT)
    out_ref[:, :dim] = tokens_ref[...]
    out_ref[:, dim:] = jnp.transpose(digits.astype(jnp.float32)).astype(out_ref.dtype)


def with_codes(experts, tokens, ids, codes):
    tok, dim = tokens.shape
    return pl.pallas_call(
        functools.partial(rows_kernel, experts, ids.shape[1]),
        out_shape=jax.ShapeDtypeStruct((tok, dim + LANES), tokens.dtype),
        compiler_params=pltpu.CompilerParams(vmem_limit_bytes=6 * MIB),
        cost_estimate=small_cost(),
    )(tokens, ids.T, codes.T)


def bring_in_kernel(n, *refs):
    copies = [
        pltpu.make_async_copy(refs[i], refs[n + i], refs[2 * n].at[i]) for i in range(n)
    ]
    for copy in copies:
        copy.start()
    for copy in copies:
        copy.wait()


def bring_in(arrays):
    n = len(arrays)
    return pl.pallas_call(
        functools.partial(bring_in_kernel, n),
        in_specs=[pl.BlockSpec(memory_space=pl.ANY)] * n,
        out_specs=[pl.BlockSpec(memory_space=pltpu.VMEM)] * n,
        out_shape=[jax.ShapeDtypeStruct(array.shape, array.dtype) for array in arrays],
        scratch_shapes=[pltpu.SemaphoreType.DMA((n,))],
        compiler_params=pltpu.CompilerParams(vmem_limit_bytes=2 * MIB),
        cost_estimate=small_cost(),
    )(*arrays)


def body(tokens, expert_ids, gate_codes, w_gate, w_up, w_down):
    nodes = lax.axis_size("node")
    ring = nodes // SPAN
    far = ring // 2
    tok, top = expert_ids.shape
    half = tok // 2

    def chip_at(pos):
        return 2 * pos if pos < far else 2 * (ring - 1 - pos) + 1

    def perm(step):
        return [
            (chip_at(pos) * SPAN + core, chip_at((pos + step) % ring) * SPAN + core)
            for pos in range(ring)
            for core in range(SPAN)
        ]

    forward, backward = perm(1), perm(-1)
    swap = [(node, node ^ 1) for node in range(nodes)]
    expert = lax.div(lax.axis_index("node"), jnp.int32(SPAN)).reshape(1)
    tokens, expert = lax.optimization_barrier((tokens, expert))

    rows = with_codes(ring, tokens, expert_ids, gate_codes)

    near = [lax.ppermute(rows, "node", forward), lax.ppermute(rows, "node", backward)]
    weights, _ = lax.optimization_barrier(((w_gate, w_up, w_down), rows))
    other = [lax.ppermute(weight, "node", swap) for weight in weights]
    own = bring_in(weights)

    near, own = lax.optimization_barrier((near, own))
    halves = split(near)
    ahead, behind = ([None, halves[0]], [None, halves[1]]), ([None, halves[2]], [None, halves[3]])
    parts = {}

    def work(names, blocks, after=()):
        held = [parts[name] for name in after]
        blocks, held = lax.optimization_barrier((blocks, held))
        parts.update(zip(after, held))
        parts.update(zip(names, expert_parts(ring, half, expert, blocks, own, other)))
        return names

    def send(s, h, after):
        held = [parts[name] for name in after]
        pair, held = lax.optimization_barrier(([ahead[h][s - 1], behind[h][s - 1]], held))
        parts.update(zip(after, held))
        ahead[h][s - 1], behind[h][s - 1] = pair
        if s < far or h == 0:
            ahead[h].append(lax.ppermute(ahead[h][s - 1], "node", forward))
        if s < far or h == 1:
            behind[h].append(lax.ppermute(behind[h][s - 1], "node", backward))

    for h in range(2):
        send(2, h, [])
    names = [(offset, h) for offset in (0, -1, 1) for h in range(2)]
    done = [work(names, [rows, *near])]
    for s in range(3, far + 1):
        for h in range(2):
            send(s, h, done.pop(0))
            done.append(work([(1 - s, h), (s - 1, h)], [ahead[h][s - 1], behind[h][s - 1]]))
    last = done.pop()
    firsts = [(1 - far, 0), (far - 1, 1)]
    held, ahead[0][far] = lax.optimization_barrier(
        ([parts[name] for name in firsts], ahead[0][far])
    )
    parts.update(zip(firsts, held))
    work([(far, 0), (far, 1)], [ahead[0][far], behind[1][far]], last)
    parts[-far, 1] = parts[far, 1]

    streams = [(h, sign) for h in range(2) for sign in (1, -1)]
    ways = {1: forward, -1: backward}
    early = [(h, sign) for h, sign in streams if (h == 0) != (sign == 1)]
    late = [stream for stream in streams if stream not in early]
    came = {}

    def pass_on(group, totals):
        for (h, sign), total in zip(group, totals):
            came[h, sign] = lax.ppermute(total, "node", ways[sign])

    def summed(group, at, after=(), **how):
        lefts = [parts[sign * at, h] for h, sign in group]
        return add(lefts, [came[stream] for stream in group], after, **how)

    pass_on(early, [parts[sign * (far - 1), h] for h, sign in early])
    late_totals = [parts[sign * far, h] for h, sign in late]
    held = [came[stream] for stream in early]
    late_totals, held = lax.optimization_barrier((late_totals, held))
    came.update(zip(early, held))
    for at in range(far - 1, 1, -1):
        pass_on(early, summed(early, at - 1))
        pass_on(late, late_totals)
        waited = [came[stream] for stream in early]
        late_totals = summed(late, at, waited, pieces=2 if at == 2 else 1)

    pieces = []
    for p in range(2):
        pass_on(late, late_totals[p::2])
        pass_on(late, summed(late, 1, first=p * (half // 2)))
        pieces.append([came[stream] for stream in late])
    shorter = dict(early)
    return close(
        [
            [parts[0, h], came[h, shorter[h]], *(piece[h] for piece in pieces)]
            for h in range(2)
        ]
    )


def solution(mesh):
    in_specs = (
        P(("groups", "node"), None),
        P(("groups", "node"), None),
        P(("groups", "node"), None),
        P(None, "node"),
        P(None, "node"),
        P("node", None),
    )
    out_specs = P(("groups", "node"), None)
    return jax.shard_map(body, mesh=mesh, in_specs=in_specs, out_specs=out_specs, check_vma=False)
```

```python
import functools

import jax
import jax.numpy as jnp
from jax import lax
from jax.experimental import pallas as pl
from jax.experimental.pallas import tpu as pltpu
from jax.sharding import PartitionSpec as P

SPAN = 2
LANES = 128
DIGIT = 64
TILE = 256
WIDE = 512
MIB = 1 << 20
AHEAD = 6 * MIB


def expert_kernel(n, experts, dim, half, expert_ref, *refs):
    blocks, weights, outs = refs[:n], refs[n : n + 6], refs[n + 6 : -3]
    rows_ref, scale_ref, hidden_ref = refs[-3:]
    hid = weights[0].shape[1]
    expert = expert_ref[0]
    first = 0
    for block in blocks:
        count = block.shape[0]
        lane = lax.broadcasted_iota(jnp.int32, (count, LANES), 1)
        at = pl.ds(first, count)
        first += count
        rows_ref[at, :] = block[:, :dim]
        digits = block[:, dim:].astype(jnp.float32)
        codes = jnp.where(lane == expert, digits * float(DIGIT), 0.0)
        codes = codes + jnp.where(lane == expert + experts, digits, 0.0)
        code = jnp.sum(codes, 1, keepdims=True) * (1.0 / 4096.0)
        scale_ref[at, :] = jnp.broadcast_to(code, (count, LANES))

    for side in range(SPAN):
        gate_ref, up_ref, _ = weights[3 * side : 3 * side + 3]

        def hidden_tile(j, carry, side=side, gate_ref=gate_ref, up_ref=up_ref):
            at = pl.ds(pl.multiple_of(j * TILE, TILE), TILE)
            rows = rows_ref[...]
            gate = jnp.dot(rows, gate_ref[:, at], preferred_element_type=jnp.float32)
            upward = jnp.dot(rows, up_ref[:, at], preferred_element_type=jnp.float32)
            hidden = gate / (1.0 + jnp.exp(-gate)) * upward * scale_ref[:, :1]
            to = pl.ds(pl.multiple_of(side * hid + j * TILE, TILE), TILE)
            hidden_ref[:, to] = hidden.astype(jnp.bfloat16)
            return carry

        lax.fori_loop(0, hid // TILE, hidden_tile, 0)

    def out_tile(j, carry):
        at = pl.ds(pl.multiple_of(j * WIDE, WIDE), WIDE)
        part = jnp.dot(
            hidden_ref[:, :hid], weights[2][:, at], preferred_element_type=jnp.float32
        ) + jnp.dot(hidden_ref[:, hid:], weights[5][:, at], preferred_element_type=jnp.float32)
        part = part.astype(jnp.bfloat16)
        for i, out in enumerate(outs):
            out[:, at] = part[i * half : (i + 1) * half, :]
        return carry

    lax.fori_loop(0, dim // WIDE, out_tile, 0)


def small_cost():
    return pl.CostEstimate(flops=1024, bytes_accessed=1024, transcendentals=0)


def expert_parts(experts, half, expert, blocks, own, other):
    dim, hid = own[0].shape
    n, rows = len(blocks), sum(block.shape[0] for block in blocks)
    specs = [pl.BlockSpec(memory_space=pltpu.SMEM)]
    specs += [pl.BlockSpec(memory_space=pltpu.VMEM)] * (n + 6)
    return pl.pallas_call(
        functools.partial(expert_kernel, n, experts, dim, half),
        in_specs=specs,
        out_specs=[pl.BlockSpec(memory_space=pltpu.VMEM)] * (rows // half),
        out_shape=[jax.ShapeDtypeStruct((half, dim), jnp.bfloat16)] * (rows // half),
        scratch_shapes=[
            pltpu.VMEM((rows, dim), jnp.bfloat16),
            pltpu.VMEM((rows, LANES), jnp.float32),
            pltpu.VMEM((rows, SPAN * hid), jnp.bfloat16),
        ],
        compiler_params=pltpu.CompilerParams(vmem_limit_bytes=8 * MIB),
        cost_estimate=small_cost(),
    )(expert, *blocks, *own, *other)


def add_kernel(n, pieces, first, *refs):
    outs = refs[-n * pieces :]
    size = outs[0].shape[0]
    for i, (left_ref, right_ref) in enumerate(zip(refs[:n], refs[n : 2 * n])):
        for p in range(pieces):
            left = left_ref[first + p * size : first + (p + 1) * size, :]
            right = right_ref[p * size : (p + 1) * size, :]
            out = outs[i * pieces + p]
            out[...] = left.astype(out.dtype) + right.astype(out.dtype)


def add(lefts, rights, after=(), pieces=1, first=0, dtype=None, cost=1024):
    n = len(lefts)
    rows, dim = rights[0].shape
    shape = jax.ShapeDtypeStruct((rows // pieces, dim), dtype or rights[0].dtype)
    return pl.pallas_call(
        functools.partial(add_kernel, n, pieces, first),
        in_specs=[pl.BlockSpec(memory_space=pltpu.VMEM)] * (2 * n)
        + [pl.BlockSpec(memory_space=pl.ANY)] * len(after),
        out_specs=[pl.BlockSpec(memory_space=pltpu.VMEM)] * (n * pieces),
        out_shape=[shape] * (n * pieces),
        compiler_params=pltpu.CompilerParams(vmem_limit_bytes=6 * MIB),
        cost_estimate=pl.CostEstimate(flops=1024, bytes_accessed=cost, transcendentals=0),
    )(*lefts, *rights, *after)


def split_kernel(n, *refs):
    for i, ref in enumerate(refs[:n]):
        half = ref.shape[0] // 2
        for h in range(2):
            refs[n + 2 * i + h][...] = ref[h * half : (h + 1) * half, :]


def split(arrays):
    n = len(arrays)
    rows, dim = arrays[0].shape
    return pl.pallas_call(
        functools.partial(split_kernel, n),
        in_specs=[pl.BlockSpec(memory_space=pltpu.VMEM)] * n,
        out_specs=[pl.BlockSpec(memory_space=pltpu.VMEM)] * (2 * n),
        out_shape=[jax.ShapeDtypeStruct((rows // 2, dim), arrays[0].dtype)] * (2 * n),
        compiler_params=pltpu.CompilerParams(vmem_limit_bytes=6 * MIB),
        cost_estimate=small_cost(),
    )(*arrays)


def close_kernel(*refs):
    out_ref, bases, pieces = refs[-1], refs[:2], refs[2:-1]
    size = pieces[0].shape[0]
    for h, base_ref in enumerate(bases):
        half = base_ref.shape[0]
        for p in range(len(pieces) // 2):
            at = slice(p * size, (p + 1) * size)
            total = base_ref[at, :] + pieces[2 * p + h][...].astype(jnp.float32)
            out_ref[h * half + p * size : h * half + (p + 1) * size, :] = total.astype(out_ref.dtype)


def close(bases, pieces):
    terms = [term for piece in pieces for term in piece]
    half, dim = bases[0].shape
    return pl.pallas_call(
        close_kernel,
        in_specs=[pl.BlockSpec(memory_space=pltpu.VMEM)] * (len(terms) + 2),
        out_shape=jax.ShapeDtypeStruct((2 * half, dim), terms[0].dtype),
        compiler_params=pltpu.CompilerParams(vmem_limit_bytes=8 * MIB),
        cost_estimate=small_cost(),
    )(*bases, *terms)


def rows_kernel(experts, top, tokens_ref, ids_ref, codes_ref, out_ref):
    tok, dim = tokens_ref.shape
    row = lax.broadcasted_iota(jnp.int32, (LANES, tok), 0)
    expert = jnp.where(row < experts, row, row - experts)
    code = jnp.zeros((LANES, tok), jnp.int32)
    for k in range(top):
        code = code + jnp.where(ids_ref[k : k + 1, :] == expert, codes_ref[k : k + 1, :], 0)
    digits = jnp.where(row < experts, code // DIGIT, code % DIGIT)
    out_ref[:, :dim] = tokens_ref[...]
    out_ref[:, dim:] = jnp.transpose(digits.astype(jnp.float32)).astype(out_ref.dtype)


def with_codes(experts, tokens, ids, codes):
    tok, dim = tokens.shape
    return pl.pallas_call(
        functools.partial(rows_kernel, experts, ids.shape[1]),
        out_shape=jax.ShapeDtypeStruct((tok, dim + LANES), tokens.dtype),
        compiler_params=pltpu.CompilerParams(vmem_limit_bytes=6 * MIB),
        cost_estimate=small_cost(),
    )(tokens, ids.T, codes.T)


def bring_in_kernel(n, *refs):
    copies = [
        pltpu.make_async_copy(refs[i], refs[n + i], refs[2 * n].at[i]) for i in range(n)
    ]
    for copy in copies:
        copy.start()
    for copy in copies:
        copy.wait()


def bring_in(arrays):
    n = len(arrays)
    return pl.pallas_call(
        functools.partial(bring_in_kernel, n),
        in_specs=[pl.BlockSpec(memory_space=pl.ANY)] * n,
        out_specs=[pl.BlockSpec(memory_space=pltpu.VMEM)] * n,
        out_shape=[jax.ShapeDtypeStruct(array.shape, array.dtype) for array in arrays],
        scratch_shapes=[pltpu.SemaphoreType.DMA((n,))],
        compiler_params=pltpu.CompilerParams(vmem_limit_bytes=2 * MIB),
        cost_estimate=small_cost(),
    )(*arrays)


def body(tokens, expert_ids, gate_codes, w_gate, w_up, w_down):
    nodes = lax.axis_size("node")
    ring = nodes // SPAN
    far = ring // 2
    tok, top = expert_ids.shape
    half = tok // 2

    def chip_at(pos):
        return 2 * pos if pos < far else 2 * (ring - 1 - pos) + 1

    def perm(step):
        return [
            (chip_at(pos) * SPAN + core, chip_at((pos + step) % ring) * SPAN + core)
            for pos in range(ring)
            for core in range(SPAN)
        ]

    forward, backward = perm(1), perm(-1)
    swap = [(node, node ^ 1) for node in range(nodes)]
    expert = lax.div(lax.axis_index("node"), jnp.int32(SPAN)).reshape(1)
    tokens, expert = lax.optimization_barrier((tokens, expert))

    rows = with_codes(ring, tokens, expert_ids, gate_codes)

    near = [lax.ppermute(rows, "node", forward), lax.ppermute(rows, "node", backward)]
    weights, _ = lax.optimization_barrier(((w_gate, w_up, w_down), rows))
    other = [lax.ppermute(weight, "node", swap) for weight in weights]
    own = bring_in(weights)

    near, own = lax.optimization_barrier((near, own))
    halves = split(near)
    ahead, behind = ([None, halves[0]], [None, halves[1]]), ([None, halves[2]], [None, halves[3]])
    parts = {}

    def work(names, blocks, after=()):
        held = [parts[name] for name in after]
        blocks, held = lax.optimization_barrier((blocks, held))
        parts.update(zip(after, held))
        parts.update(zip(names, expert_parts(ring, half, expert, blocks, own, other)))
        return names

    def send(s, h, after):
        held = [parts[name] for name in after]
        pair, held = lax.optimization_barrier(([ahead[h][s - 1], behind[h][s - 1]], held))
        parts.update(zip(after, held))
        ahead[h][s - 1], behind[h][s - 1] = pair
        if s < far or h == 0:
            ahead[h].append(lax.ppermute(ahead[h][s - 1], "node", forward))
        if s < far or h == 1:
            behind[h].append(lax.ppermute(behind[h][s - 1], "node", backward))

    for h in range(2):
        send(2, h, [])
    names = [(offset, h) for offset in (0, -1, 1) for h in range(2)]
    done = [work(names, [rows, *near])]
    for s in range(3, far + 1):
        for h in range(2):
            send(s, h, done.pop(0))
            done.append(work([(1 - s, h), (s - 1, h)], [ahead[h][s - 1], behind[h][s - 1]]))
    last = done.pop()
    firsts = [(far - 1, 1)]
    held, ahead[0][far] = lax.optimization_barrier(
        ([parts[name] for name in firsts], ahead[0][far])
    )
    parts.update(zip(firsts, held))
    work([(far, 0), (far, 1)], [ahead[0][far], behind[1][far]], last)
    parts[-far, 1] = parts[far, 1]

    early = [(h, sign) for h in range(2) for sign in (1, -1) if (h == 0) != (sign == 1)]
    late = [(h, -sign) for h, sign in early]
    ways = {1: forward, -1: backward}

    def pass_on(group, totals):
        return [lax.ppermute(t, "node", ways[sign]) for t, (h, sign) in zip(totals, group)]

    def shares(group, offset):
        return [parts[sign * offset, h] for h, sign in group]

    first = pass_on(early, shares(early, far - 1))
    last = [pass_on(late, shares(late, far))]
    for k in range(2, far + 1):
        if k < far:
            first = pass_on(early, add(shares(early, far - k), first, cost=AHEAD))
            after = []
        else:
            first = add(shares(early, 0), first, dtype=jnp.float32, cost=AHEAD)
            after = first
        terms = shares(late, far - k + 1)
        if k == far - 1:
            totals = add(terms, last[0], after, pieces=2)
            last = [pass_on(late, totals[p::2]) for p in range(2)]
        else:
            size = half // len(last)
            last = [
                pass_on(late, add(terms, came, after, first=p * size))
                for p, came in enumerate(last)
            ]
    return close(first, last)


def solution(mesh):
    in_specs = (
        P(("groups", "node"), None),
        P(("groups", "node"), None),
        P(("groups", "node"), None),
        P(None, "node"),
        P(None, "node"),
        P("node", None),
    )
    out_specs = P(("groups", "node"), None)
    return jax.shard_map(body, mesh=mesh, in_specs=in_specs, out_specs=out_specs, check_vma=False)
```

```python
import functools

import jax
import jax.numpy as jnp
from jax import lax
from jax.experimental import pallas as pl
from jax.experimental.pallas import tpu as pltpu
from jax.sharding import PartitionSpec as P

SPAN = 2
LANES = 128
DIGIT = 64
TILE = 256
WIDE = 512
MIB = 1 << 20
AHEAD = 6 * MIB


def expert_kernel(n, experts, dim, half, expert_ref, *refs):
    blocks, weights, outs = refs[:n], refs[n : n + 6], refs[n + 6 : -3]
    rows_ref, scale_ref, hidden_ref = refs[-3:]
    hid = weights[0].shape[1]
    expert = expert_ref[0]
    first = 0
    for block in blocks:
        count = block.shape[0]
        lane = lax.broadcasted_iota(jnp.int32, (count, LANES), 1)
        at = pl.ds(first, count)
        first += count
        rows_ref[at, :] = block[:, :dim]
        digits = block[:, dim:].astype(jnp.float32)
        codes = jnp.where(lane == expert, digits * float(DIGIT), 0.0)
        codes = codes + jnp.where(lane == expert + experts, digits, 0.0)
        code = jnp.sum(codes, 1, keepdims=True) * (1.0 / 4096.0)
        scale_ref[at, :] = jnp.broadcast_to(code, (count, LANES))

    for side in range(SPAN):
        gate_ref, up_ref, _ = weights[3 * side : 3 * side + 3]

        def hidden_tile(j, carry, side=side, gate_ref=gate_ref, up_ref=up_ref):
            at = pl.ds(pl.multiple_of(j * TILE, TILE), TILE)
            rows = rows_ref[...]
            gate = jnp.dot(rows, gate_ref[:, at], preferred_element_type=jnp.float32)
            upward = jnp.dot(rows, up_ref[:, at], preferred_element_type=jnp.float32)
            hidden = gate / (1.0 + jnp.exp(-gate)) * upward * scale_ref[:, :1]
            to = pl.ds(pl.multiple_of(side * hid + j * TILE, TILE), TILE)
            hidden_ref[:, to] = hidden.astype(jnp.bfloat16)
            return carry

        lax.fori_loop(0, hid // TILE, hidden_tile, 0)

    def out_tile(j, carry):
        at = pl.ds(pl.multiple_of(j * WIDE, WIDE), WIDE)
        part = jnp.dot(
            hidden_ref[:, :hid], weights[2][:, at], preferred_element_type=jnp.float32
        ) + jnp.dot(hidden_ref[:, hid:], weights[5][:, at], preferred_element_type=jnp.float32)
        part = part.astype(jnp.bfloat16)
        for i, out in enumerate(outs):
            out[:, at] = part[i * half : (i + 1) * half, :]
        return carry

    lax.fori_loop(0, dim // WIDE, out_tile, 0)


def small_cost():
    return pl.CostEstimate(flops=1024, bytes_accessed=1024, transcendentals=0)


def expert_parts(experts, half, expert, blocks, own, other, cost=1024):
    dim, hid = own[0].shape
    n, rows = len(blocks), sum(block.shape[0] for block in blocks)
    specs = [pl.BlockSpec(memory_space=pltpu.SMEM)]
    specs += [pl.BlockSpec(memory_space=pltpu.VMEM)] * (n + 6)
    return pl.pallas_call(
        functools.partial(expert_kernel, n, experts, dim, half),
        in_specs=specs,
        out_specs=[pl.BlockSpec(memory_space=pltpu.VMEM)] * (rows // half),
        out_shape=[jax.ShapeDtypeStruct((half, dim), jnp.bfloat16)] * (rows // half),
        scratch_shapes=[
            pltpu.VMEM((rows, dim), jnp.bfloat16),
            pltpu.VMEM((rows, LANES), jnp.float32),
            pltpu.VMEM((rows, SPAN * hid), jnp.bfloat16),
        ],
        compiler_params=pltpu.CompilerParams(vmem_limit_bytes=8 * MIB),
        cost_estimate=pl.CostEstimate(flops=1024, bytes_accessed=cost, transcendentals=0),
    )(expert, *blocks, *own, *other)


def add_kernel(n, pieces, first, *refs):
    outs = refs[-n * pieces :]
    size = outs[0].shape[0]
    for i, (left_ref, right_ref) in enumerate(zip(refs[:n], refs[n : 2 * n])):
        for p in range(pieces):
            left = left_ref[first + p * size : first + (p + 1) * size, :]
            right = right_ref[p * size : (p + 1) * size, :]
            out = outs[i * pieces + p]
            out[...] = left.astype(out.dtype) + right.astype(out.dtype)


def add(lefts, rights, after=(), pieces=1, first=0, dtype=None, cost=1024):
    n = len(lefts)
    rows, dim = rights[0].shape
    shape = jax.ShapeDtypeStruct((rows // pieces, dim), dtype or rights[0].dtype)
    return pl.pallas_call(
        functools.partial(add_kernel, n, pieces, first),
        in_specs=[pl.BlockSpec(memory_space=pltpu.VMEM)] * (2 * n)
        + [pl.BlockSpec(memory_space=pl.ANY)] * len(after),
        out_specs=[pl.BlockSpec(memory_space=pltpu.VMEM)] * (n * pieces),
        out_shape=[shape] * (n * pieces),
        compiler_params=pltpu.CompilerParams(vmem_limit_bytes=6 * MIB),
        cost_estimate=pl.CostEstimate(flops=1024, bytes_accessed=cost, transcendentals=0),
    )(*lefts, *rights, *after)


def split_kernel(n, *refs):
    for i, ref in enumerate(refs[:n]):
        half = ref.shape[0] // 2
        for h in range(2):
            refs[n + 2 * i + h][...] = ref[h * half : (h + 1) * half, :]


def split(arrays):
    n = len(arrays)
    rows, dim = arrays[0].shape
    return pl.pallas_call(
        functools.partial(split_kernel, n),
        in_specs=[pl.BlockSpec(memory_space=pltpu.VMEM)] * n,
        out_specs=[pl.BlockSpec(memory_space=pltpu.VMEM)] * (2 * n),
        out_shape=[jax.ShapeDtypeStruct((rows // 2, dim), arrays[0].dtype)] * (2 * n),
        compiler_params=pltpu.CompilerParams(vmem_limit_bytes=6 * MIB),
        cost_estimate=small_cost(),
    )(*arrays)


def close_kernel(*refs):
    out_ref, bases, pieces = refs[-1], refs[:2], refs[2:-1]
    size = pieces[0].shape[0]
    for h, base_ref in enumerate(bases):
        half = base_ref.shape[0]
        for p in range(len(pieces) // 2):
            at = slice(p * size, (p + 1) * size)
            total = base_ref[at, :] + pieces[2 * p + h][...].astype(jnp.float32)
            out_ref[h * half + p * size : h * half + (p + 1) * size, :] = total.astype(out_ref.dtype)


def close(bases, pieces):
    terms = [term for piece in pieces for term in piece]
    half, dim = bases[0].shape
    return pl.pallas_call(
        close_kernel,
        in_specs=[pl.BlockSpec(memory_space=pltpu.VMEM)] * (len(terms) + 2),
        out_shape=jax.ShapeDtypeStruct((2 * half, dim), terms[0].dtype),
        compiler_params=pltpu.CompilerParams(vmem_limit_bytes=8 * MIB),
        cost_estimate=small_cost(),
    )(*bases, *terms)


def rows_kernel(experts, top, tokens_ref, ids_ref, codes_ref, out_ref):
    tok, dim = tokens_ref.shape
    row = lax.broadcasted_iota(jnp.int32, (LANES, tok), 0)
    expert = jnp.where(row < experts, row, row - experts)
    code = jnp.zeros((LANES, tok), jnp.int32)
    for k in range(top):
        code = code + jnp.where(ids_ref[k : k + 1, :] == expert, codes_ref[k : k + 1, :], 0)
    digits = jnp.where(row < experts, code // DIGIT, code % DIGIT)
    out_ref[:, :dim] = tokens_ref[...]
    out_ref[:, dim:] = jnp.transpose(digits.astype(jnp.float32)).astype(out_ref.dtype)


def with_codes(experts, tokens, ids, codes):
    tok, dim = tokens.shape
    return pl.pallas_call(
        functools.partial(rows_kernel, experts, ids.shape[1]),
        out_shape=jax.ShapeDtypeStruct((tok, dim + LANES), tokens.dtype),
        compiler_params=pltpu.CompilerParams(vmem_limit_bytes=6 * MIB),
        cost_estimate=small_cost(),
    )(tokens, ids.T, codes.T)


def bring_in_kernel(n, *refs):
    copies = [
        pltpu.make_async_copy(refs[i], refs[n + i], refs[2 * n].at[i]) for i in range(n)
    ]
    for copy in copies:
        copy.start()
    for copy in copies:
        copy.wait()


def bring_in(arrays):
    n = len(arrays)
    return pl.pallas_call(
        functools.partial(bring_in_kernel, n),
        in_specs=[pl.BlockSpec(memory_space=pl.ANY)] * n,
        out_specs=[pl.BlockSpec(memory_space=pltpu.VMEM)] * n,
        out_shape=[jax.ShapeDtypeStruct(array.shape, array.dtype) for array in arrays],
        scratch_shapes=[pltpu.SemaphoreType.DMA((n,))],
        compiler_params=pltpu.CompilerParams(vmem_limit_bytes=2 * MIB),
        cost_estimate=small_cost(),
    )(*arrays)


def body(tokens, expert_ids, gate_codes, w_gate, w_up, w_down):
    nodes = lax.axis_size("node")
    ring = nodes // SPAN
    far = ring // 2
    tok, top = expert_ids.shape
    half = tok // 2

    def chip_at(pos):
        return 2 * pos if pos < far else 2 * (ring - 1 - pos) + 1

    def perm(step):
        return [
            (chip_at(pos) * SPAN + core, chip_at((pos + step) % ring) * SPAN + core)
            for pos in range(ring)
            for core in range(SPAN)
        ]

    forward, backward = perm(1), perm(-1)
    swap = [(node, node ^ 1) for node in range(nodes)]
    expert = lax.div(lax.axis_index("node"), jnp.int32(SPAN)).reshape(1)
    tokens, expert = lax.optimization_barrier((tokens, expert))

    rows = with_codes(ring, tokens, expert_ids, gate_codes)

    near = [lax.ppermute(rows, "node", forward), lax.ppermute(rows, "node", backward)]
    weights, _ = lax.optimization_barrier(((w_gate, w_up, w_down), rows))
    other = [lax.ppermute(weight, "node", swap) for weight in weights]
    own = bring_in(weights)

    near, own = lax.optimization_barrier((near, own))
    halves = split(near)
    ahead = [[None, halves[0]], [None, halves[1]]]
    behind = [[None, halves[3]], [None, halves[2]]]
    parts = {}

    def work(names, blocks, after=(), **how):
        held = [parts[name] for name in after]
        blocks, held = lax.optimization_barrier((blocks, held))
        parts.update(zip(after, held))
        parts.update(zip(names, expert_parts(ring, half, expert, blocks, own, other, **how)))
        return names

    def send(s, wave, after):
        held = [parts[name] for name in after]
        pair, held = lax.optimization_barrier(((ahead[wave][-1], behind[wave][-1]), held))
        parts.update(zip(after, held))
        ahead[wave][-1], behind[wave][-1] = pair
        ahead[wave].append(lax.ppermute(pair[0], "node", forward))
        behind[wave].append(lax.ppermute(pair[1], "node", backward))

    for wave in range(2):
        send(2, wave, [])
    names = [(offset, h) for offset in (0, -1, 1) for h in range(2)]
    done = [work(names, [rows, *near])]
    for s in range(3, far + 1):
        for wave in range(2):
            if s < far or wave == 0:
                send(s, wave, done.pop(0))
            names = [(1 - s, wave), (s - 1, 1 - wave)]
            after = done[-1] if s == far and wave == 1 else []
            done.append(work(names, [ahead[wave][s - 1], behind[wave][s - 1]], after))
    work([(far, 0), (far, 1)], [ahead[0][far], behind[0][far]], done[-1])
    parts[-far, 1] = parts[far, 1]

    firsts = [(1 - far, 0), (far - 1, 1)]
    held, after = lax.optimization_barrier(
        ([parts[name] for name in firsts], [parts[name] for name in done[-1]])
    )
    parts.update(zip(firsts, held))
    parts.update(zip(done[-1], after))

    early = [(h, sign) for h in range(2) for sign in (1, -1) if (h == 0) != (sign == 1)]
    late = [(h, -sign) for h, sign in early]
    ways = {1: forward, -1: backward}

    def pass_on(group, totals):
        return [lax.ppermute(t, "node", ways[sign]) for t, (h, sign) in zip(totals, group)]

    def shares(group, offset):
        return [parts[sign * offset, h] for h, sign in group]

    first = pass_on(early, shares(early, far - 1))
    last = [pass_on(late, shares(late, far))]
    for k in range(2, far + 1):
        if k < far:
            first = pass_on(early, add(shares(early, far - k), first, cost=AHEAD))
            after = []
        else:
            first = add(shares(early, 0), first, dtype=jnp.float32, cost=AHEAD)
            after = first
        terms = shares(late, far - k + 1)
        if k == far - 1:
            totals = add(terms, last[0], after, pieces=2)
            last = [pass_on(late, totals[p::2]) for p in range(2)]
        else:
            size = half // len(last)
            last = [
                pass_on(late, add(terms, came, after, first=p * size))
                for p, came in enumerate(last)
            ]
    return close(first, last)


def solution(mesh):
    in_specs = (
        P(("groups", "node"), None),
        P(("groups", "node"), None),
        P(("groups", "node"), None),
        P(None, "node"),
        P(None, "node"),
        P("node", None),
    )
    out_specs = P(("groups", "node"), None)
    return jax.shard_map(body, mesh=mesh, in_specs=in_specs, out_specs=out_specs, check_vma=False)
```

```python
import functools

import jax
import jax.numpy as jnp
from jax import lax
from jax.experimental import pallas as pl
from jax.experimental.pallas import tpu as pltpu
from jax.sharding import PartitionSpec as P

SPAN = 2
LANES = 128
TILE = 256
WIDE = 512
MIB = 1 << 20
FORWARD = 40 * 10**9


def expert_kernel(marks, ring, dim, half, chip_ref, table_ref, *refs):
    n = len(marks)
    blocks, weights, outs = refs[:n], refs[n : n + 6], refs[n + 6 : -3]
    rows_ref, scale_ref, hidden_ref = refs[-3:]
    hid = weights[0].shape[1]
    table = table_ref[...]
    filler = jnp.zeros((LANES - table.shape[0], table.shape[1]), table.dtype)
    table = jnp.transpose(jnp.concatenate([table, filler], 0))
    lane = lax.broadcasted_iota(jnp.int32, table.shape, 1)
    chip = chip_ref[0]
    pos = jnp.where(lax.rem(chip, 2) == 0, lax.div(chip, 2), ring - 1 - lax.div(chip, 2))
    first = 0
    for (offset, start), block in zip(marks, blocks):
        count = block.shape[0]
        origin = lax.rem(pos + (offset + ring), ring)
        origin = jnp.where(origin < ring // 2, 2 * origin, 2 * (ring - 1 - origin) + 1)
        scale = jnp.sum(jnp.where(lane == origin, table, 0.0), 1, keepdims=True)
        at = pl.ds(first, count)
        first += count
        rows_ref[at, :] = block[...]
        scale_ref[at, :] = jnp.broadcast_to(scale[start : start + count], (count, LANES))

    for side in range(SPAN):
        gate_ref, up_ref, _ = weights[3 * side : 3 * side + 3]

        def hidden_tile(j, carry, side=side, gate_ref=gate_ref, up_ref=up_ref):
            at = pl.ds(pl.multiple_of(j * TILE, TILE), TILE)
            rows = rows_ref[...]
            gate = jnp.dot(rows, gate_ref[:, at], preferred_element_type=jnp.float32)
            upward = jnp.dot(rows, up_ref[:, at], preferred_element_type=jnp.float32)
            hidden = gate / (1.0 + jnp.exp(-gate)) * upward * scale_ref[:, :1]
            to = pl.ds(pl.multiple_of(side * hid + j * TILE, TILE), TILE)
            hidden_ref[:, to] = hidden.astype(jnp.bfloat16)
            return carry

        lax.fori_loop(0, hid // TILE, hidden_tile, 0)

    def out_tile(j, carry):
        at = pl.ds(pl.multiple_of(j * WIDE, WIDE), WIDE)
        part = jnp.dot(
            hidden_ref[:, :hid], weights[2][:, at], preferred_element_type=jnp.float32
        ) + jnp.dot(hidden_ref[:, hid:], weights[5][:, at], preferred_element_type=jnp.float32)
        part = part.astype(jnp.bfloat16)
        for i, out in enumerate(outs):
            out[:, at] = part[i * half : (i + 1) * half, :]
        return carry

    lax.fori_loop(0, dim // WIDE, out_tile, 0)


def small_cost():
    return pl.CostEstimate(flops=1024, bytes_accessed=1024, transcendentals=0)


def expert_parts(marks, ring, half, chip, table, blocks, own, other):
    dim, hid = own[0].shape
    n, rows = len(blocks), sum(block.shape[0] for block in blocks)
    specs = [pl.BlockSpec(memory_space=pltpu.SMEM)]
    specs += [pl.BlockSpec(memory_space=pltpu.VMEM)] * (n + 7)
    return pl.pallas_call(
        functools.partial(expert_kernel, marks, ring, dim, half),
        in_specs=specs,
        out_specs=[pl.BlockSpec(memory_space=pltpu.VMEM)] * (rows // half),
        out_shape=[jax.ShapeDtypeStruct((half, dim), jnp.bfloat16)] * (rows // half),
        scratch_shapes=[
            pltpu.VMEM((rows, dim), jnp.bfloat16),
            pltpu.VMEM((rows, LANES), jnp.float32),
            pltpu.VMEM((rows, SPAN * hid), jnp.bfloat16),
        ],
        compiler_params=pltpu.CompilerParams(vmem_limit_bytes=8 * MIB),
        cost_estimate=small_cost(),
    )(chip, table, *blocks, *own, *other)


def add_kernel(n, pieces, first, *refs):
    outs = refs[-n * pieces :]
    size = outs[0].shape[0]
    for i, (left_ref, right_ref) in enumerate(zip(refs[:n], refs[n : 2 * n])):
        for p in range(pieces):
            left = left_ref[first + p * size : first + (p + 1) * size, :]
            right = right_ref[p * size : (p + 1) * size, :]
            out = outs[i * pieces + p]
            out[...] = left.astype(out.dtype) + right.astype(out.dtype)


def add(lefts, rights, after=(), pieces=1, first=0, dtype=None):
    n = len(lefts)
    rows, dim = rights[0].shape
    shape = jax.ShapeDtypeStruct((rows // pieces, dim), dtype or rights[0].dtype)
    return pl.pallas_call(
        functools.partial(add_kernel, n, pieces, first),
        in_specs=[pl.BlockSpec(memory_space=pltpu.VMEM)] * (2 * n)
        + [pl.BlockSpec(memory_space=pl.ANY)] * len(after),
        out_specs=[pl.BlockSpec(memory_space=pltpu.VMEM)] * (n * pieces),
        out_shape=[shape] * (n * pieces),
        compiler_params=pltpu.CompilerParams(vmem_limit_bytes=6 * MIB),
        cost_estimate=small_cost(),
    )(*lefts, *rights, *after)


def split_kernel(n, *refs):
    for i, ref in enumerate(refs[:n]):
        half = ref.shape[0] // 2
        for h in range(2):
            refs[n + 2 * i + h][...] = ref[h * half : (h + 1) * half, :]


def split(arrays):
    n = len(arrays)
    rows, dim = arrays[0].shape
    return pl.pallas_call(
        functools.partial(split_kernel, n),
        in_specs=[pl.BlockSpec(memory_space=pltpu.VMEM)] * n,
        out_specs=[pl.BlockSpec(memory_space=pltpu.VMEM)] * (2 * n),
        out_shape=[jax.ShapeDtypeStruct((rows // 2, dim), arrays[0].dtype)] * (2 * n),
        compiler_params=pltpu.CompilerParams(vmem_limit_bytes=6 * MIB),
        cost_estimate=pl.CostEstimate(flops=FORWARD, bytes_accessed=1024, transcendentals=0),
    )(*arrays)


def close_kernel(*refs):
    out_ref, bases, pieces = refs[-1], refs[:2], refs[2:-1]
    size = pieces[0].shape[0]
    for h, base_ref in enumerate(bases):
        half = base_ref.shape[0]
        for p in range(len(pieces) // 2):
            at = slice(p * size, (p + 1) * size)
            total = base_ref[at, :] + pieces[2 * p + h][...].astype(jnp.float32)
            out_ref[h * half + p * size : h * half + (p + 1) * size, :] = total.astype(out_ref.dtype)


def close(bases, pieces):
    terms = [term for piece in pieces for term in piece]
    half, dim = bases[0].shape
    return pl.pallas_call(
        close_kernel,
        in_specs=[pl.BlockSpec(memory_space=pltpu.VMEM)] * (len(terms) + 2),
        out_shape=jax.ShapeDtypeStruct((2 * half, dim), terms[0].dtype),
        compiler_params=pltpu.CompilerParams(vmem_limit_bytes=8 * MIB),
        cost_estimate=small_cost(),
    )(*bases, *terms)


def table_kernel(ids_ref, codes_ref, out_ref):
    expert = lax.broadcasted_iota(jnp.int32, out_ref.shape, 0)
    code = jnp.zeros(out_ref.shape, jnp.int32)
    for k in range(ids_ref.shape[0]):
        code = code + jnp.where(ids_ref[k : k + 1, :] == expert, codes_ref[k : k + 1, :], 0)
    out_ref[...] = code.astype(jnp.float32) * (1.0 / 4096.0)


def gate_table(experts, ids, codes):
    return pl.pallas_call(
        table_kernel,
        in_specs=[pl.BlockSpec(memory_space=pltpu.VMEM)] * 2,
        out_shape=jax.ShapeDtypeStruct((experts, ids.shape[0]), jnp.float32),
        compiler_params=pltpu.CompilerParams(vmem_limit_bytes=2 * MIB),
        cost_estimate=small_cost(),
    )(ids.T, codes.T)


def bring_in_kernel(n, *refs):
    copies = [
        pltpu.make_async_copy(refs[i], refs[n + i], refs[2 * n].at[i]) for i in range(n)
    ]
    for copy in copies:
        copy.start()
    for copy in copies:
        copy.wait()


def bring_in(arrays):
    n = len(arrays)
    return pl.pallas_call(
        functools.partial(bring_in_kernel, n),
        in_specs=[pl.BlockSpec(memory_space=pl.ANY)] * n,
        out_specs=[pl.BlockSpec(memory_space=pltpu.VMEM)] * n,
        out_shape=[jax.ShapeDtypeStruct(array.shape, array.dtype) for array in arrays],
        scratch_shapes=[pltpu.SemaphoreType.DMA((n,))],
        compiler_params=pltpu.CompilerParams(vmem_limit_bytes=2 * MIB),
        cost_estimate=small_cost(),
    )(*arrays)


def body(tokens, expert_ids, gate_codes, w_gate, w_up, w_down):
    nodes = lax.axis_size("node")
    ring = nodes // SPAN
    far = ring // 2
    tok, top = expert_ids.shape
    half = tok // 2

    def chip_at(pos):
        return 2 * pos if pos < far else 2 * (ring - 1 - pos) + 1

    def perm(step):
        return [
            (chip_at(pos) * SPAN + core, chip_at((pos + step) % ring) * SPAN + core)
            for pos in range(ring)
            for core in range(SPAN)
        ]

    forward, backward = perm(1), perm(-1)
    swap = [(node, node ^ 1) for node in range(nodes)]
    chip = lax.div(lax.axis_index("node"), jnp.int32(SPAN)).reshape(1)
    weights = (w_gate, w_up, w_down)
    tokens, weights, chip = lax.optimization_barrier((tokens, weights, chip))

    near = [lax.ppermute(tokens, "node", forward), lax.ppermute(tokens, "node", backward)]
    rails = [[SPAN * c + core for c in range(ring)] for core in range(SPAN)]
    table = lax.all_to_all(
        gate_table(ring, expert_ids, gate_codes),
        "node",
        split_axis=0,
        concat_axis=0,
        axis_index_groups=rails,
        tiled=True,
    )
    weights, table = lax.optimization_barrier((weights, table))
    other = [lax.ppermute(weight, "node", swap) for weight in weights]
    own = bring_in(weights)

    near, own = lax.optimization_barrier((near, own))
    halves = split(near)
    ahead = [[None, halves[0]], [None, halves[1]]]
    behind = [[None, halves[3]], [None, halves[2]]]
    parts = {}

    def work(names, blocks, after=()):
        held = [parts[name] for name in after]
        blocks, held = lax.optimization_barrier((blocks, held))
        parts.update(zip(after, held))
        marks = names[::2] if len(blocks) < len(names) else names
        marks = [(offset, h * half) for offset, h in marks]
        shares = expert_parts(marks, ring, half, chip, table, blocks, own, other)
        parts.update(zip(names, shares))
        return names

    def send(s, wave, after):
        held = [parts[name] for name in after]
        pair, held = lax.optimization_barrier(((ahead[wave][-1], behind[wave][-1]), held))
        parts.update(zip(after, held))
        ahead[wave][-1], behind[wave][-1] = pair
        ahead[wave].append(lax.ppermute(pair[0], "node", forward))
        behind[wave].append(lax.ppermute(pair[1], "node", backward))

    for wave in range(2):
        send(2, wave, [])
    names = [(offset, h) for offset in (0, -1, 1) for h in range(2)]
    done = [work(names, [tokens, *near])]
    for s in range(3, far + 1):
        for wave in range(2):
            if s < far or wave == 0:
                send(s, wave, done.pop(0))
            names = [(1 - s, wave), (s - 1, 1 - wave)]
            after = done[-1] if s == far and wave == 1 else []
            done.append(work(names, [ahead[wave][s - 1], behind[wave][s - 1]], after))
    work([(far, 0), (far, 1)], [ahead[0][far], behind[0][far]], done[-1])
    parts[-far, 1] = parts[far, 1]

    firsts = [(1 - far, 0), (far - 1, 1)]
    held, after = lax.optimization_barrier(
        ([parts[name] for name in firsts], [parts[name] for name in done[-1]])
    )
    parts.update(zip(firsts, held))
    parts.update(zip(done[-1], after))

    early = [(h, sign) for h in range(2) for sign in (1, -1) if (h == 0) != (sign == 1)]
    late = [(h, -sign) for h, sign in early]
    ways = {1: forward, -1: backward}

    def pass_on(group, totals):
        return [lax.ppermute(t, "node", ways[sign]) for t, (h, sign) in zip(totals, group)]

    def shares(group, offset):
        return [parts[sign * offset, h] for h, sign in group]

    first = pass_on(early, shares(early, far - 1))
    last = [pass_on(late, shares(late, far))]
    for k in range(2, far + 1):
        if k < far:
            first = pass_on(early, add(shares(early, far - k), first))
            after = []
        else:
            first = add(shares(early, 0), first, dtype=jnp.float32)
            after = first
        terms = shares(late, far - k + 1)
        if k == far - 1:
            totals = add(terms, last[0], after, pieces=2)
            last = [pass_on(late, totals[p::2]) for p in range(2)]
        else:
            size = half // len(last)
            last = [
                pass_on(late, add(terms, came, after, first=p * size))
                for p, came in enumerate(last)
            ]
    return close(first, last)


def solution(mesh):
    in_specs = (
        P(("groups", "node"), None),
        P(("groups", "node"), None),
        P(("groups", "node"), None),
        P(None, "node"),
        P(None, "node"),
        P("node", None),
    )
    out_specs = P(("groups", "node"), None)
    return jax.shard_map(body, mesh=mesh, in_specs=in_specs, out_specs=out_specs, check_vma=False)
```

```python
import functools

import jax
import jax.numpy as jnp
from jax import lax
from jax.experimental import pallas as pl
from jax.experimental.pallas import tpu as pltpu
from jax.sharding import PartitionSpec as P

SPAN = 2
LANES = 128
TILE = 256
WIDE = 512
MIB = 1 << 20
FORWARD = 40 * 10**9


def expert_kernel(marks, ring, dim, half, chip_ref, table_ref, *refs):
    n = len(marks)
    blocks, weights, outs = refs[:n], refs[n : n + 6], refs[n + 6 : -3]
    rows_ref, scale_ref, hidden_ref = refs[-3:]
    hid = weights[0].shape[1]
    table = table_ref[...]
    filler = jnp.zeros((LANES - table.shape[0], table.shape[1]), table.dtype)
    table = jnp.transpose(jnp.concatenate([table, filler], 0))
    lane = lax.broadcasted_iota(jnp.int32, table.shape, 1)
    chip = chip_ref[0]
    pos = jnp.where(lax.rem(chip, 2) == 0, lax.div(chip, 2), ring - 1 - lax.div(chip, 2))
    first = 0
    for (offset, start), block in zip(marks, blocks):
        count = block.shape[0]
        origin = lax.rem(pos + (offset + ring), ring)
        origin = jnp.where(origin < ring // 2, 2 * origin, 2 * (ring - 1 - origin) + 1)
        scale = jnp.sum(jnp.where(lane == origin, table, 0.0), 1, keepdims=True)
        at = pl.ds(first, count)
        first += count
        rows_ref[at, :] = block[...]
        scale_ref[at, :] = jnp.broadcast_to(scale[start : start + count], (count, LANES))

    for side in range(SPAN):
        gate_ref, up_ref, _ = weights[3 * side : 3 * side + 3]

        def hidden_tile(j, carry, side=side, gate_ref=gate_ref, up_ref=up_ref):
            at = pl.ds(pl.multiple_of(j * TILE, TILE), TILE)
            rows = rows_ref[...]
            gate = jnp.dot(rows, gate_ref[:, at], preferred_element_type=jnp.float32)
            upward = jnp.dot(rows, up_ref[:, at], preferred_element_type=jnp.float32)
            hidden = gate / (1.0 + jnp.exp(-gate)) * upward * scale_ref[:, :1]
            to = pl.ds(pl.multiple_of(side * hid + j * TILE, TILE), TILE)
            hidden_ref[:, to] = hidden.astype(jnp.bfloat16)
            return carry

        lax.fori_loop(0, hid // TILE, hidden_tile, 0)

    def out_tile(j, carry):
        at = pl.ds(pl.multiple_of(j * WIDE, WIDE), WIDE)
        part = jnp.dot(
            hidden_ref[:, :hid], weights[2][:, at], preferred_element_type=jnp.float32
        ) + jnp.dot(hidden_ref[:, hid:], weights[5][:, at], preferred_element_type=jnp.float32)
        part = part.astype(jnp.bfloat16)
        for i, out in enumerate(outs):
            out[:, at] = part[i * half : (i + 1) * half, :]
        return carry

    lax.fori_loop(0, dim // WIDE, out_tile, 0)


def small_cost():
    return pl.CostEstimate(flops=1024, bytes_accessed=1024, transcendentals=0)


def expert_parts(marks, ring, half, chip, table, blocks, own, other):
    dim, hid = own[0].shape
    n, rows = len(blocks), sum(block.shape[0] for block in blocks)
    specs = [pl.BlockSpec(memory_space=pltpu.SMEM)]
    specs += [pl.BlockSpec(memory_space=pltpu.VMEM)] * (n + 7)
    return pl.pallas_call(
        functools.partial(expert_kernel, marks, ring, dim, half),
        in_specs=specs,
        out_specs=[pl.BlockSpec(memory_space=pltpu.VMEM)] * (rows // half),
        out_shape=[jax.ShapeDtypeStruct((half, dim), jnp.bfloat16)] * (rows // half),
        scratch_shapes=[
            pltpu.VMEM((rows, dim), jnp.bfloat16),
            pltpu.VMEM((rows, LANES), jnp.float32),
            pltpu.VMEM((rows, SPAN * hid), jnp.bfloat16),
        ],
        compiler_params=pltpu.CompilerParams(vmem_limit_bytes=8 * MIB),
        cost_estimate=small_cost(),
    )(chip, table, *blocks, *own, *other)


def add_kernel(n, pieces, first, *refs):
    outs = refs[-n * pieces :]
    size = outs[0].shape[0]
    for i, (left_ref, right_ref) in enumerate(zip(refs[:n], refs[n : 2 * n])):
        for p in range(pieces):
            left = left_ref[first + p * size : first + (p + 1) * size, :]
            right = right_ref[p * size : (p + 1) * size, :]
            out = outs[i * pieces + p]
            out[...] = left.astype(out.dtype) + right.astype(out.dtype)


def add(lefts, rights, after=(), pieces=1, first=0, dtype=None):
    n = len(lefts)
    rows, dim = rights[0].shape
    shape = jax.ShapeDtypeStruct((rows // pieces, dim), dtype or rights[0].dtype)
    return pl.pallas_call(
        functools.partial(add_kernel, n, pieces, first),
        in_specs=[pl.BlockSpec(memory_space=pltpu.VMEM)] * (2 * n)
        + [pl.BlockSpec(memory_space=pl.ANY)] * len(after),
        out_specs=[pl.BlockSpec(memory_space=pltpu.VMEM)] * (n * pieces),
        out_shape=[shape] * (n * pieces),
        compiler_params=pltpu.CompilerParams(vmem_limit_bytes=6 * MIB),
        cost_estimate=small_cost(),
    )(*lefts, *rights, *after)


def split_kernel(n, *refs):
    for i, ref in enumerate(refs[:n]):
        half = ref.shape[0] // 2
        for h in range(2):
            refs[n + 2 * i + h][...] = ref[h * half : (h + 1) * half, :]


def split(arrays):
    n = len(arrays)
    rows, dim = arrays[0].shape
    return pl.pallas_call(
        functools.partial(split_kernel, n),
        in_specs=[pl.BlockSpec(memory_space=pltpu.VMEM)] * n,
        out_specs=[pl.BlockSpec(memory_space=pltpu.VMEM)] * (2 * n),
        out_shape=[jax.ShapeDtypeStruct((rows // 2, dim), arrays[0].dtype)] * (2 * n),
        compiler_params=pltpu.CompilerParams(vmem_limit_bytes=6 * MIB),
        cost_estimate=pl.CostEstimate(flops=FORWARD, bytes_accessed=1024, transcendentals=0),
    )(*arrays)


def close_kernel(*refs):
    out_ref, bases, pieces = refs[-1], refs[:2], refs[2:-1]
    size = pieces[0].shape[0]
    for h, base_ref in enumerate(bases):
        half = base_ref.shape[0]
        for p in range(len(pieces) // 2):
            at = slice(p * size, (p + 1) * size)
            total = base_ref[at, :] + pieces[2 * p + h][...].astype(jnp.float32)
            out_ref[h * half + p * size : h * half + (p + 1) * size, :] = total.astype(out_ref.dtype)


def close(bases, pieces):
    terms = [term for piece in pieces for term in piece]
    half, dim = bases[0].shape
    return pl.pallas_call(
        close_kernel,
        in_specs=[pl.BlockSpec(memory_space=pltpu.VMEM)] * (len(terms) + 2),
        out_shape=jax.ShapeDtypeStruct((2 * half, dim), terms[0].dtype),
        compiler_params=pltpu.CompilerParams(vmem_limit_bytes=8 * MIB),
        cost_estimate=small_cost(),
    )(*bases, *terms)


def table_kernel(ids_ref, codes_ref, out_ref):
    expert = lax.broadcasted_iota(jnp.int32, out_ref.shape, 0)
    code = jnp.zeros(out_ref.shape, jnp.int32)
    for k in range(ids_ref.shape[0]):
        code = code + jnp.where(ids_ref[k : k + 1, :] == expert, codes_ref[k : k + 1, :], 0)
    out_ref[...] = code.astype(jnp.float32) * (1.0 / 4096.0)


def gate_table(experts, ids, codes):
    return pl.pallas_call(
        table_kernel,
        in_specs=[pl.BlockSpec(memory_space=pltpu.VMEM)] * 2,
        out_shape=jax.ShapeDtypeStruct((experts, ids.shape[0]), jnp.float32),
        compiler_params=pltpu.CompilerParams(vmem_limit_bytes=2 * MIB),
        cost_estimate=small_cost(),
    )(ids.T, codes.T)


def bring_in_kernel(n, *refs):
    copies = [
        pltpu.make_async_copy(refs[i], refs[n + i], refs[2 * n].at[i]) for i in range(n)
    ]
    for copy in copies:
        copy.start()
    for copy in copies:
        copy.wait()


def bring_in(arrays):
    n = len(arrays)
    return pl.pallas_call(
        functools.partial(bring_in_kernel, n),
        in_specs=[pl.BlockSpec(memory_space=pl.ANY)] * n,
        out_specs=[pl.BlockSpec(memory_space=pltpu.VMEM)] * n,
        out_shape=[jax.ShapeDtypeStruct(array.shape, array.dtype) for array in arrays],
        scratch_shapes=[pltpu.SemaphoreType.DMA((n,))],
        compiler_params=pltpu.CompilerParams(vmem_limit_bytes=2 * MIB),
        cost_estimate=small_cost(),
    )(*arrays)


def body(tokens, expert_ids, gate_codes, w_gate, w_up, w_down):
    nodes = lax.axis_size("node")
    ring = nodes // SPAN
    far = ring // 2
    tok, top = expert_ids.shape
    half = tok // 2

    def chip_at(pos):
        return 2 * pos if pos < far else 2 * (ring - 1 - pos) + 1

    def perm(step):
        return [
            (chip_at(pos) * SPAN + core, chip_at((pos + step) % ring) * SPAN + core)
            for pos in range(ring)
            for core in range(SPAN)
        ]

    forward, backward = perm(1), perm(-1)
    swap = [(node, node ^ 1) for node in range(nodes)]
    chip = lax.div(lax.axis_index("node"), jnp.int32(SPAN)).reshape(1)
    weights = (w_gate, w_up, w_down)
    tokens, weights, chip = lax.optimization_barrier((tokens, weights, chip))

    near = [lax.ppermute(tokens, "node", forward), lax.ppermute(tokens, "node", backward)]
    other = [lax.ppermute(weight, "node", swap) for weight in weights]
    rails = [[SPAN * c + core for c in range(ring)] for core in range(SPAN)]
    table = lax.all_to_all(
        gate_table(ring, expert_ids, gate_codes),
        "node",
        split_axis=0,
        concat_axis=0,
        axis_index_groups=rails,
        tiled=True,
    )
    near, weights, other, table = lax.optimization_barrier((near, weights, other, table))
    own = bring_in(weights)

    halves = split(near)
    ahead = [[None, halves[0]], [None, halves[1]]]
    behind = [[None, halves[3]], [None, halves[2]]]
    parts = {}

    def work(names, blocks, after=()):
        held = [parts[name] for name in after]
        blocks, held = lax.optimization_barrier((blocks, held))
        parts.update(zip(after, held))
        marks = names[::2] if len(blocks) < len(names) else names
        marks = [(offset, h * half) for offset, h in marks]
        shares = expert_parts(marks, ring, half, chip, table, blocks, own, other)
        parts.update(zip(names, shares))
        return names

    def send(s, wave, after):
        held = [parts[name] for name in after]
        pair, held = lax.optimization_barrier(((ahead[wave][-1], behind[wave][-1]), held))
        parts.update(zip(after, held))
        ahead[wave][-1], behind[wave][-1] = pair
        ahead[wave].append(lax.ppermute(pair[0], "node", forward))
        behind[wave].append(lax.ppermute(pair[1], "node", backward))

    for wave in range(2):
        send(2, wave, [])
    names = [(offset, h) for offset in (0, -1, 1) for h in range(2)]
    done = [[], work(names, [tokens, *near])]
    for s in range(3, far + 1):
        for wave in range(2):
            if s < far or wave == 0:
                send(s, wave, done.pop(0))
            names = [(1 - s, wave), (s - 1, 1 - wave)]
            blocks = [ahead[wave][s - 1], behind[wave][s - 1]]
            done.append(work(names, blocks, done[-1]))
    work([(far, 0), (far, 1)], [ahead[0][far], behind[0][far]], done[-1])
    parts[-far, 1] = parts[far, 1]

    firsts = [(1 - far, 0), (far - 1, 1)]
    held, after = lax.optimization_barrier(
        ([parts[name] for name in firsts], [parts[name] for name in done[-1]])
    )
    parts.update(zip(firsts, held))
    parts.update(zip(done[-1], after))

    early = [(h, sign) for h in range(2) for sign in (1, -1) if (h == 0) != (sign == 1)]
    late = [(h, -sign) for h, sign in early]
    ways = {1: forward, -1: backward}

    def pass_on(group, totals):
        return [lax.ppermute(t, "node", ways[sign]) for t, (h, sign) in zip(totals, group)]

    def shares(group, offset):
        return [parts[sign * offset, h] for h, sign in group]

    first = pass_on(early, shares(early, far - 1))
    last = [pass_on(late, shares(late, far))]
    for k in range(2, far + 1):
        if k < far:
            first = pass_on(early, add(shares(early, far - k), first))
            after = []
        else:
            first = add(shares(early, 0), first, dtype=jnp.float32)
            after = first
        terms = shares(late, far - k + 1)
        if k == far - 1:
            totals = add(terms, last[0], after, pieces=2)
            last = [pass_on(late, totals[p::2]) for p in range(2)]
        else:
            size = half // len(last)
            last = [
                pass_on(late, add(terms, came, after, first=p * size))
                for p, came in enumerate(last)
            ]
    return close(first, last)


def solution(mesh):
    in_specs = (
        P(("groups", "node"), None),
        P(("groups", "node"), None),
        P(("groups", "node"), None),
        P(None, "node"),
        P(None, "node"),
        P("node", None),
    )
    out_specs = P(("groups", "node"), None)
    return jax.shard_map(body, mesh=mesh, in_specs=in_specs, out_specs=out_specs, check_vma=False)
```

```python
import functools

import jax
import jax.numpy as jnp
from jax import lax
from jax.experimental import pallas as pl
from jax.experimental.pallas import tpu as pltpu
from jax.sharding import PartitionSpec as P

SPAN = 2
LANES = 128
TILE = 256
WIDE = 512
MIB = 1 << 20
FORWARD = 40 * 10**9


def expert_kernel(marks, ring, dim, half, chip_ref, table_ref, *refs):
    n = len(marks)
    blocks, weights, outs = refs[:n], refs[n : n + 6], refs[n + 6 : -3]
    rows_ref, scale_ref, hidden_ref = refs[-3:]
    hid = weights[0].shape[1]
    table = table_ref[...]
    filler = jnp.zeros((LANES - table.shape[0], table.shape[1]), table.dtype)
    table = jnp.transpose(jnp.concatenate([table, filler], 0))
    lane = lax.broadcasted_iota(jnp.int32, table.shape, 1)
    chip = chip_ref[0]
    pos = jnp.where(lax.rem(chip, 2) == 0, lax.div(chip, 2), ring - 1 - lax.div(chip, 2))
    first = 0
    for (offset, start), block in zip(marks, blocks):
        count = block.shape[0]
        origin = lax.rem(pos + (offset + ring), ring)
        origin = jnp.where(origin < ring // 2, 2 * origin, 2 * (ring - 1 - origin) + 1)
        scale = jnp.sum(jnp.where(lane == origin, table, 0.0), 1, keepdims=True)
        at = pl.ds(first, count)
        first += count
        rows_ref[at, :] = block[...]
        scale_ref[at, :] = jnp.broadcast_to(scale[start : start + count], (count, LANES))

    for side in range(SPAN):
        gate_ref, up_ref, _ = weights[3 * side : 3 * side + 3]

        def hidden_tile(j, carry, side=side, gate_ref=gate_ref, up_ref=up_ref):
            at = pl.ds(pl.multiple_of(j * TILE, TILE), TILE)
            rows = rows_ref[...]
            gate = jnp.dot(rows, gate_ref[:, at], preferred_element_type=jnp.float32)
            upward = jnp.dot(rows, up_ref[:, at], preferred_element_type=jnp.float32)
            hidden = gate / (1.0 + jnp.exp(-gate)) * upward * scale_ref[:, :1]
            to = pl.ds(pl.multiple_of(side * hid + j * TILE, TILE), TILE)
            hidden_ref[:, to] = hidden.astype(jnp.bfloat16)
            return carry

        lax.fori_loop(0, hid // TILE, hidden_tile, 0)

    def out_tile(j, carry):
        at = pl.ds(pl.multiple_of(j * WIDE, WIDE), WIDE)
        part = jnp.dot(
            hidden_ref[:, :hid], weights[2][:, at], preferred_element_type=jnp.float32
        ) + jnp.dot(hidden_ref[:, hid:], weights[5][:, at], preferred_element_type=jnp.float32)
        part = part.astype(jnp.bfloat16)
        for i, out in enumerate(outs):
            out[:, at] = part[i * half : (i + 1) * half, :]
        return carry

    lax.fori_loop(0, dim // WIDE, out_tile, 0)


def small_cost():
    return pl.CostEstimate(flops=1024, bytes_accessed=1024, transcendentals=0)


def expert_parts(marks, ring, half, chip, table, blocks, own, other):
    dim, hid = own[0].shape
    n, rows = len(blocks), sum(block.shape[0] for block in blocks)
    specs = [pl.BlockSpec(memory_space=pltpu.SMEM)]
    specs += [pl.BlockSpec(memory_space=pltpu.VMEM)] * (n + 7)
    return pl.pallas_call(
        functools.partial(expert_kernel, marks, ring, dim, half),
        in_specs=specs,
        out_specs=[pl.BlockSpec(memory_space=pltpu.VMEM)] * (rows // half),
        out_shape=[jax.ShapeDtypeStruct((half, dim), jnp.bfloat16)] * (rows // half),
        scratch_shapes=[
            pltpu.VMEM((rows, dim), jnp.bfloat16),
            pltpu.VMEM((rows, LANES), jnp.float32),
            pltpu.VMEM((rows, SPAN * hid), jnp.bfloat16),
        ],
        compiler_params=pltpu.CompilerParams(vmem_limit_bytes=8 * MIB),
        cost_estimate=small_cost(),
    )(chip, table, *blocks, *own, *other)


def add_kernel(n, pieces, first, *refs):
    outs = refs[-n * pieces :]
    size = outs[0].shape[0]
    for i, (left_ref, right_ref) in enumerate(zip(refs[:n], refs[n : 2 * n])):
        for p in range(pieces):
            left = left_ref[first + p * size : first + (p + 1) * size, :]
            right = right_ref[p * size : (p + 1) * size, :]
            out = outs[i * pieces + p]
            out[...] = left.astype(out.dtype) + right.astype(out.dtype)


def add(lefts, rights, after=(), pieces=1, first=0, dtype=None):
    n = len(lefts)
    rows, dim = rights[0].shape
    shape = jax.ShapeDtypeStruct((rows // pieces, dim), dtype or rights[0].dtype)
    return pl.pallas_call(
        functools.partial(add_kernel, n, pieces, first),
        in_specs=[pl.BlockSpec(memory_space=pltpu.VMEM)] * (2 * n)
        + [pl.BlockSpec(memory_space=pl.ANY)] * len(after),
        out_specs=[pl.BlockSpec(memory_space=pltpu.VMEM)] * (n * pieces),
        out_shape=[shape] * (n * pieces),
        compiler_params=pltpu.CompilerParams(vmem_limit_bytes=6 * MIB),
        cost_estimate=small_cost(),
    )(*lefts, *rights, *after)


def split_kernel(n, *refs):
    for i, ref in enumerate(refs[:n]):
        half = ref.shape[0] // 2
        for h in range(2):
            refs[n + 2 * i + h][...] = ref[h * half : (h + 1) * half, :]


def split(arrays):
    n = len(arrays)
    rows, dim = arrays[0].shape
    return pl.pallas_call(
        functools.partial(split_kernel, n),
        in_specs=[pl.BlockSpec(memory_space=pltpu.VMEM)] * n,
        out_specs=[pl.BlockSpec(memory_space=pltpu.VMEM)] * (2 * n),
        out_shape=[jax.ShapeDtypeStruct((rows // 2, dim), arrays[0].dtype)] * (2 * n),
        compiler_params=pltpu.CompilerParams(vmem_limit_bytes=6 * MIB),
        cost_estimate=pl.CostEstimate(flops=FORWARD, bytes_accessed=1024, transcendentals=0),
    )(*arrays)


def close_kernel(*refs):
    out_ref, bases, pieces = refs[-1], refs[:2], refs[2:-1]
    size = pieces[0].shape[0]
    for h, base_ref in enumerate(bases):
        half = base_ref.shape[0]
        for p in range(len(pieces) // 2):
            at = slice(p * size, (p + 1) * size)
            total = base_ref[at, :] + pieces[2 * p + h][...].astype(jnp.float32)
            out_ref[h * half + p * size : h * half + (p + 1) * size, :] = total.astype(out_ref.dtype)


def close(bases, pieces):
    terms = [term for piece in pieces for term in piece]
    half, dim = bases[0].shape
    return pl.pallas_call(
        close_kernel,
        in_specs=[pl.BlockSpec(memory_space=pltpu.VMEM)] * (len(terms) + 2),
        out_shape=jax.ShapeDtypeStruct((2 * half, dim), terms[0].dtype),
        compiler_params=pltpu.CompilerParams(vmem_limit_bytes=8 * MIB),
        cost_estimate=small_cost(),
    )(*bases, *terms)


def table_kernel(ids_ref, codes_ref, out_ref):
    expert = lax.broadcasted_iota(jnp.int32, out_ref.shape, 0)
    code = jnp.zeros(out_ref.shape, jnp.int32)
    for k in range(ids_ref.shape[0]):
        code = code + jnp.where(ids_ref[k : k + 1, :] == expert, codes_ref[k : k + 1, :], 0)
    out_ref[...] = code.astype(jnp.float32) * (1.0 / 4096.0)


def gate_table(experts, ids, codes):
    return pl.pallas_call(
        table_kernel,
        in_specs=[pl.BlockSpec(memory_space=pltpu.VMEM)] * 2,
        out_shape=jax.ShapeDtypeStruct((experts, ids.shape[0]), jnp.float32),
        compiler_params=pltpu.CompilerParams(vmem_limit_bytes=2 * MIB),
        cost_estimate=small_cost(),
    )(ids.T, codes.T)


def bring_in_kernel(n, *refs):
    copies = [
        pltpu.make_async_copy(refs[i], refs[n + i], refs[2 * n].at[i]) for i in range(n)
    ]
    for copy in copies:
        copy.start()
    for copy in copies:
        copy.wait()


def bring_in(arrays):
    n = len(arrays)
    return pl.pallas_call(
        functools.partial(bring_in_kernel, n),
        in_specs=[pl.BlockSpec(memory_space=pl.ANY)] * n,
        out_specs=[pl.BlockSpec(memory_space=pltpu.VMEM)] * n,
        out_shape=[jax.ShapeDtypeStruct(array.shape, array.dtype) for array in arrays],
        scratch_shapes=[pltpu.SemaphoreType.DMA((n,))],
        compiler_params=pltpu.CompilerParams(vmem_limit_bytes=2 * MIB),
        cost_estimate=small_cost(),
    )(*arrays)


def body(tokens, expert_ids, gate_codes, w_gate, w_up, w_down):
    nodes = lax.axis_size("node")
    ring = nodes // SPAN
    far = ring // 2
    tok, top = expert_ids.shape
    half = tok // 2

    def chip_at(pos):
        return 2 * pos if pos < far else 2 * (ring - 1 - pos) + 1

    def perm(step):
        return [
            (chip_at(pos) * SPAN + core, chip_at((pos + step) % ring) * SPAN + core)
            for pos in range(ring)
            for core in range(SPAN)
        ]

    forward, backward = perm(1), perm(-1)
    swap = [(node, node ^ 1) for node in range(nodes)]
    chip = lax.div(lax.axis_index("node"), jnp.int32(SPAN)).reshape(1)
    weights = (w_gate, w_up, w_down)
    tokens, weights, chip = lax.optimization_barrier((tokens, weights, chip))

    near = [lax.ppermute(tokens, "node", forward), lax.ppermute(tokens, "node", backward)]
    other = [lax.ppermute(weight, "node", swap) for weight in weights]
    rails = [[SPAN * c + core for c in range(ring)] for core in range(SPAN)]
    table = lax.all_to_all(
        gate_table(ring, expert_ids, gate_codes),
        "node",
        split_axis=0,
        concat_axis=0,
        axis_index_groups=rails,
        tiled=True,
    )
    near, weights, other, table = lax.optimization_barrier((near, weights, other, table))
    own = bring_in(weights)

    halves = split(near)
    ahead = [[None, halves[0]], [None, halves[1]]]
    behind = [[None, halves[3]], [None, halves[2]]]
    parts = {}

    def work(names, blocks, after=()):
        held = [parts[name] for name in after]
        blocks, held = lax.optimization_barrier((blocks, held))
        parts.update(zip(after, held))
        marks = names[::2] if len(blocks) < len(names) else names
        marks = [(offset, h * half) for offset, h in marks]
        shares = expert_parts(marks, ring, half, chip, table, blocks, own, other)
        parts.update(zip(names, shares))
        return names

    def send(s, wave, after):
        held = [parts[name] for name in after]
        pair, held = lax.optimization_barrier(((ahead[wave][-1], behind[wave][-1]), held))
        parts.update(zip(after, held))
        ahead[wave][-1], behind[wave][-1] = pair
        ahead[wave].append(lax.ppermute(pair[0], "node", forward))
        behind[wave].append(lax.ppermute(pair[1], "node", backward))

    for wave in range(2):
        send(2, wave, [])
    names = [(offset, h) for offset in (0, -1, 1) for h in range(2)]
    done = [work(names, [tokens, *near])]
    for s in range(3, far + 1):
        for wave in range(2):
            if s < far or wave == 0:
                send(s, wave, done.pop(0))
            names = [(1 - s, wave), (s - 1, 1 - wave)]
            blocks = [ahead[wave][s - 1], behind[wave][s - 1]]
            done.append(work(names, blocks, done[-1] if done else []))
    work([(far, 0), (far, 1)], [ahead[0][far], behind[0][far]], done[-1])
    parts[-far, 1] = parts[far, 1]

    firsts = [(1 - far, 0), (far - 1, 1)]
    held, after = lax.optimization_barrier(
        ([parts[name] for name in firsts], [parts[name] for name in done[-1]])
    )
    parts.update(zip(firsts, held))
    parts.update(zip(done[-1], after))

    early = [(h, sign) for h in range(2) for sign in (1, -1) if (h == 0) != (sign == 1)]
    late = [(h, -sign) for h, sign in early]
    ways = {1: forward, -1: backward}

    def pass_on(group, totals):
        return [lax.ppermute(t, "node", ways[sign]) for t, (h, sign) in zip(totals, group)]

    def shares(group, offset):
        return [parts[sign * offset, h] for h, sign in group]

    first = pass_on(early, shares(early, far - 1))
    last = [pass_on(late, shares(late, far))]
    for k in range(2, far + 1):
        if k < far:
            first = pass_on(early, add(shares(early, far - k), first))
            after = []
        else:
            first = add(shares(early, 0), first, dtype=jnp.float32)
            after = first
        terms = shares(late, far - k + 1)
        if k == far - 1:
            totals = add(terms, last[0], after, pieces=2)
            last = [pass_on(late, totals[p::2]) for p in range(2)]
        else:
            size = half // len(last)
            last = [
                pass_on(late, add(terms, came, after, first=p * size))
                for p, came in enumerate(last)
            ]
    return close(first, last)


def solution(mesh):
    in_specs = (
        P(("groups", "node"), None),
        P(("groups", "node"), None),
        P(("groups", "node"), None),
        P(None, "node"),
        P(None, "node"),
        P("node", None),
    )
    out_specs = P(("groups", "node"), None)
    return jax.shard_map(body, mesh=mesh, in_specs=in_specs, out_specs=out_specs, check_vma=False)
```

```python
import functools

import jax
import jax.numpy as jnp
from jax import lax
from jax.experimental import pallas as pl
from jax.experimental.pallas import tpu as pltpu
from jax.sharding import PartitionSpec as P

SPAN = 2
LANES = 128
DIGIT = 64
TILE = 256
WIDE = 512
MIB = 1 << 20
AHEAD = 6 * MIB
FORWARD = 40 * 10**9


def expert_kernel(n, experts, dim, half, expert_ref, *refs):
    blocks, weights, outs = refs[:n], refs[n : n + 6], refs[n + 6 : -3]
    rows_ref, scale_ref, hidden_ref = refs[-3:]
    hid = weights[0].shape[1]
    expert = expert_ref[0]
    first = 0
    for block in blocks:
        count = block.shape[0]
        lane = lax.broadcasted_iota(jnp.int32, (count, LANES), 1)
        at = pl.ds(first, count)
        first += count
        rows_ref[at, :] = block[:, :dim]
        digits = block[:, dim:].astype(jnp.float32)
        codes = jnp.where(lane == expert, digits * float(DIGIT), 0.0)
        codes = codes + jnp.where(lane == expert + experts, digits, 0.0)
        code = jnp.sum(codes, 1, keepdims=True) * (1.0 / 4096.0)
        scale_ref[at, :] = jnp.broadcast_to(code, (count, LANES))

    for side in range(SPAN):
        gate_ref, up_ref, _ = weights[3 * side : 3 * side + 3]

        def hidden_tile(j, carry, side=side, gate_ref=gate_ref, up_ref=up_ref):
            at = pl.ds(pl.multiple_of(j * TILE, TILE), TILE)
            rows = rows_ref[...]
            gate = jnp.dot(rows, gate_ref[:, at], preferred_element_type=jnp.float32)
            upward = jnp.dot(rows, up_ref[:, at], preferred_element_type=jnp.float32)
            hidden = gate / (1.0 + jnp.exp(-gate)) * upward * scale_ref[:, :1]
            to = pl.ds(pl.multiple_of(side * hid + j * TILE, TILE), TILE)
            hidden_ref[:, to] = hidden.astype(jnp.bfloat16)
            return carry

        lax.fori_loop(0, hid // TILE, hidden_tile, 0)

    def out_tile(j, carry):
        at = pl.ds(pl.multiple_of(j * WIDE, WIDE), WIDE)
        part = jnp.dot(
            hidden_ref[:, :hid], weights[2][:, at], preferred_element_type=jnp.float32
        ) + jnp.dot(hidden_ref[:, hid:], weights[5][:, at], preferred_element_type=jnp.float32)
        part = part.astype(jnp.bfloat16)
        for i, out in enumerate(outs):
            out[:, at] = part[i * half : (i + 1) * half, :]
        return carry

    lax.fori_loop(0, dim // WIDE, out_tile, 0)


def small_cost():
    return pl.CostEstimate(flops=1024, bytes_accessed=1024, transcendentals=0)


def expert_parts(experts, half, expert, blocks, own, other, cost=1024):
    dim, hid = own[0].shape
    n, rows = len(blocks), sum(block.shape[0] for block in blocks)
    specs = [pl.BlockSpec(memory_space=pltpu.SMEM)]
    specs += [pl.BlockSpec(memory_space=pltpu.VMEM)] * (n + 6)
    return pl.pallas_call(
        functools.partial(expert_kernel, n, experts, dim, half),
        in_specs=specs,
        out_specs=[pl.BlockSpec(memory_space=pltpu.VMEM)] * (rows // half),
        out_shape=[jax.ShapeDtypeStruct((half, dim), jnp.bfloat16)] * (rows // half),
        scratch_shapes=[
            pltpu.VMEM((rows, dim), jnp.bfloat16),
            pltpu.VMEM((rows, LANES), jnp.float32),
            pltpu.VMEM((rows, SPAN * hid), jnp.bfloat16),
        ],
        compiler_params=pltpu.CompilerParams(vmem_limit_bytes=8 * MIB),
        cost_estimate=pl.CostEstimate(flops=1024, bytes_accessed=cost, transcendentals=0),
    )(expert, *blocks, *own, *other)


def add_kernel(n, pieces, first, *refs):
    outs = refs[-n * pieces :]
    size = outs[0].shape[0]
    for i, (left_ref, right_ref) in enumerate(zip(refs[:n], refs[n : 2 * n])):
        for p in range(pieces):
            left = left_ref[first + p * size : first + (p + 1) * size, :]
            right = right_ref[p * size : (p + 1) * size, :]
            out = outs[i * pieces + p]
            out[...] = left.astype(out.dtype) + right.astype(out.dtype)


def add(lefts, rights, after=(), pieces=1, first=0, dtype=None, cost=1024):
    n = len(lefts)
    rows, dim = rights[0].shape
    shape = jax.ShapeDtypeStruct((rows // pieces, dim), dtype or rights[0].dtype)
    return pl.pallas_call(
        functools.partial(add_kernel, n, pieces, first),
        in_specs=[pl.BlockSpec(memory_space=pltpu.VMEM)] * (2 * n)
        + [pl.BlockSpec(memory_space=pl.ANY)] * len(after),
        out_specs=[pl.BlockSpec(memory_space=pltpu.VMEM)] * (n * pieces),
        out_shape=[shape] * (n * pieces),
        compiler_params=pltpu.CompilerParams(vmem_limit_bytes=6 * MIB),
        cost_estimate=pl.CostEstimate(flops=1024, bytes_accessed=cost, transcendentals=0),
    )(*lefts, *rights, *after)


def split_kernel(n, *refs):
    for i, ref in enumerate(refs[:n]):
        half = ref.shape[0] // 2
        for h in range(2):
            refs[n + 2 * i + h][...] = ref[h * half : (h + 1) * half, :]


def split(arrays):
    n = len(arrays)
    rows, dim = arrays[0].shape
    return pl.pallas_call(
        functools.partial(split_kernel, n),
        in_specs=[pl.BlockSpec(memory_space=pltpu.VMEM)] * n,
        out_specs=[pl.BlockSpec(memory_space=pltpu.VMEM)] * (2 * n),
        out_shape=[jax.ShapeDtypeStruct((rows // 2, dim), arrays[0].dtype)] * (2 * n),
        compiler_params=pltpu.CompilerParams(vmem_limit_bytes=6 * MIB),
        cost_estimate=pl.CostEstimate(flops=FORWARD, bytes_accessed=1024, transcendentals=0),
    )(*arrays)


def merge_kernel(n, *refs):
    for i, out in enumerate(refs[n + n // 2 :]):
        rows_ref, digits_ref = refs[i], refs[n + i // 2]
        half, dim = rows_ref.shape
        start = i % 2 * half
        out[:, :dim] = rows_ref[...]
        out[:, dim:] = digits_ref[start : start + half, :]


def merged(halves, digits):
    n = len(halves)
    rows, dim = halves[0].shape
    return pl.pallas_call(
        functools.partial(merge_kernel, n),
        in_specs=[pl.BlockSpec(memory_space=pltpu.VMEM)] * (n + n // 2),
        out_specs=[pl.BlockSpec(memory_space=pltpu.VMEM)] * n,
        out_shape=[jax.ShapeDtypeStruct((rows, dim + LANES), halves[0].dtype)] * n,
        compiler_params=pltpu.CompilerParams(vmem_limit_bytes=6 * MIB),
        cost_estimate=small_cost(),
    )(*halves, *digits)


def close_kernel(*refs):
    out_ref, bases, pieces = refs[-1], refs[:2], refs[2:-1]
    size = pieces[0].shape[0]
    for h, base_ref in enumerate(bases):
        half = base_ref.shape[0]
        for p in range(len(pieces) // 2):
            at = slice(p * size, (p + 1) * size)
            total = base_ref[at, :] + pieces[2 * p + h][...].astype(jnp.float32)
            out_ref[h * half + p * size : h * half + (p + 1) * size, :] = total.astype(out_ref.dtype)


def close(bases, pieces):
    terms = [term for piece in pieces for term in piece]
    half, dim = bases[0].shape
    return pl.pallas_call(
        close_kernel,
        in_specs=[pl.BlockSpec(memory_space=pltpu.VMEM)] * (len(terms) + 2),
        out_shape=jax.ShapeDtypeStruct((2 * half, dim), terms[0].dtype),
        compiler_params=pltpu.CompilerParams(vmem_limit_bytes=8 * MIB),
        cost_estimate=small_cost(),
    )(*bases, *terms)


def digits_kernel(experts, ids_ref, codes_ref, out_ref):
    tok = out_ref.shape[0]
    row = lax.broadcasted_iota(jnp.int32, (LANES, tok), 0)
    expert = jnp.where(row < experts, row, row - experts)
    code = jnp.zeros((LANES, tok), jnp.int32)
    for k in range(ids_ref.shape[0]):
        code = code + jnp.where(ids_ref[k : k + 1, :] == expert, codes_ref[k : k + 1, :], 0)
    digits = jnp.where(row < experts, code // DIGIT, code % DIGIT)
    out_ref[...] = jnp.transpose(digits.astype(jnp.float32)).astype(out_ref.dtype)


def code_digits(experts, ids, codes):
    return pl.pallas_call(
        functools.partial(digits_kernel, experts),
        in_specs=[pl.BlockSpec(memory_space=pltpu.VMEM)] * 2,
        out_shape=jax.ShapeDtypeStruct((ids.shape[0], LANES), jnp.bfloat16),
        compiler_params=pltpu.CompilerParams(vmem_limit_bytes=2 * MIB),
        cost_estimate=small_cost(),
    )(ids.T, codes.T)


def bring_in_kernel(n, *refs):
    copies = [
        pltpu.make_async_copy(refs[i], refs[n + i], refs[2 * n].at[i]) for i in range(n)
    ]
    for copy in copies:
        copy.start()
    for copy in copies:
        copy.wait()


def bring_in(arrays):
    n = len(arrays)
    return pl.pallas_call(
        functools.partial(bring_in_kernel, n),
        in_specs=[pl.BlockSpec(memory_space=pl.ANY)] * n,
        out_specs=[pl.BlockSpec(memory_space=pltpu.VMEM)] * n,
        out_shape=[jax.ShapeDtypeStruct(array.shape, array.dtype) for array in arrays],
        scratch_shapes=[pltpu.SemaphoreType.DMA((n,))],
        compiler_params=pltpu.CompilerParams(vmem_limit_bytes=2 * MIB),
        cost_estimate=small_cost(),
    )(*arrays)


def body(tokens, expert_ids, gate_codes, w_gate, w_up, w_down):
    nodes = lax.axis_size("node")
    ring = nodes // SPAN
    far = ring // 2
    tok, top = expert_ids.shape
    half = tok // 2

    def chip_at(pos):
        return 2 * pos if pos < far else 2 * (ring - 1 - pos) + 1

    def perm(step):
        return [
            (chip_at(pos) * SPAN + core, chip_at((pos + step) % ring) * SPAN + core)
            for pos in range(ring)
            for core in range(SPAN)
        ]

    forward, backward = perm(1), perm(-1)
    swap = [(node, node ^ 1) for node in range(nodes)]
    expert = lax.div(lax.axis_index("node"), jnp.int32(SPAN)).reshape(1)
    weights = (w_gate, w_up, w_down)
    tokens, weights, expert = lax.optimization_barrier((tokens, weights, expert))

    near = [lax.ppermute(tokens, "node", way) for way in (forward, backward)]
    other = [lax.ppermute(weight, "node", swap) for weight in weights]
    digits = code_digits(ring, expert_ids, gate_codes)
    digits, *other[:2] = lax.optimization_barrier((digits, *other[:2]))
    marks = [lax.ppermute(digits, "node", way) for way in (forward, backward)]
    halves, marks, other, weights = lax.optimization_barrier(
        (split(near), marks, other, weights)
    )
    own = bring_in(weights)

    halves = merged(halves, marks)
    mine = merged([tokens[:half], tokens[half:]], [digits])
    ahead = [[None, halves[0]], [None, halves[1]]]
    behind = [[None, halves[3]], [None, halves[2]]]
    parts = {}

    def work(names, blocks, after=(), **how):
        held = [parts[name] for name in after]
        blocks, held = lax.optimization_barrier((blocks, held))
        parts.update(zip(after, held))
        parts.update(zip(names, expert_parts(ring, half, expert, blocks, own, other, **how)))
        return names

    def send(s, wave, after):
        held = [parts[name] for name in after]
        pair, held = lax.optimization_barrier(((ahead[wave][-1], behind[wave][-1]), held))
        parts.update(zip(after, held))
        ahead[wave][-1], behind[wave][-1] = pair
        ahead[wave].append(lax.ppermute(pair[0], "node", forward))
        behind[wave].append(lax.ppermute(pair[1], "node", backward))

    for wave in range(2):
        send(2, wave, [])
    names = [(offset, h) for offset in (0, -1, 1) for h in range(2)]
    done = [work(names, [*mine, *halves])]
    for s in range(3, far + 1):
        for wave in range(2):
            if s < far or wave == 0:
                send(s, wave, done.pop(0))
            names = [(1 - s, wave), (s - 1, 1 - wave)]
            after = done[-1] if s == far and wave == 1 else []
            done.append(work(names, [ahead[wave][s - 1], behind[wave][s - 1]], after))
    work([(far, 0), (far, 1)], [ahead[0][far], behind[0][far]], done[-1])
    parts[-far, 1] = parts[far, 1]

    firsts = [(1 - far, 0), (far - 1, 1)]
    held, after = lax.optimization_barrier(
        ([parts[name] for name in firsts], [parts[name] for name in done[-1]])
    )
    parts.update(zip(firsts, held))
    parts.update(zip(done[-1], after))

    early = [(h, sign) for h in range(2) for sign in (1, -1) if (h == 0) != (sign == 1)]
    late = [(h, -sign) for h, sign in early]
    ways = {1: forward, -1: backward}

    def pass_on(group, totals):
        return [lax.ppermute(t, "node", ways[sign]) for t, (h, sign) in zip(totals, group)]

    def shares(group, offset):
        return [parts[sign * offset, h] for h, sign in group]

    first = pass_on(early, shares(early, far - 1))
    last = [pass_on(late, shares(late, far))]
    for k in range(2, far + 1):
        if k < far:
            first = pass_on(early, add(shares(early, far - k), first, cost=AHEAD))
            after = []
        else:
            first = add(shares(early, 0), first, dtype=jnp.float32, cost=AHEAD)
            after = first
        terms = shares(late, far - k + 1)
        if k == far - 1:
            totals = add(terms, last[0], after, pieces=2)
            last = [pass_on(late, totals[p::2]) for p in range(2)]
        else:
            size = half // len(last)
            last = [
                pass_on(late, add(terms, came, after, first=p * size))
                for p, came in enumerate(last)
            ]
    return close(first, last)


def solution(mesh):
    in_specs = (
        P(("groups", "node"), None),
        P(("groups", "node"), None),
        P(("groups", "node"), None),
        P(None, "node"),
        P(None, "node"),
        P("node", None),
    )
    out_specs = P(("groups", "node"), None)
    return jax.shard_map(body, mesh=mesh, in_specs=in_specs, out_specs=out_specs, check_vma=False)
```

```python
import functools

import jax
import jax.numpy as jnp
from jax import lax
from jax.experimental import pallas as pl
from jax.experimental.pallas import tpu as pltpu
from jax.sharding import PartitionSpec as P

SPAN = 2
LANES = 128
DIGIT = 64
TILE = 256
WIDE = 512
MIB = 1 << 20
AHEAD = 6 * MIB
FORWARD = 40 * 10**9


def expert_kernel(n, shifts, experts, dim, half, expert_ref, *refs):
    blocks, sources = refs[:n], refs[n : 2 * n]
    weights, outs = refs[2 * n : 2 * n + 6], refs[2 * n + 6 : -3]
    rows_ref, scale_ref, hidden_ref = refs[-3:]
    hid = weights[0].shape[1]
    expert = expert_ref[0]
    first = 0
    for block, source, shift in zip(blocks, sources, shifts):
        count = block.shape[0]
        mine = expert + shift
        lane = lax.broadcasted_iota(jnp.int32, (count, LANES), 1)
        at = pl.ds(first, count)
        first += count
        rows_ref[at, :] = block[:, :dim]
        digits = source[:, dim:].astype(jnp.float32)
        codes = jnp.where(lane == mine, digits * float(DIGIT), 0.0)
        codes = codes + jnp.where(lane == mine + experts, digits, 0.0)
        code = jnp.sum(codes, 1, keepdims=True) * (1.0 / 4096.0)
        scale_ref[at, :] = jnp.broadcast_to(code, (count, LANES))

    for side in range(SPAN):
        gate_ref, up_ref, _ = weights[3 * side : 3 * side + 3]

        def hidden_tile(j, carry, side=side, gate_ref=gate_ref, up_ref=up_ref):
            at = pl.ds(pl.multiple_of(j * TILE, TILE), TILE)
            rows = rows_ref[...]
            gate = jnp.dot(rows, gate_ref[:, at], preferred_element_type=jnp.float32)
            upward = jnp.dot(rows, up_ref[:, at], preferred_element_type=jnp.float32)
            hidden = gate / (1.0 + jnp.exp(-gate)) * upward * scale_ref[:, :1]
            to = pl.ds(pl.multiple_of(side * hid + j * TILE, TILE), TILE)
            hidden_ref[:, to] = hidden.astype(jnp.bfloat16)
            return carry

        lax.fori_loop(0, hid // TILE, hidden_tile, 0)

    def out_tile(j, carry):
        at = pl.ds(pl.multiple_of(j * WIDE, WIDE), WIDE)
        part = jnp.dot(
            hidden_ref[:, :hid], weights[2][:, at], preferred_element_type=jnp.float32
        ) + jnp.dot(hidden_ref[:, hid:], weights[5][:, at], preferred_element_type=jnp.float32)
        part = part.astype(jnp.bfloat16)
        for i, out in enumerate(outs):
            out[:, at] = part[i * half : (i + 1) * half, :]
        return carry

    lax.fori_loop(0, dim // WIDE, out_tile, 0)


def small_cost():
    return pl.CostEstimate(flops=1024, bytes_accessed=1024, transcendentals=0)


def expert_parts(experts, half, expert, blocks, sources, shifts, own, other, cost=1024):
    dim, hid = own[0].shape
    n, rows = len(blocks), sum(block.shape[0] for block in blocks)
    specs = [pl.BlockSpec(memory_space=pltpu.SMEM)]
    specs += [pl.BlockSpec(memory_space=pltpu.VMEM)] * (2 * n + 6)
    return pl.pallas_call(
        functools.partial(expert_kernel, n, shifts, experts, dim, half),
        in_specs=specs,
        out_specs=[pl.BlockSpec(memory_space=pltpu.VMEM)] * (rows // half),
        out_shape=[jax.ShapeDtypeStruct((half, dim), jnp.bfloat16)] * (rows // half),
        scratch_shapes=[
            pltpu.VMEM((rows, dim), jnp.bfloat16),
            pltpu.VMEM((rows, LANES), jnp.float32),
            pltpu.VMEM((rows, SPAN * hid), jnp.bfloat16),
        ],
        compiler_params=pltpu.CompilerParams(vmem_limit_bytes=8 * MIB),
        cost_estimate=pl.CostEstimate(flops=cost, bytes_accessed=1024, transcendentals=0),
    )(expert, *blocks, *sources, *own, *other)


def add_kernel(n, pieces, first, *refs):
    outs = refs[-n * pieces :]
    size = outs[0].shape[0]
    for i, (left_ref, right_ref) in enumerate(zip(refs[:n], refs[n : 2 * n])):
        for p in range(pieces):
            left = left_ref[first + p * size : first + (p + 1) * size, :]
            right = right_ref[p * size : (p + 1) * size, :]
            out = outs[i * pieces + p]
            out[...] = left.astype(out.dtype) + right.astype(out.dtype)


def add(lefts, rights, after=(), pieces=1, first=0, dtype=None, cost=1024):
    n = len(lefts)
    rows, dim = rights[0].shape
    shape = jax.ShapeDtypeStruct((rows // pieces, dim), dtype or rights[0].dtype)
    return pl.pallas_call(
        functools.partial(add_kernel, n, pieces, first),
        in_specs=[pl.BlockSpec(memory_space=pltpu.VMEM)] * (2 * n)
        + [pl.BlockSpec(memory_space=pl.ANY)] * len(after),
        out_specs=[pl.BlockSpec(memory_space=pltpu.VMEM)] * (n * pieces),
        out_shape=[shape] * (n * pieces),
        compiler_params=pltpu.CompilerParams(vmem_limit_bytes=6 * MIB),
        cost_estimate=pl.CostEstimate(flops=1024, bytes_accessed=cost, transcendentals=0),
    )(*lefts, *rights, *after)


def split_kernel(n, *refs):
    for i, ref in enumerate(refs[:n]):
        half = ref.shape[0] // 2
        for h in range(2):
            refs[n + 2 * i + h][...] = ref[h * half : (h + 1) * half, :]


def split(arrays):
    n = len(arrays)
    rows, dim = arrays[0].shape
    return pl.pallas_call(
        functools.partial(split_kernel, n),
        in_specs=[pl.BlockSpec(memory_space=pltpu.VMEM)] * n,
        out_specs=[pl.BlockSpec(memory_space=pltpu.VMEM)] * (2 * n),
        out_shape=[jax.ShapeDtypeStruct((rows // 2, dim), arrays[0].dtype)] * (2 * n),
        compiler_params=pltpu.CompilerParams(vmem_limit_bytes=6 * MIB),
        cost_estimate=pl.CostEstimate(flops=FORWARD, bytes_accessed=1024, transcendentals=0),
    )(*arrays)


def merge_kernel(n, starts, *refs):
    for i, out in enumerate(refs[2 * n :]):
        half, dim = refs[i].shape
        out[:, :dim] = refs[i][...]
        out[:, dim:] = refs[n + i][starts[i] : starts[i] + half, :]


def merged(halves, digits, starts):
    n = len(halves)
    rows, dim = halves[0].shape
    return pl.pallas_call(
        functools.partial(merge_kernel, n, starts),
        in_specs=[pl.BlockSpec(memory_space=pltpu.VMEM)] * (2 * n),
        out_specs=[pl.BlockSpec(memory_space=pltpu.VMEM)] * n,
        out_shape=[jax.ShapeDtypeStruct((rows, dim + LANES), halves[0].dtype)] * n,
        compiler_params=pltpu.CompilerParams(vmem_limit_bytes=6 * MIB),
        cost_estimate=small_cost(),
    )(*halves, *digits)


def close_kernel(*refs):
    out_ref, bases, pieces = refs[-1], refs[:2], refs[2:-1]
    size = pieces[0].shape[0]
    for h, base_ref in enumerate(bases):
        half = base_ref.shape[0]
        for p in range(len(pieces) // 2):
            at = slice(p * size, (p + 1) * size)
            total = base_ref[at, :] + pieces[2 * p + h][...].astype(jnp.float32)
            out_ref[h * half + p * size : h * half + (p + 1) * size, :] = total.astype(out_ref.dtype)


def close(bases, pieces):
    terms = [term for piece in pieces for term in piece]
    half, dim = bases[0].shape
    return pl.pallas_call(
        close_kernel,
        in_specs=[pl.BlockSpec(memory_space=pltpu.VMEM)] * (len(terms) + 2),
        out_shape=jax.ShapeDtypeStruct((2 * half, dim), terms[0].dtype),
        compiler_params=pltpu.CompilerParams(vmem_limit_bytes=8 * MIB),
        cost_estimate=small_cost(),
    )(*bases, *terms)


def digits_kernel(experts, ids_ref, codes_ref, out_ref):
    tok = out_ref.shape[0]
    row = lax.broadcasted_iota(jnp.int32, (LANES, tok), 0)
    part, expert = row // experts, lax.rem(row, experts)

    def swapped(ref, k):
        return jnp.concatenate([ref[k : k + 1, tok // 2 :], ref[k : k + 1, : tok // 2]], 1)

    code = jnp.zeros((LANES, tok), jnp.int32)
    for k in range(ids_ref.shape[0]):
        ids = jnp.where(part < 2, ids_ref[k : k + 1, :], swapped(ids_ref, k))
        codes = jnp.where(part < 2, codes_ref[k : k + 1, :], swapped(codes_ref, k))
        code = code + jnp.where(ids == expert, codes, 0)
    digits = jnp.where(lax.rem(part, 2) == 0, code // DIGIT, code % DIGIT)
    out_ref[...] = jnp.transpose(digits.astype(jnp.float32)).astype(out_ref.dtype)


def code_digits(experts, ids, codes):
    return pl.pallas_call(
        functools.partial(digits_kernel, experts),
        in_specs=[pl.BlockSpec(memory_space=pltpu.VMEM)] * 2,
        out_shape=jax.ShapeDtypeStruct((ids.shape[0], LANES), jnp.bfloat16),
        compiler_params=pltpu.CompilerParams(vmem_limit_bytes=2 * MIB),
        cost_estimate=small_cost(),
    )(ids.T, codes.T)


def bring_in_kernel(n, *refs):
    copies = [
        pltpu.make_async_copy(refs[i], refs[n + i], refs[2 * n].at[i]) for i in range(n)
    ]
    for copy in copies:
        copy.start()
    for copy in copies:
        copy.wait()


def bring_in(arrays):
    n = len(arrays)
    return pl.pallas_call(
        functools.partial(bring_in_kernel, n),
        in_specs=[pl.BlockSpec(memory_space=pl.ANY)] * n,
        out_specs=[pl.BlockSpec(memory_space=pltpu.VMEM)] * n,
        out_shape=[jax.ShapeDtypeStruct(array.shape, array.dtype) for array in arrays],
        scratch_shapes=[pltpu.SemaphoreType.DMA((n,))],
        compiler_params=pltpu.CompilerParams(vmem_limit_bytes=2 * MIB),
        cost_estimate=small_cost(),
    )(*arrays)


def body(tokens, expert_ids, gate_codes, w_gate, w_up, w_down):
    nodes = lax.axis_size("node")
    ring = nodes // SPAN
    far = ring // 2
    tok, top = expert_ids.shape
    half = tok // 2

    def chip_at(pos):
        return 2 * pos if pos < far else 2 * (ring - 1 - pos) + 1

    def perm(step):
        return [
            (chip_at(pos) * SPAN + core, chip_at((pos + step) % ring) * SPAN + core)
            for pos in range(ring)
            for core in range(SPAN)
        ]

    forward, backward = perm(1), perm(-1)
    swap = [(node, node ^ 1) for node in range(nodes)]
    expert = lax.div(lax.axis_index("node"), jnp.int32(SPAN)).reshape(1)
    weights = (w_gate, w_up, w_down)
    tokens, weights, expert = lax.optimization_barrier((tokens, weights, expert))

    near = [lax.ppermute(tokens, "node", way) for way in (forward, backward)]
    other = [lax.ppermute(weight, "node", swap) for weight in weights]
    digits = code_digits(ring, expert_ids, gate_codes)
    digits, *other[:2] = lax.optimization_barrier((digits, *other[:2]))
    marks = [lax.ppermute(digits, "node", way) for way in (forward, backward)]
    halves, marks, other, weights = lax.optimization_barrier(
        (split(near), marks, other, weights)
    )
    own = bring_in(weights)

    lead = merged([halves[0], halves[3]], marks, (0, half))
    mine = merged([tokens[:half], tokens[half:]], [digits, digits], (0, half))
    ahead = [[None, lead[0]], [None, halves[1]]]
    behind = [[None, lead[1]], [None, halves[2]]]
    parts = {}

    def work(names, blocks, sources, after=(), **how):
        held = [parts[name] for name in after]
        blocks, held = lax.optimization_barrier((blocks, held))
        parts.update(zip(after, held))
        shifts = [0 if block.shape == source.shape else 2 * ring for block, source in zip(blocks, sources)]
        shares = expert_parts(ring, half, expert, blocks, sources, shifts, own, other, **how)
        parts.update(zip(names, shares))
        return names

    def send(s, wave, after):
        held = [parts[name] for name in after]
        pair, held = lax.optimization_barrier(((ahead[wave][-1], behind[wave][-1]), held))
        parts.update(zip(after, held))
        ahead[wave][-1], behind[wave][-1] = pair
        ahead[wave].append(lax.ppermute(pair[0], "node", forward))
        behind[wave].append(lax.ppermute(pair[1], "node", backward))

    for wave in range(2):
        send(2, wave, [])
    names = [(offset, h) for offset in (0, -1, 1) for h in range(2)]
    blocks = [*mine, lead[0], halves[1], halves[2], lead[1]]
    done = [work(names, blocks, [*mine, lead[0], lead[0], lead[1], lead[1]])]
    for s in range(3, far + 1):
        for wave in range(2):
            if s < far or wave == 0:
                send(s, wave, done.pop(0))
            names = [(1 - s, wave), (s - 1, 1 - wave)]
            after = done[-1] if s == far and wave == 1 else []
            blocks = [ahead[wave][s - 1], behind[wave][s - 1]]
            sources = [ahead[0][s - 1], behind[0][s - 1]]
            cost = FORWARD // 4 if wave else 1024
            done.append(work(names, blocks, sources, after, cost=cost))
    last = [ahead[0][far], behind[0][far]]
    work([(far, 0), (far, 1)], last, last, done[-1])
    parts[-far, 1] = parts[far, 1]

    firsts = [(1 - far, 0), (far - 1, 1)]
    held, after = lax.optimization_barrier(
        ([parts[name] for name in firsts], [parts[name] for name in done[-1]])
    )
    parts.update(zip(firsts, held))
    parts.update(zip(done[-1], after))

    early = [(h, sign) for h in range(2) for sign in (1, -1) if (h == 0) != (sign == 1)]
    late = [(h, -sign) for h, sign in early]
    ways = {1: forward, -1: backward}

    def pass_on(group, totals):
        return [lax.ppermute(t, "node", ways[sign]) for t, (h, sign) in zip(totals, group)]

    def shares(group, offset):
        return [parts[sign * offset, h] for h, sign in group]

    first = pass_on(early, shares(early, far - 1))
    last = [pass_on(late, shares(late, far))]
    for k in range(2, far + 1):
        if k < far:
            first = pass_on(early, add(shares(early, far - k), first, cost=AHEAD))
            after = []
        else:
            first = add(shares(early, 0), first, dtype=jnp.float32, cost=AHEAD)
            after = first
        terms = shares(late, far - k + 1)
        if k == far - 1:
            totals = add(terms, last[0], after, pieces=2)
            last = [pass_on(late, totals[p::2]) for p in range(2)]
        else:
            size = half // len(last)
            last = [
                pass_on(late, add(terms, came, after, first=p * size))
                for p, came in enumerate(last)
            ]
    return close(first, last)


def solution(mesh):
    in_specs = (
        P(("groups", "node"), None),
        P(("groups", "node"), None),
        P(("groups", "node"), None),
        P(None, "node"),
        P(None, "node"),
        P("node", None),
    )
    out_specs = P(("groups", "node"), None)
    return jax.shard_map(body, mesh=mesh, in_specs=in_specs, out_specs=out_specs, check_vma=False)
```

```python
import functools

import jax
import jax.numpy as jnp
from jax import lax
from jax.experimental import pallas as pl
from jax.experimental.pallas import tpu as pltpu
from jax.sharding import PartitionSpec as P

SPAN = 2
LANES = 128
DIGIT = 64
TILE = 256
WIDE = 512
MIB = 1 << 20
AHEAD = 6 * MIB
FORWARD = 40 * 10**9


def expert_kernel(n, shifts, experts, dim, half, expert_ref, *refs):
    blocks, sources = refs[:n], refs[n : 2 * n]
    weights, outs = refs[2 * n : 2 * n + 6], refs[2 * n + 6 : -3]
    rows_ref, scale_ref, hidden_ref = refs[-3:]
    hid = weights[0].shape[1]
    expert = expert_ref[0]
    first = 0
    for block, source, shift in zip(blocks, sources, shifts):
        count = block.shape[0]
        mine = expert + shift
        lane = lax.broadcasted_iota(jnp.int32, (count, LANES), 1)
        at = pl.ds(first, count)
        first += count
        rows_ref[at, :] = block[:, :dim]
        digits = source[:, dim:].astype(jnp.float32)
        codes = jnp.where(lane == mine, digits * float(DIGIT), 0.0)
        codes = codes + jnp.where(lane == mine + experts, digits, 0.0)
        code = jnp.sum(codes, 1, keepdims=True) * (1.0 / 4096.0)
        scale_ref[at, :] = jnp.broadcast_to(code, (count, LANES))

    for side in range(SPAN):
        gate_ref, up_ref, _ = weights[3 * side : 3 * side + 3]

        def hidden_tile(j, carry, side=side, gate_ref=gate_ref, up_ref=up_ref):
            at = pl.ds(pl.multiple_of(j * TILE, TILE), TILE)
            rows = rows_ref[...]
            gate = jnp.dot(rows, gate_ref[:, at], preferred_element_type=jnp.float32)
            upward = jnp.dot(rows, up_ref[:, at], preferred_element_type=jnp.float32)
            hidden = gate / (1.0 + jnp.exp(-gate)) * upward * scale_ref[:, :1]
            to = pl.ds(pl.multiple_of(side * hid + j * TILE, TILE), TILE)
            hidden_ref[:, to] = hidden.astype(jnp.bfloat16)
            return carry

        lax.fori_loop(0, hid // TILE, hidden_tile, 0)

    def out_tile(j, carry):
        at = pl.ds(pl.multiple_of(j * WIDE, WIDE), WIDE)
        part = jnp.dot(
            hidden_ref[:, :hid], weights[2][:, at], preferred_element_type=jnp.float32
        ) + jnp.dot(hidden_ref[:, hid:], weights[5][:, at], preferred_element_type=jnp.float32)
        part = part.astype(jnp.bfloat16)
        for i, out in enumerate(outs):
            out[:, at] = part[i * half : (i + 1) * half, :]
        return carry

    lax.fori_loop(0, dim // WIDE, out_tile, 0)


def small_cost():
    return pl.CostEstimate(flops=1024, bytes_accessed=1024, transcendentals=0)


def expert_parts(experts, half, expert, blocks, sources, shifts, own, other, cost=1024):
    dim, hid = own[0].shape
    n, rows = len(blocks), sum(block.shape[0] for block in blocks)
    specs = [pl.BlockSpec(memory_space=pltpu.SMEM)]
    specs += [pl.BlockSpec(memory_space=pltpu.VMEM)] * (2 * n + 6)
    return pl.pallas_call(
        functools.partial(expert_kernel, n, shifts, experts, dim, half),
        in_specs=specs,
        out_specs=[pl.BlockSpec(memory_space=pltpu.VMEM)] * (rows // half),
        out_shape=[jax.ShapeDtypeStruct((half, dim), jnp.bfloat16)] * (rows // half),
        scratch_shapes=[
            pltpu.VMEM((rows, dim), jnp.bfloat16),
            pltpu.VMEM((rows, LANES), jnp.float32),
            pltpu.VMEM((rows, SPAN * hid), jnp.bfloat16),
        ],
        compiler_params=pltpu.CompilerParams(vmem_limit_bytes=8 * MIB),
        cost_estimate=pl.CostEstimate(flops=cost, bytes_accessed=1024, transcendentals=0),
    )(expert, *blocks, *sources, *own, *other)


def add_kernel(n, pieces, first, *refs):
    outs = refs[-n * pieces :]
    size = outs[0].shape[0]
    for i, (left_ref, right_ref) in enumerate(zip(refs[:n], refs[n : 2 * n])):
        for p in range(pieces):
            left = left_ref[first + p * size : first + (p + 1) * size, :]
            right = right_ref[p * size : (p + 1) * size, :]
            out = outs[i * pieces + p]
            out[...] = left.astype(out.dtype) + right.astype(out.dtype)


def add(lefts, rights, after=(), pieces=1, first=0, dtype=None, cost=1024):
    n = len(lefts)
    rows, dim = rights[0].shape
    shape = jax.ShapeDtypeStruct((rows // pieces, dim), dtype or rights[0].dtype)
    return pl.pallas_call(
        functools.partial(add_kernel, n, pieces, first),
        in_specs=[pl.BlockSpec(memory_space=pltpu.VMEM)] * (2 * n)
        + [pl.BlockSpec(memory_space=pl.ANY)] * len(after),
        out_specs=[pl.BlockSpec(memory_space=pltpu.VMEM)] * (n * pieces),
        out_shape=[shape] * (n * pieces),
        compiler_params=pltpu.CompilerParams(vmem_limit_bytes=6 * MIB),
        cost_estimate=pl.CostEstimate(flops=1024, bytes_accessed=cost, transcendentals=0),
    )(*lefts, *rights, *after)


def split_kernel(n, *refs):
    for i, ref in enumerate(refs[:n]):
        half = ref.shape[0] // 2
        for h in range(2):
            refs[n + 2 * i + h][...] = ref[h * half : (h + 1) * half, :]


def split(arrays):
    n = len(arrays)
    rows, dim = arrays[0].shape
    return pl.pallas_call(
        functools.partial(split_kernel, n),
        in_specs=[pl.BlockSpec(memory_space=pltpu.VMEM)] * n,
        out_specs=[pl.BlockSpec(memory_space=pltpu.VMEM)] * (2 * n),
        out_shape=[jax.ShapeDtypeStruct((rows // 2, dim), arrays[0].dtype)] * (2 * n),
        compiler_params=pltpu.CompilerParams(vmem_limit_bytes=6 * MIB),
        cost_estimate=pl.CostEstimate(flops=FORWARD, bytes_accessed=1024, transcendentals=0),
    )(*arrays)


def merge_kernel(n, starts, *refs):
    for i, out in enumerate(refs[2 * n :]):
        half, dim = refs[i].shape
        out[:, :dim] = refs[i][...]
        out[:, dim:] = refs[n + i][starts[i] : starts[i] + half, :]


def merged(halves, digits, starts):
    n = len(halves)
    rows, dim = halves[0].shape
    return pl.pallas_call(
        functools.partial(merge_kernel, n, starts),
        in_specs=[pl.BlockSpec(memory_space=pltpu.VMEM)] * (2 * n),
        out_specs=[pl.BlockSpec(memory_space=pltpu.VMEM)] * n,
        out_shape=[jax.ShapeDtypeStruct((rows, dim + LANES), halves[0].dtype)] * n,
        compiler_params=pltpu.CompilerParams(vmem_limit_bytes=6 * MIB),
        cost_estimate=small_cost(),
    )(*halves, *digits)


def close_kernel(*refs):
    out_ref, bases, pieces = refs[-1], refs[:2], refs[2:-1]
    size = pieces[0].shape[0]
    for h, base_ref in enumerate(bases):
        half = base_ref.shape[0]
        for p in range(len(pieces) // 2):
            at = slice(p * size, (p + 1) * size)
            total = base_ref[at, :] + pieces[2 * p + h][...].astype(jnp.float32)
            out_ref[h * half + p * size : h * half + (p + 1) * size, :] = total.astype(out_ref.dtype)


def close(bases, pieces):
    terms = [term for piece in pieces for term in piece]
    half, dim = bases[0].shape
    return pl.pallas_call(
        close_kernel,
        in_specs=[pl.BlockSpec(memory_space=pltpu.VMEM)] * (len(terms) + 2),
        out_shape=jax.ShapeDtypeStruct((2 * half, dim), terms[0].dtype),
        compiler_params=pltpu.CompilerParams(vmem_limit_bytes=8 * MIB),
        cost_estimate=small_cost(),
    )(*bases, *terms)


def digits_kernel(experts, ids_ref, codes_ref, out_ref):
    tok = out_ref.shape[0]
    row = lax.broadcasted_iota(jnp.int32, (LANES, tok), 0)
    part, expert = row // experts, lax.rem(row, experts)

    def swapped(ref, k):
        return jnp.concatenate([ref[k : k + 1, tok // 2 :], ref[k : k + 1, : tok // 2]], 1)

    code = jnp.zeros((LANES, tok), jnp.int32)
    for k in range(ids_ref.shape[0]):
        ids = jnp.where(part < 2, ids_ref[k : k + 1, :], swapped(ids_ref, k))
        codes = jnp.where(part < 2, codes_ref[k : k + 1, :], swapped(codes_ref, k))
        code = code + jnp.where(ids == expert, codes, 0)
    digits = jnp.where(lax.rem(part, 2) == 0, code // DIGIT, code % DIGIT)
    out_ref[...] = jnp.transpose(digits.astype(jnp.float32)).astype(out_ref.dtype)


def code_digits(experts, ids, codes):
    return pl.pallas_call(
        functools.partial(digits_kernel, experts),
        in_specs=[pl.BlockSpec(memory_space=pltpu.VMEM)] * 2,
        out_shape=jax.ShapeDtypeStruct((ids.shape[0], LANES), jnp.bfloat16),
        compiler_params=pltpu.CompilerParams(vmem_limit_bytes=2 * MIB),
        cost_estimate=small_cost(),
    )(ids.T, codes.T)


def bring_in_kernel(n, *refs):
    copies = [
        pltpu.make_async_copy(refs[i], refs[n + i], refs[2 * n].at[i]) for i in range(n)
    ]
    for copy in copies:
        copy.start()
    for copy in copies:
        copy.wait()


def bring_in(arrays):
    n = len(arrays)
    return pl.pallas_call(
        functools.partial(bring_in_kernel, n),
        in_specs=[pl.BlockSpec(memory_space=pl.ANY)] * n,
        out_specs=[pl.BlockSpec(memory_space=pltpu.VMEM)] * n,
        out_shape=[jax.ShapeDtypeStruct(array.shape, array.dtype) for array in arrays],
        scratch_shapes=[pltpu.SemaphoreType.DMA((n,))],
        compiler_params=pltpu.CompilerParams(vmem_limit_bytes=2 * MIB),
        cost_estimate=small_cost(),
    )(*arrays)


def body(tokens, expert_ids, gate_codes, w_gate, w_up, w_down):
    nodes = lax.axis_size("node")
    ring = nodes // SPAN
    far = ring // 2
    tok, top = expert_ids.shape
    half = tok // 2

    def chip_at(pos):
        return 2 * pos if pos < far else 2 * (ring - 1 - pos) + 1

    def perm(step):
        return [
            (chip_at(pos) * SPAN + core, chip_at((pos + step) % ring) * SPAN + core)
            for pos in range(ring)
            for core in range(SPAN)
        ]

    forward, backward = perm(1), perm(-1)
    swap = [(node, node ^ 1) for node in range(nodes)]
    expert = lax.div(lax.axis_index("node"), jnp.int32(SPAN)).reshape(1)
    weights = (w_gate, w_up, w_down)
    tokens, weights, expert = lax.optimization_barrier((tokens, weights, expert))

    near = [lax.ppermute(tokens, "node", way) for way in (forward, backward)]
    other = [lax.ppermute(weight, "node", swap) for weight in weights]
    digits = code_digits(ring, expert_ids, gate_codes)
    digits, *other[:2] = lax.optimization_barrier((digits, *other[:2]))
    marks = [lax.ppermute(digits, "node", way) for way in (forward, backward)]
    halves, marks, other, weights = lax.optimization_barrier(
        (split(near), marks, other, weights)
    )
    own = bring_in(weights)

    lead = merged([halves[0], halves[3]], marks, (0, half))
    mine = merged([tokens[:half], tokens[half:]], [digits, digits], (0, half))
    ahead = [[None, lead[0]], [None, halves[1]]]
    behind = [[None, lead[1]], [None, halves[2]]]
    parts = {}

    def work(names, blocks, sources, after=(), **how):
        held = [parts[name] for name in after]
        blocks, held = lax.optimization_barrier((blocks, held))
        parts.update(zip(after, held))
        shifts = [0 if block.shape == source.shape else 2 * ring for block, source in zip(blocks, sources)]
        shares = expert_parts(ring, half, expert, blocks, sources, shifts, own, other, **how)
        parts.update(zip(names, shares))
        return names

    def send(s, wave, after):
        held = [parts[name] for name in after]
        pair, held = lax.optimization_barrier(((ahead[wave][-1], behind[wave][-1]), held))
        parts.update(zip(after, held))
        ahead[wave][-1], behind[wave][-1] = pair
        ahead[wave].append(lax.ppermute(pair[0], "node", forward))
        behind[wave].append(lax.ppermute(pair[1], "node", backward))

    for wave in range(2):
        send(2, wave, [])
    names = [(offset, h) for offset in (0, -1, 1) for h in range(2)]
    blocks = [*mine, lead[0], halves[1], halves[2], lead[1]]
    done = [work(names, blocks, [*mine, lead[0], lead[0], lead[1], lead[1]])]
    for s in range(3, far + 1):
        for wave in range(2):
            if s < far or wave == 0:
                send(s, wave, done.pop(0))
            names = [(1 - s, wave), (s - 1, 1 - wave)]
            after = done[-1] if s == far and wave == 1 else []
            blocks = [ahead[wave][s - 1], behind[wave][s - 1]]
            sources = [ahead[0][s - 1], behind[0][s - 1]]
            cost = FORWARD // 4 if wave else 1024
            done.append(work(names, blocks, sources, after, cost=cost))
    last = [ahead[0][far], behind[0][far]]
    work([(far, 0), (far, 1)], last, last, done[-1])
    parts[-far, 1] = parts[far, 1]

    early = [(h, sign) for h in range(2) for sign in (1, -1) if (h == 0) != (sign == 1)]
    late = [(h, -sign) for h, sign in early]
    ways = {1: forward, -1: backward}

    def pass_on(group, totals):
        return [lax.ppermute(t, "node", ways[sign]) for t, (h, sign) in zip(totals, group)]

    def shares(group, offset):
        return [parts[sign * offset, h] for h, sign in group]

    first = pass_on(early, shares(early, far - 1))
    last = [pass_on(late, shares(late, far))]
    for k in range(2, far + 1):
        if k < far:
            first = pass_on(early, add(shares(early, far - k), first, cost=AHEAD))
            after = []
        else:
            first = add(shares(early, 0), first, dtype=jnp.float32, cost=AHEAD)
            after = first
        terms = shares(late, far - k + 1)
        if k == far - 1:
            totals = add(terms, last[0], after, pieces=2)
            last = [pass_on(late, totals[p::2]) for p in range(2)]
        else:
            size = half // len(last)
            last = [
                pass_on(late, add(terms, came, after, first=p * size))
                for p, came in enumerate(last)
            ]
    return close(first, last)


def solution(mesh):
    in_specs = (
        P(("groups", "node"), None),
        P(("groups", "node"), None),
        P(("groups", "node"), None),
        P(None, "node"),
        P(None, "node"),
        P("node", None),
    )
    out_specs = P(("groups", "node"), None)
    return jax.shard_map(body, mesh=mesh, in_specs=in_specs, out_specs=out_specs, check_vma=False)
```

```python
import functools

import jax
import jax.numpy as jnp
from jax import lax
from jax.experimental import pallas as pl
from jax.experimental.pallas import tpu as pltpu
from jax.sharding import PartitionSpec as P

SPAN = 2
LANES = 128
DIGIT = 64
TILE = 256
WIDE = 512
MIB = 1 << 20
AHEAD = 6 * MIB
FORWARD = 40 * 10**9


def expert_kernel(n, shifts, experts, dim, half, expert_ref, *refs):
    blocks, sources = refs[:n], refs[n : 2 * n]
    weights, outs = refs[2 * n : 2 * n + 6], refs[2 * n + 6 : -3]
    rows_ref, scale_ref, hidden_ref = refs[-3:]
    hid = weights[0].shape[1]
    expert = expert_ref[0]
    first = 0
    for block, source, shift in zip(blocks, sources, shifts):
        count = block.shape[0]
        mine = expert + shift
        lane = lax.broadcasted_iota(jnp.int32, (count, LANES), 1)
        at = pl.ds(first, count)
        first += count
        rows_ref[at, :] = block[:, :dim]
        digits = source[:, dim:].astype(jnp.float32)
        codes = jnp.where(lane == mine, digits * float(DIGIT), 0.0)
        codes = codes + jnp.where(lane == mine + experts, digits, 0.0)
        code = jnp.sum(codes, 1, keepdims=True) * (1.0 / 4096.0)
        scale_ref[at, :] = jnp.broadcast_to(code, (count, LANES))

    for side in range(SPAN):
        gate_ref, up_ref, _ = weights[3 * side : 3 * side + 3]

        def hidden_tile(j, carry, side=side, gate_ref=gate_ref, up_ref=up_ref):
            at = pl.ds(pl.multiple_of(j * TILE, TILE), TILE)
            rows = rows_ref[...]
            gate = jnp.dot(rows, gate_ref[:, at], preferred_element_type=jnp.float32)
            upward = jnp.dot(rows, up_ref[:, at], preferred_element_type=jnp.float32)
            hidden = gate / (1.0 + jnp.exp(-gate)) * upward * scale_ref[:, :1]
            to = pl.ds(pl.multiple_of(side * hid + j * TILE, TILE), TILE)
            hidden_ref[:, to] = hidden.astype(jnp.bfloat16)
            return carry

        lax.fori_loop(0, hid // TILE, hidden_tile, 0)

    def out_tile(j, carry):
        at = pl.ds(pl.multiple_of(j * WIDE, WIDE), WIDE)
        part = jnp.dot(
            hidden_ref[:, :hid], weights[2][:, at], preferred_element_type=jnp.float32
        ) + jnp.dot(hidden_ref[:, hid:], weights[5][:, at], preferred_element_type=jnp.float32)
        part = part.astype(jnp.bfloat16)
        for i, out in enumerate(outs):
            out[:, at] = part[i * half : (i + 1) * half, :]
        return carry

    lax.fori_loop(0, dim // WIDE, out_tile, 0)


def small_cost():
    return pl.CostEstimate(flops=1024, bytes_accessed=1024, transcendentals=0)


def expert_parts(experts, half, expert, blocks, sources, shifts, own, other, cost=1024):
    dim, hid = own[0].shape
    n, rows = len(blocks), sum(block.shape[0] for block in blocks)
    specs = [pl.BlockSpec(memory_space=pltpu.SMEM)]
    specs += [pl.BlockSpec(memory_space=pltpu.VMEM)] * (2 * n + 6)
    return pl.pallas_call(
        functools.partial(expert_kernel, n, shifts, experts, dim, half),
        in_specs=specs,
        out_specs=[pl.BlockSpec(memory_space=pltpu.VMEM)] * (rows // half),
        out_shape=[jax.ShapeDtypeStruct((half, dim), jnp.bfloat16)] * (rows // half),
        scratch_shapes=[
            pltpu.VMEM((rows, dim), jnp.bfloat16),
            pltpu.VMEM((rows, LANES), jnp.float32),
            pltpu.VMEM((rows, SPAN * hid), jnp.bfloat16),
        ],
        compiler_params=pltpu.CompilerParams(vmem_limit_bytes=8 * MIB),
        cost_estimate=pl.CostEstimate(flops=cost, bytes_accessed=1024, transcendentals=0),
    )(expert, *blocks, *sources, *own, *other)


def add_kernel(n, pieces, first, *refs):
    outs = refs[-n * pieces :]
    size = outs[0].shape[0]
    for i, (left_ref, right_ref) in enumerate(zip(refs[:n], refs[n : 2 * n])):
        for p in range(pieces):
            left = left_ref[first + p * size : first + (p + 1) * size, :]
            right = right_ref[p * size : (p + 1) * size, :]
            out = outs[i * pieces + p]
            out[...] = left.astype(out.dtype) + right.astype(out.dtype)


def add(lefts, rights, after=(), pieces=1, first=0, dtype=None, cost=1024):
    n = len(lefts)
    rows, dim = rights[0].shape
    shape = jax.ShapeDtypeStruct((rows // pieces, dim), dtype or rights[0].dtype)
    return pl.pallas_call(
        functools.partial(add_kernel, n, pieces, first),
        in_specs=[pl.BlockSpec(memory_space=pltpu.VMEM)] * (2 * n)
        + [pl.BlockSpec(memory_space=pl.ANY)] * len(after),
        out_specs=[pl.BlockSpec(memory_space=pltpu.VMEM)] * (n * pieces),
        out_shape=[shape] * (n * pieces),
        compiler_params=pltpu.CompilerParams(vmem_limit_bytes=6 * MIB),
        cost_estimate=pl.CostEstimate(flops=1024, bytes_accessed=cost, transcendentals=0),
    )(*lefts, *rights, *after)


def split_kernel(n, *refs):
    for i, ref in enumerate(refs[:n]):
        half = ref.shape[0] // 2
        for h in range(2):
            refs[n + 2 * i + h][...] = ref[h * half : (h + 1) * half, :]


def split(arrays):
    n = len(arrays)
    rows, dim = arrays[0].shape
    return pl.pallas_call(
        functools.partial(split_kernel, n),
        in_specs=[pl.BlockSpec(memory_space=pltpu.VMEM)] * n,
        out_specs=[pl.BlockSpec(memory_space=pltpu.VMEM)] * (2 * n),
        out_shape=[jax.ShapeDtypeStruct((rows // 2, dim), arrays[0].dtype)] * (2 * n),
        compiler_params=pltpu.CompilerParams(vmem_limit_bytes=6 * MIB),
        cost_estimate=pl.CostEstimate(flops=FORWARD, bytes_accessed=1024, transcendentals=0),
    )(*arrays)


def merge_kernel(n, starts, *refs):
    for i, out in enumerate(refs[2 * n :]):
        half, dim = refs[i].shape
        out[:, :dim] = refs[i][...]
        out[:, dim:] = refs[n + i][starts[i] : starts[i] + half, :]


def merged(halves, digits, starts):
    n = len(halves)
    rows, dim = halves[0].shape
    return pl.pallas_call(
        functools.partial(merge_kernel, n, starts),
        in_specs=[pl.BlockSpec(memory_space=pltpu.VMEM)] * (2 * n),
        out_specs=[pl.BlockSpec(memory_space=pltpu.VMEM)] * n,
        out_shape=[jax.ShapeDtypeStruct((rows, dim + LANES), halves[0].dtype)] * n,
        compiler_params=pltpu.CompilerParams(vmem_limit_bytes=6 * MIB),
        cost_estimate=small_cost(),
    )(*halves, *digits)


def close_kernel(*refs):
    out_ref, bases, pieces = refs[-1], refs[:2], refs[2:-1]
    size = pieces[0].shape[0]
    for h, base_ref in enumerate(bases):
        half = base_ref.shape[0]
        for p in range(len(pieces) // 2):
            at = slice(p * size, (p + 1) * size)
            total = base_ref[at, :] + pieces[2 * p + h][...].astype(jnp.float32)
            out_ref[h * half + p * size : h * half + (p + 1) * size, :] = total.astype(out_ref.dtype)


def close(bases, pieces):
    terms = [term for piece in pieces for term in piece]
    half, dim = bases[0].shape
    return pl.pallas_call(
        close_kernel,
        in_specs=[pl.BlockSpec(memory_space=pltpu.VMEM)] * (len(terms) + 2),
        out_shape=jax.ShapeDtypeStruct((2 * half, dim), terms[0].dtype),
        compiler_params=pltpu.CompilerParams(vmem_limit_bytes=8 * MIB),
        cost_estimate=small_cost(),
    )(*bases, *terms)


def digits_kernel(experts, ids_ref, codes_ref, out_ref):
    tok = out_ref.shape[0]
    row = lax.broadcasted_iota(jnp.int32, (LANES, tok), 0)
    part, expert = row // experts, lax.rem(row, experts)

    def swapped(ref, k):
        return jnp.concatenate([ref[k : k + 1, tok // 2 :], ref[k : k + 1, : tok // 2]], 1)

    code = jnp.zeros((LANES, tok), jnp.int32)
    for k in range(ids_ref.shape[0]):
        ids = jnp.where(part < 2, ids_ref[k : k + 1, :], swapped(ids_ref, k))
        codes = jnp.where(part < 2, codes_ref[k : k + 1, :], swapped(codes_ref, k))
        code = code + jnp.where(ids == expert, codes, 0)
    digits = jnp.where(lax.rem(part, 2) == 0, code // DIGIT, code % DIGIT)
    out_ref[...] = jnp.transpose(digits.astype(jnp.float32)).astype(out_ref.dtype)


def code_digits(experts, ids, codes):
    return pl.pallas_call(
        functools.partial(digits_kernel, experts),
        in_specs=[pl.BlockSpec(memory_space=pltpu.VMEM)] * 2,
        out_shape=jax.ShapeDtypeStruct((ids.shape[0], LANES), jnp.bfloat16),
        compiler_params=pltpu.CompilerParams(vmem_limit_bytes=2 * MIB),
        cost_estimate=small_cost(),
    )(ids.T, codes.T)


def bring_in_kernel(n, *refs):
    copies = [
        pltpu.make_async_copy(refs[i], refs[n + i], refs[2 * n].at[i]) for i in range(n)
    ]
    for copy in copies:
        copy.start()
    for copy in copies:
        copy.wait()


def bring_in(arrays):
    n = len(arrays)
    return pl.pallas_call(
        functools.partial(bring_in_kernel, n),
        in_specs=[pl.BlockSpec(memory_space=pl.ANY)] * n,
        out_specs=[pl.BlockSpec(memory_space=pltpu.VMEM)] * n,
        out_shape=[jax.ShapeDtypeStruct(array.shape, array.dtype) for array in arrays],
        scratch_shapes=[pltpu.SemaphoreType.DMA((n,))],
        compiler_params=pltpu.CompilerParams(vmem_limit_bytes=2 * MIB),
        cost_estimate=small_cost(),
    )(*arrays)


def body(tokens, expert_ids, gate_codes, w_gate, w_up, w_down):
    nodes = lax.axis_size("node")
    ring = nodes // SPAN
    far = ring // 2
    tok, top = expert_ids.shape
    half = tok // 2

    def chip_at(pos):
        return 2 * pos if pos < far else 2 * (ring - 1 - pos) + 1

    def perm(step):
        return [
            (chip_at(pos) * SPAN + core, chip_at((pos + step) % ring) * SPAN + core)
            for pos in range(ring)
            for core in range(SPAN)
        ]

    forward, backward = perm(1), perm(-1)
    swap = [(node, node ^ 1) for node in range(nodes)]
    expert = lax.div(lax.axis_index("node"), jnp.int32(SPAN)).reshape(1)
    weights = (w_gate, w_up, w_down)
    tokens, weights, expert = lax.optimization_barrier((tokens, weights, expert))

    near = [lax.ppermute(tokens, "node", way) for way in (forward, backward)]
    other = [lax.ppermute(weight, "node", swap) for weight in weights]
    digits = code_digits(ring, expert_ids, gate_codes)
    digits, *other[:2] = lax.optimization_barrier((digits, *other[:2]))
    marks = [lax.ppermute(digits, "node", way) for way in (forward, backward)]
    halves, marks, other, weights = lax.optimization_barrier(
        (split(near), marks, other, weights)
    )
    own = bring_in(weights)

    lead = merged([halves[0], halves[3]], marks, (0, half))
    mine = merged([tokens[:half], tokens[half:]], [digits, digits], (0, half))
    ahead = [[None, lead[0]], [None, halves[1]]]
    behind = [[None, lead[1]], [None, halves[2]]]
    parts = {}

    def work(names, blocks, sources, after=(), **how):
        held = [parts[name] for name in after]
        blocks, held = lax.optimization_barrier((blocks, held))
        parts.update(zip(after, held))
        shifts = [0 if block.shape == source.shape else 2 * ring for block, source in zip(blocks, sources)]
        shares = expert_parts(ring, half, expert, blocks, sources, shifts, own, other, **how)
        parts.update(zip(names, shares))
        return names

    def send(s, wave, after):
        held = [parts[name] for name in after]
        pair, held = lax.optimization_barrier(((ahead[wave][-1], behind[wave][-1]), held))
        parts.update(zip(after, held))
        ahead[wave][-1], behind[wave][-1] = pair
        ahead[wave].append(lax.ppermute(pair[0], "node", forward))
        behind[wave].append(lax.ppermute(pair[1], "node", backward))

    for wave in range(2):
        send(2, wave, [])
    names = [(offset, h) for offset in (0, -1, 1) for h in range(2)]
    blocks = [*mine, lead[0], halves[1], halves[2], lead[1]]
    done = [work(names, blocks, [*mine, lead[0], lead[0], lead[1], lead[1]])]
    for s in range(3, far + 1):
        for wave in range(2):
            if s < far or wave == 0:
                send(s, wave, done.pop(0))
            names = [(1 - s, wave), (s - 1, 1 - wave)]
            after = done[-1] if s == far and wave == 1 else []
            blocks = [ahead[wave][s - 1], behind[wave][s - 1]]
            sources = [ahead[0][s - 1], behind[0][s - 1]]
            cost = FORWARD // 4 if wave else 1024
            done.append(work(names, blocks, sources, after, cost=cost))
    last = [ahead[0][far], behind[0][far]]
    work([(far, 0), (far, 1)], last, last)
    parts[-far, 1] = parts[far, 1]

    early = [(h, sign) for h in range(2) for sign in (1, -1) if (h == 0) != (sign == 1)]
    late = [(h, -sign) for h, sign in early]
    ways = {1: forward, -1: backward}

    def pass_on(group, totals):
        return [lax.ppermute(t, "node", ways[sign]) for t, (h, sign) in zip(totals, group)]

    def shares(group, offset):
        return [parts[sign * offset, h] for h, sign in group]

    first = pass_on(early, shares(early, far - 1))
    last = [pass_on(late, shares(late, far))]
    for k in range(2, far + 1):
        if k < far:
            first = pass_on(early, add(shares(early, far - k), first, cost=AHEAD))
            after = []
        else:
            first = add(shares(early, 0), first, dtype=jnp.float32, cost=AHEAD)
            after = first
        terms = shares(late, far - k + 1)
        if k == far - 1:
            totals = add(terms, last[0], after, pieces=2)
            last = [pass_on(late, totals[p::2]) for p in range(2)]
        else:
            size = half // len(last)
            last = [
                pass_on(late, add(terms, came, after, first=p * size))
                for p, came in enumerate(last)
            ]
    return close(first, last)


def solution(mesh):
    in_specs = (
        P(("groups", "node"), None),
        P(("groups", "node"), None),
        P(("groups", "node"), None),
        P(None, "node"),
        P(None, "node"),
        P("node", None),
    )
    out_specs = P(("groups", "node"), None)
    return jax.shard_map(body, mesh=mesh, in_specs=in_specs, out_specs=out_specs, check_vma=False)
```
